32 devices in a mesh: dom: 16 (over z, x, core), feat: 2 (over y).
Axes of the slice: x: 2, y: 2, z: 4, core: 2. Of those that a mesh axis runs over, the one named last changes fastest.
Arguments:
- features: float32 [16384, 512], P('dom', 'feat'), may hold values from -6 to 6
- weight: float32 [512, 512], P(None, 'feat'), may hold values from -0.25 to 0.25
- cotangent: float32 [16384, 512], P('dom', 'feat'), may hold values from -6 to 6
- block_rows: int32 [16, 4, 24], P('dom'), may hold values from 0 to 7, as said below
- block_cols: int32 [16, 4, 24], P('dom'), may hold values from 0 to 7, as said below
- block_counts: int32 [16, 4], P('dom'), may hold values from 1 to 24, as said below
- block_values: float32 [16, 4, 24, 128, 128], P('dom'), may hold values from -0.25 to 0.25
Outputs:
- activated: float32 [16384, 512], P('dom', 'feat')
- feature_grad: float32 [16384, 512], P('dom', 'feat')
- weight_grad: float32 [512, 512], P(None, 'feat')
The draws below stay inside these ranges and needn't reach their ends.
Inputs may be any that keep to these rules, and one draw needn't show every extreme that they name: `block_rows`: every entry is below 8; within one partition and slot the pairs (block_rows, block_cols) are all different. `block_cols`: every entry is below 8. `block_counts`: some partition has 24 blocks in every slot.
All inputs are finite; a program needn't handle non-finite values.
Results may differ from the reference program's by a relative error of at most 0.0003.
Values sent between devices are 32-bit elements; how exact they have to be, the bound alone decides.
No kernel may reach another device: no remote copies, remote signals or barrier semaphores. Data moves between devices by JAX's collectives and lax.ppermute only.
A program may use at most 128 MiB of HBM per device.

```python
import math
import jax
import jax.numpy as jnp
from jax import lax

HID = 512
BLOCK = 128
WIN = 4
BLOCK_ROWS = 8
CAP = 24
PARTS_SIZE = 16
NODES = 16384


def block_pairs(key):
    subkeys = jax.random.split(key, PARTS_SIZE * WIN)

    def single_order(subkey):
        return jax.random.permutation(subkey, BLOCK_ROWS * BLOCK_ROWS)
    orders = jax.vmap(single_order)(subkeys)
    return orders[:, :CAP].reshape(PARTS_SIZE, WIN, CAP).astype(jnp.int32)


def draw_block_rows(key, part):
    pairs = block_pairs(key)
    return (pairs // BLOCK_ROWS).astype(jnp.int32)


def draw_block_cols(key, part):
    pairs = block_pairs(key)
    return (pairs % BLOCK_ROWS).astype(jnp.int32)


def draw_block_counts(key, part):
    key = jax.random.fold_in(key, 7)
    first_key, second_key, third_key = jax.random.split(key, 3)
    first = jax.random.randint(first_key, (PARTS_SIZE, WIN), 0, CAP)
    second = jax.random.randint(second_key, (PARTS_SIZE, WIN), 0, CAP + 1)
    counts = 1 + first * second // CAP
    busiest = jax.random.randint(third_key, (), 0, PARTS_SIZE)
    positions = jnp.arange(PARTS_SIZE, dtype=jnp.int32)[:, None]
    counts = jnp.where(positions == busiest, CAP, counts)
    return counts.astype(jnp.int32)


def levels(stream_key, dims, pieces, least, high):
    level = 1.0
    for axis_at, shards_of in pieces:
        draws = jax.random.uniform(jax.random.fold_in(jax.random.fold_in(stream_key, 6), axis_at), (shards_of,), jnp.float32, least / len(pieces), high / len(pieces))
        level = level * jnp.repeat(jnp.exp(draws), dims[axis_at] // shards_of).reshape((-1,) + (1,) * (len(dims) - 1 - axis_at))
    return level


def normal_values(own_key, extent, scale, reach, pieces=(), kind=jnp.bfloat16):
    loudness = levels(own_key, extent, pieces, -0.22, 0.18) if pieces else 1.0
    drawn = jax.random.normal(own_key, extent, jnp.float32) * scale * loudness
    return jnp.minimum(jnp.maximum(drawn, -reach), reach).astype(kind)


def setup_inputs(seed: int = 0) -> dict:
    splits = jax.random.split(jax.random.key(seed), 8)
    return {
        "features": normal_values(splits[0], (NODES, HID), 1.0, 6.0, ((0, 16), (1, 2)), jnp.float32),
        "weight": normal_values(splits[1], (HID, HID), HID ** -0.5, 0.25, ((1, 2),), jnp.float32),
        "cotangent": normal_values(splits[2], (NODES, HID), 1.0, 6.0, ((0, 16), (1, 2)), jnp.float32),
        "block_rows": draw_block_rows(jax.random.fold_in(splits[7], 71), 0),
        "block_cols": draw_block_cols(jax.random.fold_in(splits[7], 71), 0),
        "block_counts": draw_block_counts(jax.random.fold_in(splits[7], 71), 0),
        "block_values": normal_values(splits[6], (PARTS_SIZE, WIN, CAP, BLOCK, BLOCK), (4 * BLOCK) ** -0.5, 0.25, ((0, 16),), jnp.float32),
    }


def aggregate(dense, block_rows, block_cols, block_counts, block_values):
    width = dense.shape[1]
    grouped = dense.reshape(PARTS_SIZE, BLOCK_ROWS, BLOCK, width)
    live = (jnp.arange(CAP, dtype=jnp.int32)[None, None, :] < block_counts[:, :, None]).astype(jnp.float32)

    def one_part(part_index):
        total = jnp.zeros((BLOCK_ROWS, BLOCK, width), jnp.float32)
        for slot_index in range(WIN):
            source_index = ((part_index - slot_index) % PARTS_SIZE).astype(jnp.int32)
            source = lax.dynamic_index_in_dim(grouped, source_index, 0, keepdims=False)
            picked = source[block_cols[part_index, slot_index]]
            blocks = block_values[part_index, slot_index] * live[part_index, slot_index][:, None, None]
            product = jnp.einsum('cij,cjh->cih', blocks, picked, precision=lax.Precision.HIGHEST)
            total = total.at[block_rows[part_index, slot_index]].add(product)
        return total
    return lax.map(one_part, jnp.arange(PARTS_SIZE, dtype=jnp.int32)).reshape(NODES, width)

def reference(features, weight, cotangent, block_rows, block_cols, block_counts, block_values):

    def forward(inputs, matrix):
        hidden = jnp.dot(inputs, matrix, precision=lax.Precision.HIGHEST, preferred_element_type=jnp.float32)
        pre = aggregate(hidden, block_rows, block_cols, block_counts, block_values)
        return jax.nn.silu(pre)
    activated, pullback = jax.vjp(forward, features, weight)
    feature_grad, weight_grad = pullback(cotangent)
    weight_grad = weight_grad * jnp.float32(1.0 / math.sqrt(NODES))
    return (activated, feature_grad, weight_grad)
```

```python
import functools
import math

import jax
import jax.numpy as jnp
from jax import lax
from jax.experimental import pallas as pl
from jax.experimental.pallas import tpu as pltpu
from jax.sharding import PartitionSpec as P

F32 = jnp.float32
BF16 = jnp.bfloat16
CHUNKS = 2
VMEM = 48 * 1024 * 1024


def split(value):
    high = value.astype(BF16)
    low = (value - high.astype(F32)).astype(BF16)
    return high, low


def mm(a, b, dims=((1,), (0,))):
    return lax.dot_general(a, b, (dims, ((), ())), preferred_element_type=F32)


def mm3(ah, al, bh, bl, dims=((1,), (0,))):
    return mm(ah, bh, dims) + (mm(ah, bl, dims) + mm(al, bh, dims))


def cost(flops, moved):
    return pl.CostEstimate(flops=int(flops), bytes_accessed=int(moved), transcendentals=0)


def lay_out_kernel(rows, cols, counts, blocks, ah, al, th, tl):
    slot = pl.program_id(0)
    cap = blocks.shape[1]
    size = blocks.shape[2]
    for out in (ah, al, th, tl):
        out[...] = jnp.zeros_like(out)

    def one(k, carry):
        r = pl.multiple_of(rows[slot * cap + k] * size, size)
        c = pl.multiple_of(cols[slot * cap + k] * size, size)
        block = blocks[0, k]
        high, low = split(block)
        ah[0, pl.ds(r, size), pl.ds(c, size)] = high
        al[0, pl.ds(r, size), pl.ds(c, size)] = low
        high, low = split(block.T)
        th[0, pl.ds(c, size), pl.ds(r, size)] = high
        tl[0, pl.ds(c, size), pl.ds(r, size)] = low
        return carry

    lax.fori_loop(0, jnp.minimum(counts[slot], cap), one, 0)


def lay_out(rows, cols, counts, blocks, size_all):
    window, cap, size, _ = blocks.shape
    shape = jax.ShapeDtypeStruct((window, size_all, size_all), BF16)
    spec = pl.BlockSpec((1, size_all, size_all), lambda s, *_: (s, 0, 0))
    return pl.pallas_call(
        lay_out_kernel,
        grid_spec=pltpu.PrefetchScalarGridSpec(
            num_scalar_prefetch=3,
            grid=(window,),
            in_specs=[pl.BlockSpec((1, cap, size, size), lambda s, *_: (s, 0, 0, 0))],
            out_specs=[spec] * 4,
        ),
        out_shape=[shape] * 4,
        compiler_params=pltpu.CompilerParams(vmem_limit_bytes=VMEM),
        cost_estimate=cost(0, 40e6),
        name="lay_out",
    )(rows.reshape(-1), cols.reshape(-1), counts.reshape(-1), blocks)


def slot_kernel(n_src, n_add, slot, mh, ml, *refs):
    sources, addends, (out,), (both,) = (
        refs[:n_src],
        refs[n_src : n_src + n_add],
        refs[n_src + n_add : n_src + n_add + 1],
        refs[n_src + n_add + 1 :],
    )
    width = out.shape[-1]

    @pl.when(pl.program_id(0) == 0)
    def _():
        total = sources[0][...]
        for source in sources[1:]:
            total = total + source[...]
        high, low = split(total)
        both[:, :width] = high
        both[:, width:] = low

    first = mm(mh[0], both[...])
    total = first[:, :width] + (first[:, width:] + mm(ml[0], both[:, :width]))
    for addend in addends:
        total = total + addend[...]
    out[...] = total


def slot_product(name, slot, mh, ml, sources, addends=()):
    window, rows, depth = mh.shape
    width = sources[0].shape[1]
    tile = rows // 4
    matrix = pl.BlockSpec((1, tile, depth), lambda i, s: (s[0], i, 0))
    whole = pl.BlockSpec((depth, width), lambda i, s: (0, 0))
    part = pl.BlockSpec((tile, width), lambda i, s: (i, 0))
    return pl.pallas_call(
        functools.partial(slot_kernel, len(sources), len(addends)),
        grid_spec=pltpu.PrefetchScalarGridSpec(
            num_scalar_prefetch=1,
            grid=(rows // tile,),
            in_specs=[matrix] * 2 + [whole] * len(sources) + [part] * len(addends),
            out_specs=part,
            scratch_shapes=[pltpu.VMEM((depth, 2 * width), BF16)],
        ),
        out_shape=jax.ShapeDtypeStruct((rows, width), F32),
        compiler_params=pltpu.CompilerParams(vmem_limit_bytes=VMEM),
        cost_estimate=cost(8 * rows * depth * width, 4 * rows * depth),
        name=name,
    )(slot, mh, ml, *sources, *addends)


def middle_kernel(n, side, *refs):
    own, far = refs[:n], refs[n : 2 * n]
    w_own, w_far, cot, act, grad = refs[2 * n : 2 * n + 5]
    g_own, g_far = refs[2 * n + 5 : 3 * n + 5], refs[3 * n + 5 : 4 * n + 5]
    wh, wl = refs[4 * n + 5 :]
    half = w_own.shape[0]
    width = half // n

    @pl.when(pl.program_id(0) == 0)
    def _():
        for i, w in enumerate((w_own, w_far)):
            high, low = split(w[...])
            wh[i] = high
            wl[i] = low

    pre = None
    for i, group in enumerate((own, far)):
        rows = jnp.concatenate([ref[...] for ref in group], axis=1)
        high, low = split(rows)
        term = mm3(high, low, wh[i], wl[i])
        pre = term if pre is None else pre + term
    s = 1.0 / (1.0 + jnp.exp(-pre))
    act[...] = pre * s
    pg = cot[...] * (s + pre * s * (1.0 - s))
    grad[...] = pg
    ph, pl_ = split(pg)
    for i, group in ((1, g_far), (0, g_own)):
        term = mm3(ph, pl_, wh[i], wl[i], ((1,), (1,)))
        for j, ref in enumerate(group):
            ref[...] = term[:, j * width : (j + 1) * width]


def middle(side, own, far, weight, cot):
    n = len(own)
    rows, hidden = cot.shape
    half = weight.shape[0] // 2
    width = half // n
    tile = rows // 4
    part = pl.BlockSpec((tile, width), lambda i, s: (i, 0))
    wide = pl.BlockSpec((tile, hidden), lambda i, s: (i, 0))
    piece = jax.ShapeDtypeStruct((rows, width), F32)
    full = jax.ShapeDtypeStruct((rows, hidden), F32)
    out = pl.pallas_call(
        functools.partial(middle_kernel, n),
        grid_spec=pltpu.PrefetchScalarGridSpec(
            num_scalar_prefetch=1,
            grid=(rows // tile,),
            in_specs=[part] * (2 * n)
            + [
                pl.BlockSpec((half, hidden), lambda i, s: (s[0], 0)),
                pl.BlockSpec((half, hidden), lambda i, s: (1 - s[0], 0)),
                wide,
            ],
            out_specs=[wide, wide] + [part] * (2 * n),
            scratch_shapes=[pltpu.VMEM((2, half, hidden), BF16)] * 2,
        ),
        out_shape=[full, full] + [piece] * (2 * n),
        compiler_params=pltpu.CompilerParams(vmem_limit_bytes=VMEM),
        cost_estimate=cost(24 * rows * half * hidden, 8e6),
        name="middle",
    )(side, *own, *far, weight, weight, cot)
    return out[0], out[1], out[2 : 2 + n], out[2 + n :]


def weight_kernel(n, scale, side, *refs):
    own, far = refs[:n], refs[n : 2 * n]
    grad, out = refs[2 * n :]
    half = out.shape[0] // 2
    gh, gl = split(grad[...])
    for group, at in ((own, side[0]), (far, 1 - side[0])):
        rows = jnp.concatenate([ref[...] for ref in group], axis=1)
        high, low = split(rows.T)
        term = mm3(high, low, gh, gl)
        out[pl.ds(pl.multiple_of(at * half, half), half), :] = term * scale


def weight_term(side, own, far, grad, scale):
    n = len(own)
    rows, hidden = grad.shape
    half = own[0].shape[1] * n
    return pl.pallas_call(
        functools.partial(weight_kernel, n, scale),
        grid_spec=pltpu.PrefetchScalarGridSpec(
            num_scalar_prefetch=1,
            grid=(1,),
            in_specs=[pl.BlockSpec(a.shape, lambda i, s: (0, 0)) for a in (*own, *far, grad)],
            out_specs=pl.BlockSpec((2 * half, hidden), lambda i, s: (0, 0)),
        ),
        out_shape=jax.ShapeDtypeStruct((2 * half, hidden), F32),
        compiler_params=pltpu.CompilerParams(vmem_limit_bytes=VMEM),
        cost_estimate=cost(12 * rows * half * hidden, 4e6),
        name="weight_term",
    )(side, *own, *far, grad)


def moved(value, axis, even, odd):
    peers = lax.axis_size(axis)
    perm = [(i, (i + (odd if i % 2 else even)) % peers) for i in range(peers)]
    return lax.ppermute(value, axis, perm)


def swapped(value, axis, bit):
    peers = lax.axis_size(axis)
    return lax.ppermute(value, axis, [(i, i ^ bit) for i in range(peers)])


def summed(value, axis):
    peers = lax.axis_size(axis)
    if peers & (peers - 1) or value.shape[0] % peers:
        return lax.psum(value, axis)
    me = lax.axis_index(axis)
    bits = [1 << i for i in range(peers.bit_length() - 1)]
    for bit in bits:
        half = value.shape[0] // 2
        upper = (me // bit) % 2
        keep = lax.dynamic_slice_in_dim(value, upper * half, half, 0)
        give = lax.dynamic_slice_in_dim(value, (1 - upper) * half, half, 0)
        value = keep + swapped(give, axis, bit)
    for bit in reversed(bits):
        upper = (me // bit) % 2
        other = swapped(value, axis, bit)
        value = jnp.where(
            upper == 0,
            jnp.concatenate([value, other], axis=0),
            jnp.concatenate([other, value], axis=0),
        )
    return value


def body(features, weight, cotangent, block_rows, block_cols, block_counts, block_values):
    rows_here = features.shape[0]
    width = features.shape[1] // CHUNKS
    parts = lax.axis_size("dom")
    odd = lax.axis_index("dom") % 2
    side = lax.axis_index("feat").astype(jnp.int32).reshape(1)
    slot_near = (1 + 2 * odd).astype(jnp.int32).reshape(1)
    slot_far = (3 - 2 * odd).astype(jnp.int32).reshape(1)
    slot_two = jnp.full((1,), 2, jnp.int32)
    slot_own = jnp.zeros((1,), jnp.int32)

    pieces = [features[:, i * width : (i + 1) * width] for i in range(CHUNKS)]
    arrived = []
    for piece in pieces:
        near = moved(piece, "dom", 3, 1)
        far = moved(piece, "dom", 1, 3)
        arrived.append((near, far))

    ah, al, th, tl = lay_out(block_rows[0], block_cols[0], block_counts[0], block_values[0], rows_here)

    own = []
    received = []
    for piece, (near, far) in zip(pieces, arrived):
        two = swapped(near, "dom", 1)
        total = slot_product("agg_own", slot_own, ah, al, [piece])
        total = slot_product("agg_far", slot_far, ah, al, [far], [total])
        total = slot_product("agg_near", slot_near, ah, al, [near], [total])
        total = slot_product("agg_two", slot_two, ah, al, [two], [total])
        own.append(total)
        received.append(swapped(total, "feat", 1))

    activated, pre_grad, g_own, g_far = middle(side, own, received, weight, cotangent)
    scale = 1.0 / math.sqrt(rows_here * parts)
    g_parts = [(mine, swapped(other, "feat", 1)) for mine, other in zip(g_own, g_far)]
    local_weight = weight_term(side, own, received, pre_grad, scale)
    weight_grad = summed(local_weight, "dom")

    outs = []
    for g in g_parts:
        two = slot_product("back_two", slot_two, th, tl, g)
        two = swapped(two, "dom", 1)
        far = slot_product("back_far", slot_far, th, tl, g)
        far = moved(far, "dom", -3, -1)
        near = slot_product("back_near", slot_near, th, tl, g, [two])
        near = moved(near, "dom", -1, -3)
        mine = slot_product("back_own", slot_own, th, tl, g)
        outs.append(mine + far + near)
    feature_grad = jnp.concatenate(outs, axis=1)
    return (activated, feature_grad, weight_grad)


def solution(mesh):
    in_specs = (
        P("dom", "feat"),
        P(None, "feat"),
        P("dom", "feat"),
        P("dom", None, None),
        P("dom", None, None),
        P("dom", None),
        P("dom", None, None, None, None),
    )
    out_specs = (P("dom", "feat"), P("dom", "feat"), P(None, "feat"))
    return jax.shard_map(body, mesh=mesh, in_specs=in_specs, out_specs=out_specs, check_vma=False)
```

```python
import functools
import math

import jax
import jax.numpy as jnp
from jax import lax
from jax.experimental import pallas as pl
from jax.experimental.pallas import tpu as pltpu
from jax.sharding import PartitionSpec as P

F32 = jnp.float32
BF16 = jnp.bfloat16
CHUNKS = 2
TILE = 256
VMEM = 12 * 1024 * 1024


def split(value):
    high = value.astype(BF16)
    low = (value - high.astype(F32)).astype(BF16)
    return high, low


def mm(a, b, dims=((1,), (0,))):
    return lax.dot_general(a, b, (dims, ((), ())), preferred_element_type=F32)


def mm3(ah, al, bh, bl, dims=((1,), (0,))):
    return mm(ah, bh, dims) + (mm(ah, bl, dims) + mm(al, bh, dims))


def cost(flops, moved):
    return pl.CostEstimate(flops=int(flops), bytes_accessed=int(moved), transcendentals=0)


def lay_out_kernel(rows, cols, counts, blocks, ah, al, th, tl, mark):
    slot = pl.program_id(0)
    cap = blocks.shape[1]
    size = blocks.shape[2]
    for out in (ah, al, th, tl):
        out[slot] = jnp.zeros(out.shape[1:], out.dtype)

    def one(k, carry):
        r = pl.multiple_of(rows[slot * cap + k] * size, size)
        c = pl.multiple_of(cols[slot * cap + k] * size, size)
        block = blocks[0, k]
        high, low = split(block)
        ah[slot, pl.ds(r, size), pl.ds(c, size)] = high
        al[slot, pl.ds(r, size), pl.ds(c, size)] = low
        high, low = split(block.T)
        th[slot, pl.ds(c, size), pl.ds(r, size)] = high
        tl[slot, pl.ds(c, size), pl.ds(r, size)] = low
        return carry

    lax.fori_loop(0, jnp.minimum(counts[slot], cap), one, 0)
    mark[...] = jnp.zeros_like(mark)


def lay_out(rows, cols, counts, blocks, size_all):
    window, cap, size, _ = blocks.shape
    shape = pltpu.VMEM((window, size_all, size_all), BF16)
    return pl.pallas_call(
        lay_out_kernel,
        grid_spec=pltpu.PrefetchScalarGridSpec(
            num_scalar_prefetch=3,
            grid=(window,),
            in_specs=[pl.BlockSpec((1, cap, size, size), lambda s, *_: (s, 0, 0, 0))],
            out_specs=[pl.BlockSpec(memory_space=pltpu.VMEM)] * 5,
        ),
        out_shape=[shape] * 4 + [pltpu.VMEM((8, 128), F32)],
        compiler_params=pltpu.CompilerParams(vmem_limit_bytes=VMEM),
        cost_estimate=cost(0, 20e6),
        name="lay_out",
    )(rows.reshape(-1), cols.reshape(-1), counts.reshape(-1), blocks)


def slot_kernel(n_src, n_add, slot, mh, ml, *refs):
    sources, addends, (out,), (both,) = (
        refs[:n_src],
        refs[n_src : n_src + n_add],
        refs[n_src + n_add : n_src + n_add + 1],
        refs[n_src + n_add + 1 :],
    )
    width = out.shape[-1]
    at = slot[0]
    total = sources[0][...]
    for source in sources[1:]:
        total = total + source[...]
    high, low = split(total)
    both[:, :width] = high
    both[:, width:] = low

    def term(start):
        deep = pl.ds(start, TILE)
        first = mm(mh[at, :, deep], both[deep, :])
        return first[:, :width] + (first[:, width:] + mm(ml[at, :, deep], both[deep, :width]))

    start = term(0)
    for addend in addends:
        start = start + addend[...]
    out[...] = start

    def step(k, carry):
        out[...] += term(pl.multiple_of(k * TILE, TILE))
        return carry

    lax.fori_loop(1, both.shape[0] // TILE, step, 0)


def slot_product(name, slot, mh, ml, sources, addends=()):
    window, rows, depth = mh.shape
    width = sources[0].shape[1]
    vmem = pl.BlockSpec(memory_space=pltpu.VMEM)
    here = [pltpu.with_memory_space_constraint(a, pltpu.VMEM) for a in (mh, ml, *sources, *addends)]
    return pl.pallas_call(
        functools.partial(slot_kernel, len(sources), len(addends)),
        in_specs=[pl.BlockSpec(memory_space=pltpu.SMEM)] + [vmem] * len(here),
        out_specs=vmem,
        scratch_shapes=[pltpu.VMEM((depth, 2 * width), BF16)],
        out_shape=pltpu.VMEM((rows, width), F32),
        compiler_params=pltpu.CompilerParams(vmem_limit_bytes=VMEM),
        cost_estimate=cost(8 * rows * depth * width, 4 * rows * depth),
        name=name,
    )(slot, *here)


def pre_kernel(has_base, own, far, w_own, w_far, *refs):
    out = refs[-1]
    total = refs[0][...] if has_base else None
    for rows, w in ((own, w_own), (far, w_far)):
        wh, wl = split(w[...])
        high, low = split(rows[...])
        term = mm3(high, low, wh, wl)
        total = term if total is None else total + term
    out[...] = total


def pre_term(side, chunk, own, far, weight, base=None):
    rows, width = own.shape
    hidden = weight.shape[1]
    n = weight.shape[0] // 2 // width
    whole = pl.BlockSpec((rows, width), lambda i, s: (0, 0))
    wide = pl.BlockSpec((rows, hidden), lambda i, s: (0, 0))
    extra = [] if base is None else [base]
    return pl.pallas_call(
        lambda side, *refs: pre_kernel(bool(extra), *refs),
        grid_spec=pltpu.PrefetchScalarGridSpec(
            num_scalar_prefetch=1,
            grid=(1,),
            in_specs=[
                whole,
                whole,
                pl.BlockSpec((width, hidden), lambda i, s: (n * s[0] + chunk, 0)),
                pl.BlockSpec((width, hidden), lambda i, s: (n * (1 - s[0]) + chunk, 0)),
            ]
            + [wide] * len(extra),
            out_specs=wide,
        ),
        out_shape=jax.ShapeDtypeStruct((rows, hidden), F32),
        compiler_params=pltpu.CompilerParams(vmem_limit_bytes=VMEM),
        cost_estimate=cost(12 * rows * width * hidden, 4e6),
        name="pre_term",
    )(side, own, far, weight, weight, *extra)


def middle_kernel(n, side, own, far, base, w, cot, act, grad, *refs):
    g_own, g_far = refs[:n], refs[n : 2 * n]
    wh, wl = refs[2 * n :]
    half = w.shape[0] // 2
    width = half // n

    @pl.when(pl.program_id(0) == 0)
    def _():
        high, low = split(w[...])
        wh[...] = high
        wl[...] = low

    def weight_rows(which, chunk):
        at = pl.multiple_of(which * half + chunk * width, width)
        return wh[pl.ds(at, width), :], wl[pl.ds(at, width), :]

    pre = base[...]
    for rows, which in ((own, side[0]), (far, 1 - side[0])):
        pre = pre + mm3(*split(rows[...]), *weight_rows(which, n - 1))
    s = 1.0 / (1.0 + jnp.exp(-pre))
    act[...] = pre * s
    pg = cot[...] * (s + pre * s * (1.0 - s))
    grad[...] = pg
    high, low = split(pg)
    for which, group in ((1 - side[0], g_far), (side[0], g_own)):
        at = pl.ds(pl.multiple_of(which * half, half), half)
        term = mm3(high, low, wh[at, :], wl[at, :], ((1,), (1,)))
        for j, ref in enumerate(group):
            ref[...] = term[:, j * width : (j + 1) * width]


def middle(side, n, own, far, base, weight, cot):
    rows, hidden = cot.shape
    width = own.shape[1]
    tile = rows // 2
    part = pl.BlockSpec((tile, width), lambda i, s: (i, 0))
    wide = pl.BlockSpec((tile, hidden), lambda i, s: (i, 0))
    piece = jax.ShapeDtypeStruct((rows, width), F32)
    full = jax.ShapeDtypeStruct((rows, hidden), F32)
    out = pl.pallas_call(
        functools.partial(middle_kernel, n),
        grid_spec=pltpu.PrefetchScalarGridSpec(
            num_scalar_prefetch=1,
            grid=(rows // tile,),
            in_specs=[part, part, wide, pl.BlockSpec(weight.shape, lambda i, s: (0, 0)), wide],
            out_specs=[wide, wide] + [part] * (2 * n),
            scratch_shapes=[pltpu.VMEM(weight.shape, BF16)] * 2,
        ),
        out_shape=[full, full] + [piece] * (2 * n),
        compiler_params=pltpu.CompilerParams(vmem_limit_bytes=VMEM),
        cost_estimate=cost(24 * rows * width * n * hidden, 8e6),
        name="middle",
    )(side, own, far, base, weight, cot)
    return out[0], out[1], out[2 : 2 + n], out[2 + n :]


def weight_kernel(n, scale, side, *refs):
    own, far = refs[:n], refs[n : 2 * n]
    grad, out = refs[2 * n :]
    half = out.shape[0] // 2
    gh, gl = split(grad[...])
    for group, at in ((own, side[0]), (far, 1 - side[0])):
        rows = jnp.concatenate([ref[...] for ref in group], axis=1)
        high, low = split(rows.T)
        term = mm3(high, low, gh, gl)
        out[pl.ds(pl.multiple_of(at * half, half), half), :] = term * scale


def weight_term(side, own, far, grad, scale):
    n = len(own)
    rows, hidden = grad.shape
    half = own[0].shape[1] * n
    return pl.pallas_call(
        functools.partial(weight_kernel, n, scale),
        grid_spec=pltpu.PrefetchScalarGridSpec(
            num_scalar_prefetch=1,
            grid=(1,),
            in_specs=[pl.BlockSpec(a.shape, lambda i, s: (0, 0)) for a in (*own, *far, grad)],
            out_specs=pl.BlockSpec((2 * half, hidden), lambda i, s: (0, 0)),
        ),
        out_shape=jax.ShapeDtypeStruct((2 * half, hidden), F32),
        compiler_params=pltpu.CompilerParams(vmem_limit_bytes=VMEM),
        cost_estimate=cost(12 * rows * half * hidden, 4e6),
        name="weight_term",
    )(side, *own, *far, grad)


def moved(value, axis, even, odd):
    peers = lax.axis_size(axis)
    perm = [(i, (i + (odd if i % 2 else even)) % peers) for i in range(peers)]
    return lax.ppermute(value, axis, perm)


def swapped(value, axis, bit):
    peers = lax.axis_size(axis)
    return lax.ppermute(value, axis, [(i, i ^ bit) for i in range(peers)])


def after(value, *others):
    return lax.optimization_barrier((value, *others))[0]


def summed(value, axis):
    peers = lax.axis_size(axis)
    if peers & (peers - 1) or value.shape[0] % peers:
        return lax.psum(value, axis)
    me = lax.axis_index(axis)
    bits = [1 << i for i in range(peers.bit_length() - 1)]
    for bit in bits:
        half = value.shape[0] // 2
        upper = (me // bit) % 2
        keep = lax.dynamic_slice_in_dim(value, upper * half, half, 0)
        give = lax.dynamic_slice_in_dim(value, (1 - upper) * half, half, 0)
        value = keep + swapped(give, axis, bit)
    for bit in reversed(bits):
        upper = (me // bit) % 2
        other = swapped(value, axis, bit)
        value = jnp.where(
            upper == 0,
            jnp.concatenate([value, other], axis=0),
            jnp.concatenate([other, value], axis=0),
        )
    return value


def body(features, weight, cotangent, block_rows, block_cols, block_counts, block_values):
    rows_here = features.shape[0]
    width = features.shape[1] // CHUNKS
    parts = lax.axis_size("dom")
    odd = lax.axis_index("dom") % 2
    side = lax.axis_index("feat").astype(jnp.int32).reshape(1)
    slot_near = (1 + 2 * odd).astype(jnp.int32).reshape(1)
    slot_far = (3 - 2 * odd).astype(jnp.int32).reshape(1)
    slot_two = jnp.full((1,), 2, jnp.int32)
    slot_own = jnp.zeros((1,), jnp.int32)

    pieces = [features[:, i * width : (i + 1) * width] for i in range(CHUNKS)]
    arrived = []
    for piece in pieces:
        near = moved(piece, "dom", 3, 1)
        far = moved(piece, "dom", 1, 3)
        arrived.append((near, far))

    ah, al, th, tl, mark = lay_out(block_rows[0], block_cols[0], block_counts[0], block_values[0], rows_here)

    arrived = [(after(near, mark), far) for near, far in arrived]
    twos = [swapped(near, "dom", 1) for near, _ in arrived]
    starts = [slot_product("agg_own", slot_own, ah, al, [piece]) for piece in pieces]
    own = []
    received = []
    for total, (near, far), two in zip(starts, arrived, twos):
        if own:
            total, far, near, two, own[-1] = lax.optimization_barrier((total, far, near, two, own[-1]))
        total = slot_product("agg_far", slot_far, ah, al, [far], [total])
        total = slot_product("agg_near", slot_near, ah, al, [near], [total])
        total = slot_product("agg_two", slot_two, ah, al, [two], [total])
        own.append(total)
        received.append(swapped(total, "feat", 1))

    base = None
    for i in range(CHUNKS - 1):
        base = pre_term(side, i, own[i], received[i], weight, base)
    activated, pre_grad, g_own, g_far = middle(
        side, CHUNKS, own[-1], received[-1], base, weight, cotangent
    )
    scale = 1.0 / math.sqrt(rows_here * parts)
    local_weight = weight_term(side, own, received, pre_grad, scale)
    g_parts = []
    for mine, other in zip(g_own, g_far):
        other = after(other, g_parts[-1][1], local_weight) if g_parts else other
        g_parts.append((mine, swapped(other, "feat", 1)))

    outs = []
    for g in g_parts:
        two = slot_product("back_two", slot_two, th, tl, g)
        two = swapped(two, "dom", 1)
        far = slot_product("back_far", slot_far, th, tl, g)
        if not outs:
            local_weight = after(local_weight, far)
            weight_grad = summed(local_weight, "dom")
        far = moved(far, "dom", -3, -1)
        near = slot_product("back_near", slot_near, th, tl, g, [two])
        near = moved(near, "dom", -1, -3)
        mine = slot_product("back_own", slot_own, th, tl, g)
        outs.append(mine + far + near)
    feature_grad = jnp.concatenate(outs, axis=1)
    return (activated, feature_grad, weight_grad)


def solution(mesh):
    in_specs = (
        P("dom", "feat"),
        P(None, "feat"),
        P("dom", "feat"),
        P("dom", None, None),
        P("dom", None, None),
        P("dom", None),
        P("dom", None, None, None, None),
    )
    out_specs = (P("dom", "feat"), P("dom", "feat"), P(None, "feat"))
    return jax.shard_map(body, mesh=mesh, in_specs=in_specs, out_specs=out_specs, check_vma=False)
```

```python
import functools
import math

import jax
import jax.numpy as jnp
from jax import lax
from jax.experimental import pallas as pl
from jax.experimental.pallas import tpu as pltpu
from jax.sharding import PartitionSpec as P

F32 = jnp.float32
BF16 = jnp.bfloat16
CHUNKS = 2
TILE = 256
VMEM = 12 * 1024 * 1024


def split(value):
    high = value.astype(BF16)
    low = (value - high.astype(F32)).astype(BF16)
    return high, low


def mm(a, b, dims=((1,), (0,))):
    return lax.dot_general(a, b, (dims, ((), ())), preferred_element_type=F32)


def mm3(ah, al, bh, bl, dims=((1,), (0,))):
    return mm(ah, bh, dims) + (mm(ah, bl, dims) + mm(al, bh, dims))


def cost(flops, moved):
    return pl.CostEstimate(flops=int(flops), bytes_accessed=int(moved), transcendentals=0)


def lay_out_kernel(rows, cols, counts, who, blocks, ah, al, th, tl, mark):
    slot = pl.program_id(0)
    cap = blocks.shape[1]
    size = blocks.shape[2]
    for out in (ah, al, th, tl):
        out[slot] = jnp.zeros(out.shape[1:], out.dtype)

    def one(k, carry):
        r = pl.multiple_of(rows[slot, k] * size, size)
        c = pl.multiple_of(cols[slot, k] * size, size)
        block = blocks[0, k]
        high, low = split(block)
        ah[slot, pl.ds(r, size), pl.ds(c, size)] = high
        al[slot, pl.ds(r, size), pl.ds(c, size)] = low
        high, low = split(block.T)
        th[slot, pl.ds(c, size), pl.ds(r, size)] = high
        tl[slot, pl.ds(c, size), pl.ds(r, size)] = low
        return carry

    lax.fori_loop(0, jnp.minimum(counts[0, slot], cap), one, 0)
    mark[...] = jnp.full(mark.shape, who[0].astype(F32))


def lay_out(rows, cols, counts, who, blocks, size_all):
    window, cap, size, _ = blocks.shape
    shape = pltpu.VMEM((window, size_all, size_all), BF16)
    return pl.pallas_call(
        lay_out_kernel,
        grid_spec=pltpu.PrefetchScalarGridSpec(
            num_scalar_prefetch=4,
            grid=(window,),
            in_specs=[pl.BlockSpec((1, cap, size, size), lambda s, *_: (s, 0, 0, 0))],
            out_specs=[pl.BlockSpec(memory_space=pltpu.VMEM)] * 5,
        ),
        out_shape=[shape] * 4 + [pltpu.VMEM((8, 128), F32)],
        compiler_params=pltpu.CompilerParams(vmem_limit_bytes=VMEM),
        cost_estimate=cost(0, 20e6),
        name="lay_out",
    )(rows, cols, counts, who, blocks)


def product_kernel(slots, counts, n_add, who, mh, ml, *refs):
    refs = list(refs)
    groups = [[refs.pop(0) for _ in range(n)] for n in counts]
    addends = [refs.pop(0) for _ in range(n_add)]
    out = refs.pop(0)
    width = out.shape[-1]
    places = []
    for (slot, column), sources, both in zip(slots, groups, refs):
        places.append(slot if slot >= 0 else who[-slot])
        part = pl.ds(column, width)
        total = sources[0][:, part]
        for source in sources[1:]:
            total = total + source[:, part]
        high, low = split(total)
        both[:, :width] = high
        both[:, width:] = low

    def step(start):
        deep = pl.ds(start, TILE)
        total = None
        for at, both in zip(places, refs):
            first = mm(mh[at, :, deep], both[deep, :])
            term = first[:, :width] + (first[:, width:] + mm(ml[at, :, deep], both[deep, :width]))
            total = term if total is None else total + term
        return total

    start = step(0)
    for addend in addends:
        start = start + addend[...]
    out[...] = start

    def more(k, carry):
        out[...] += step(pl.multiple_of(k * TILE, TILE))
        return carry

    lax.fori_loop(1, mh.shape[2] // TILE, more, 0)


def product(name, who, mh, ml, terms, addends=()):
    window, rows, depth = mh.shape
    width = terms[0][1][0].shape[1]
    slots = [(t[0], t[2] if len(t) > 2 else 0) for t in terms]
    vmem = pl.BlockSpec(memory_space=pltpu.VMEM)
    sources = [source for t in terms for source in t[1]]
    here = [pltpu.with_memory_space_constraint(a, pltpu.VMEM) for a in (mh, ml, *sources, *addends)]
    return pl.pallas_call(
        functools.partial(
            product_kernel, slots, [len(t[1]) for t in terms], len(addends)
        ),
        in_specs=[pl.BlockSpec(memory_space=pltpu.SMEM)] + [vmem] * len(here),
        out_specs=vmem,
        scratch_shapes=[pltpu.VMEM((depth, 2 * width), BF16)] * len(terms),
        out_shape=pltpu.VMEM((rows, width), F32),
        compiler_params=pltpu.CompilerParams(vmem_limit_bytes=VMEM),
        cost_estimate=cost(8 * len(terms) * rows * depth * width, 4 * rows * depth),
        name=name,
    )(who, *here)


def pre_kernel(has_base, own, far, w_own, w_far, *refs):
    out = refs[-1]
    total = refs[0][...] if has_base else None
    for rows, w in ((own, w_own), (far, w_far)):
        wh, wl = split(w[...])
        high, low = split(rows[...])
        term = mm3(high, low, wh, wl)
        total = term if total is None else total + term
    out[...] = total


def pre_term(who, chunk, own, far, weight, base=None):
    rows, width = own.shape
    hidden = weight.shape[1]
    n = weight.shape[0] // 2 // width
    whole = pl.BlockSpec((rows, width), lambda i, s: (0, 0))
    wide = pl.BlockSpec((rows, hidden), lambda i, s: (0, 0))
    extra = [] if base is None else [base]
    return pl.pallas_call(
        lambda who, *refs: pre_kernel(bool(extra), *refs),
        grid_spec=pltpu.PrefetchScalarGridSpec(
            num_scalar_prefetch=1,
            grid=(1,),
            in_specs=[
                whole,
                whole,
                pl.BlockSpec((width, hidden), lambda i, s: (n * s[1] + chunk, 0)),
                pl.BlockSpec((width, hidden), lambda i, s: (n * (1 - s[1]) + chunk, 0)),
            ]
            + [wide] * len(extra),
            out_specs=wide,
        ),
        out_shape=jax.ShapeDtypeStruct((rows, hidden), F32),
        compiler_params=pltpu.CompilerParams(vmem_limit_bytes=VMEM),
        cost_estimate=cost(12 * rows * width * hidden, 4e6),
        name="pre_term",
    )(who, own, far, weight, weight, *extra)


def middle_kernel(n, who, own, far, base, w, cot, act, grad, *refs):
    g_own, g_far = refs[:n], refs[n : 2 * n]
    wh, wl = refs[2 * n :]
    half = w.shape[0] // 2
    width = half // n

    @pl.when(pl.program_id(0) == 0)
    def _():
        high, low = split(w[...])
        wh[...] = high
        wl[...] = low

    def weight_rows(which, chunk):
        at = pl.multiple_of(which * half + chunk * width, width)
        return wh[pl.ds(at, width), :], wl[pl.ds(at, width), :]

    pre = base[...]
    for rows, which in ((own, who[1]), (far, 1 - who[1])):
        pre = pre + mm3(*split(rows[...]), *weight_rows(which, n - 1))
    s = 1.0 / (1.0 + jnp.exp(-pre))
    act[...] = pre * s
    pg = cot[...] * (s + pre * s * (1.0 - s))
    grad[...] = pg
    high, low = split(pg)
    for which, group in ((1 - who[1], g_far), (who[1], g_own)):
        at = pl.ds(pl.multiple_of(which * half, half), half)
        term = mm3(high, low, wh[at, :], wl[at, :], ((1,), (1,)))
        for j, ref in enumerate(group):
            ref[...] = term[:, j * width : (j + 1) * width]


def middle(who, n, own, far, base, weight, cot):
    rows, hidden = cot.shape
    width = own.shape[1]
    tile = rows // 2
    part = pl.BlockSpec((tile, width), lambda i, s: (i, 0))
    wide = pl.BlockSpec((tile, hidden), lambda i, s: (i, 0))
    piece = jax.ShapeDtypeStruct((rows, width), F32)
    full = jax.ShapeDtypeStruct((rows, hidden), F32)
    out = pl.pallas_call(
        functools.partial(middle_kernel, n),
        grid_spec=pltpu.PrefetchScalarGridSpec(
            num_scalar_prefetch=1,
            grid=(rows // tile,),
            in_specs=[part, part, wide, pl.BlockSpec(weight.shape, lambda i, s: (0, 0)), wide],
            out_specs=[wide, wide] + [part] * (2 * n),
            scratch_shapes=[pltpu.VMEM(weight.shape, BF16)] * 2,
        ),
        out_shape=[full, full] + [piece] * (2 * n),
        compiler_params=pltpu.CompilerParams(vmem_limit_bytes=VMEM),
        cost_estimate=cost(24 * rows * width * n * hidden, 8e6),
        name="middle",
    )(who, own, far, base, weight, cot)
    return out[0], out[1], out[2 : 2 + n], out[2 + n :]


def weight_kernel(n, scale, keep_rows, who, *refs):
    own, far = refs[:n], refs[n : 2 * n]
    grad, outs, full = refs[2 * n], refs[2 * n + 1 : -1], refs[-1]
    half = full.shape[0] // 2
    gh, gl = split(grad[...])
    for group, at in ((own, who[1]), (far, 1 - who[1])):
        rows = jnp.concatenate([ref[...] for ref in group], axis=1)
        high, low = split(rows.T)
        term = mm3(high, low, gh, gl)
        full[pl.ds(pl.multiple_of(at * half, half), half), :] = term * scale
    hand_out(full, outs, who[2])


def hand_out(full, outs, place):
    rows = full.shape[0] // len(outs)
    place = place if len(outs) > 1 else 0
    for k, out in enumerate(outs):
        out[...] = full[pl.ds(pl.multiple_of((place ^ k) * rows, rows), rows), :]


def weight_term(who, own, far, grad, scale, pieces):
    n = len(own)
    rows, hidden = grad.shape
    depth = own[0].shape[1] * n * 2
    return pl.pallas_call(
        functools.partial(weight_kernel, n, scale, depth // pieces),
        in_specs=[pl.BlockSpec(memory_space=pltpu.SMEM)]
        + [pl.BlockSpec(memory_space=pltpu.VMEM)] * (2 * n + 1),
        out_specs=[pl.BlockSpec(memory_space=pltpu.VMEM)] * pieces,
        scratch_shapes=[pltpu.VMEM((depth, hidden), F32)],
        out_shape=[jax.ShapeDtypeStruct((depth // pieces, hidden), F32)] * pieces,
        compiler_params=pltpu.CompilerParams(vmem_limit_bytes=VMEM),
        cost_estimate=cost(6 * rows * depth * hidden, 4e6),
        name="weight_term",
    )(who, *own, *far, grad)


def add_kernel(count, at, who, *refs):
    parts, outs, full = refs[:count], refs[count:-1], refs[-1]
    total = parts[0][...]
    for part in parts[1:]:
        total = total + part[...]
    full[...] = total
    hand_out(full, outs, who[at])


def add_parts(name, who, at, parts, pieces):
    rows, hidden = parts[0].shape
    vmem = pl.BlockSpec(memory_space=pltpu.VMEM)
    return pl.pallas_call(
        functools.partial(add_kernel, len(parts), at),
        in_specs=[pl.BlockSpec(memory_space=pltpu.SMEM)] + [vmem] * len(parts),
        out_specs=[vmem] * pieces,
        scratch_shapes=[pltpu.VMEM((rows, hidden), F32)],
        out_shape=[jax.ShapeDtypeStruct((rows // pieces, hidden), F32)] * pieces,
        compiler_params=pltpu.CompilerParams(vmem_limit_bytes=VMEM),
        cost_estimate=cost(0, 1e5),
        name=name,
    )(who, *parts)


def join_kernel(at, who, *refs):
    parts, out = refs[:-1], refs[-1]
    rows = parts[0].shape[0]
    for k, part in enumerate(parts):
        out[pl.ds(pl.multiple_of((who[at] ^ k) * rows, rows), rows), :] = part[...]


def join_parts(name, who, at, parts):
    rows, hidden = parts[0].shape
    vmem = pl.BlockSpec(memory_space=pltpu.VMEM)
    return pl.pallas_call(
        functools.partial(join_kernel, at),
        in_specs=[pl.BlockSpec(memory_space=pltpu.SMEM)] + [vmem] * len(parts),
        out_specs=vmem,
        out_shape=jax.ShapeDtypeStruct((rows * len(parts), hidden), F32),
        compiler_params=pltpu.CompilerParams(vmem_limit_bytes=VMEM),
        cost_estimate=cost(0, 1e5),
        name=name,
    )(who, *parts)


def moved(value, axis, even, odd):
    peers = lax.axis_size(axis)
    perm = [(i, (i + (odd if i % 2 else even)) % peers) for i in range(peers)]
    return lax.ppermute(value, axis, perm)


def swapped(value, axis, bit):
    peers = lax.axis_size(axis)
    return lax.ppermute(value, axis, [(i, i ^ bit) for i in range(peers)])


def after(value, *others):
    return lax.optimization_barrier((value, *others))[0]


def spread(parts, stride):
    return [parts[0]] + [swapped(parts[k], "dom", k * stride) for k in range(1, len(parts))]


def body(features, weight, cotangent, block_rows, block_cols, block_counts, block_values):
    rows_here = features.shape[0]
    width = features.shape[1] // CHUNKS
    parts = lax.axis_size("dom")
    place = lax.axis_index("dom").astype(jnp.int32)
    odd = place & 1
    side = lax.axis_index("feat").astype(jnp.int32)
    who = jnp.stack([place, side, place & 3, (place >> 2) & 3, 1 + 2 * odd, 3 - 2 * odd])
    near_slot, far_slot = -4, -5

    pieces = [features[:, i * width : (i + 1) * width] for i in range(CHUNKS)]
    far = moved(features, "dom", 1, 3)
    nears = [moved(piece, "dom", 3, 1) for piece in pieces]

    ah, al, th, tl, mark = lay_out(
        block_rows[0], block_cols[0], block_counts, who, block_values[0], rows_here
    )

    starts = []
    for i, piece in enumerate(pieces):
        terms = [(0, [piece]), (far_slot, [after(far, *starts)], i * width)]
        starts.append(product("agg_a", who, ah, al, terms))
    own = []
    received = []
    base = None
    for i, (total, near) in enumerate(zip(starts, nears)):
        near = after(near, *own, *starts)
        two = swapped(near, "dom", 1)
        if received:
            base = pre_term(who, i - 1, own[-1], received[-1], weight, base)
            total = after(total, base)
        total = product("agg_b", who, ah, al, [(near_slot, [near]), (2, [two])], [total])
        own.append(total)
        received.append(swapped(total, "feat", 1))
    activated, pre_grad, g_own, g_far = middle(
        who, CHUNKS, own[-1], received[-1], base, weight, cotangent
    )
    g_parts = [(mine, swapped(other, "feat", 1)) for mine, other in zip(g_own, g_far)]

    scale = 1.0 / math.sqrt(rows_here * parts)
    quick = parts == 16
    terms = weight_term(who, own, received, pre_grad, scale, 4 if quick else 1)
    if quick:
        held = add_parts("add_near", who, 3, spread(terms, 1), 4)
        sent = spread(held, 4)
        last = held[0]
    else:
        weight_grad = lax.psum(terms[0], "dom")
        last = terms[0]

    nears = []
    mines = []
    for i, g in enumerate(g_parts):
        g = (after(g[0], last), g[1])
        last = product("back_two", who, th, tl, [(2, g)])
        two = swapped(last, "dom", 1)
        last = product("back_far", who, th, tl, [(far_slot, [after(g[0], last), g[1]])])
        far = moved(last, "dom", -3, -1)
        if quick and i == 1:
            last = join_parts("join_away", who, 3, [after(sent[0], last), *sent[1:]])
            sent = spread([last] * 4, 1)
        last = product(
            "back_near", who, th, tl, [(near_slot, [after(g[0], last, *nears), g[1]])], [two]
        )
        nears.append(moved(last, "dom", -1, -3))
        if quick and i == 0:
            last = add_parts("add_away", who, 0, [after(sent[0], last), *sent[1:]], 1)[0]
            sent = spread([last] * 4, 4)
        if quick and i == 1:
            last = join_parts("join_near", who, 2, [after(sent[0], last), *sent[1:]])
            weight_grad = last
        last = product("back_own", who, th, tl, [(0, [after(g[0], last), g[1]])], [far])
        mines.append(last)
    feature_grad = jnp.concatenate([mine + near for mine, near in zip(mines, nears)], axis=1)
    return (activated, feature_grad, weight_grad)


def solution(mesh):
    in_specs = (
        P("dom", "feat"),
        P(None, "feat"),
        P("dom", "feat"),
        P("dom", None, None),
        P("dom", None, None),
        P("dom", None),
        P("dom", None, None, None, None),
    )
    out_specs = (P("dom", "feat"), P("dom", "feat"), P(None, "feat"))
    return jax.shard_map(body, mesh=mesh, in_specs=in_specs, out_specs=out_specs, check_vma=False)
```

```python
import functools
import math

import jax
import jax.numpy as jnp
from jax import lax
from jax.experimental import pallas as pl
from jax.experimental.pallas import tpu as pltpu
from jax.sharding import PartitionSpec as P

F32 = jnp.float32
BF16 = jnp.bfloat16
TILE = 256
GROUP = 4
LIMIT = 12 * 1024 * 1024
IN_VMEM = pl.BlockSpec(memory_space=pltpu.VMEM)
IN_SMEM = pl.BlockSpec(memory_space=pltpu.SMEM)

SIDE, NEAR, FAR, TWO, OWN = range(5)


def split(value):
    high = value.astype(BF16)
    low = (value - high.astype(F32)).astype(BF16)
    return high, low


def mm(a, b, dims=((1,), (0,))):
    return lax.dot_general(a, b, (dims, ((), ())), preferred_element_type=F32)


def mm3(a, b, dims=((1,), (0,))):
    (ah, al), (bh, bl) = a, b
    return mm(ah, bh, dims) + (mm(ah, bl, dims) + mm(al, bh, dims))


def call(name, kernel, who, operands, shapes, scratch=(), flops=0, place=pltpu.VMEM):
    moved = sum(a.size * a.dtype.itemsize for a in operands)
    pinned = [pltpu.with_memory_space_constraint(a, pltpu.VMEM) for a in operands]
    return pl.pallas_call(
        kernel,
        in_specs=[IN_SMEM] + [IN_VMEM] * len(operands),
        out_specs=[IN_VMEM] * len(shapes),
        out_shape=[place(*shape) for shape in shapes],
        scratch_shapes=list(scratch),
        compiler_params=pltpu.CompilerParams(vmem_limit_bytes=LIMIT),
        cost_estimate=pl.CostEstimate(flops=int(flops), bytes_accessed=moved, transcendentals=0),
        name=name,
    )(who, *pinned)


def lay_out_kernel(rows, cols, counts, who, blocks, ah, al, th, tl):
    slot = pl.program_id(0)
    cap = blocks.shape[1]
    size = blocks.shape[2]
    for out in (ah, al, th, tl):
        out[slot] = jnp.zeros(out.shape[1:], out.dtype)

    def one(k, carry):
        r = pl.multiple_of(rows[slot, k] * size, size)
        c = pl.multiple_of(cols[slot, k] * size, size)
        block = blocks[0, k]
        high, low = split(block)
        ah[slot, pl.ds(r, size), pl.ds(c, size)] = high
        al[slot, pl.ds(r, size), pl.ds(c, size)] = low
        high, low = split(block.T)
        th[slot, pl.ds(c, size), pl.ds(r, size)] = high
        tl[slot, pl.ds(c, size), pl.ds(r, size)] = low
        return carry

    lax.fori_loop(0, jnp.minimum(counts[0, slot], cap), one, 0)


def lay_out(rows, cols, counts, who, blocks, size_all):
    window, cap, size, _ = blocks.shape
    shape = pltpu.VMEM((window, size_all, size_all), BF16)
    return pl.pallas_call(
        lay_out_kernel,
        grid_spec=pltpu.PrefetchScalarGridSpec(
            num_scalar_prefetch=4,
            grid=(window,),
            in_specs=[pl.BlockSpec((1, cap, size, size), lambda s, *_: (s, 0, 0, 0))],
            out_specs=[IN_VMEM] * 4,
        ),
        out_shape=[shape] * 4,
        compiler_params=pltpu.CompilerParams(vmem_limit_bytes=LIMIT),
        cost_estimate=pl.CostEstimate(flops=0, bytes_accessed=20_000_000, transcendentals=0),
        name="lay_out",
    )(rows, cols, counts, who, blocks)


def forward_kernel(slots, part, has_base, who, mh, ml, *refs):
    n = len(slots)
    sources, refs = refs[:n], refs[n:]
    base, refs = (refs[0], refs[1:]) if has_base else (None, refs)
    out, (highs, lows) = refs[0], refs[1:]
    rows = out.shape[0]
    from_row = 0 if part is None else pl.multiple_of((who[SIDE] ^ part) * rows, rows)
    here = pl.ds(from_row, rows)
    for i, source in enumerate(sources):
        highs[i], lows[i] = split(source[...])

    def step(start):
        deep = pl.ds(start, TILE)
        total = None
        for i, slot in enumerate(slots):
            at = who[slot]
            a = mh[at, here, deep], ml[at, here, deep]
            term = mm3(a, (highs[i, deep, :], lows[i, deep, :]))
            total = term if total is None else total + term
        return total

    first = step(0)
    if base is not None:
        first = first + (base[here, :] if base.shape[0] > rows else base[...])
    out[...] = first

    def more(k, carry):
        out[...] += step(pl.multiple_of(k * TILE, TILE))
        return carry

    lax.fori_loop(1, mh.shape[2] // TILE, more, 0)


def forward(name, who, mh, ml, terms, base=None, part=None):
    slots = [slot for slot, _ in terms]
    sources = [source for _, source in terms]
    depth, width = sources[0].shape
    rows = mh.shape[1] // (1 if part is None else 2)
    extra = [] if base is None else [base]
    return call(
        name,
        functools.partial(forward_kernel, slots, part, base is not None),
        who,
        [mh, ml, *sources, *extra],
        [((rows, width), F32)],
        [pltpu.VMEM((len(terms), depth, width), BF16)] * 2,
        6 * len(terms) * rows * depth * width,
    )[0]


def backward_kernel(slots, part, n_add, who, mh, ml, source, *refs):
    addends, outs, (high, low) = refs[:n_add], refs[n_add:-2], refs[-2:]
    depth = source.shape[0]
    high[...], low[...] = split(source[...])
    from_col = pl.multiple_of((who[SIDE] ^ part) * depth, depth)
    for i, (slot, out) in enumerate(zip(slots, outs)):
        at = who[slot]

        def step(start):
            deep = pl.ds(start, TILE)
            cols = pl.ds(pl.multiple_of(from_col + start, TILE), TILE)
            return mm3((mh[at, :, cols], ml[at, :, cols]), (high[deep, :], low[deep, :]))

        total = step(0)
        for addend in addends:
            total = total + addend[...]
        out[...] = total

        def more(k, carry):
            out[...] += step(pl.multiple_of(k * TILE, TILE))
            return carry

        lax.fori_loop(1, depth // TILE, more, 0)


def backward(name, who, mh, ml, slots, source, addends, part):
    depth, width = source.shape
    rows = mh.shape[1]
    return call(
        name,
        functools.partial(backward_kernel, slots, part, len(addends)),
        who,
        [mh, ml, source, *addends],
        [((rows, width), F32)] * len(slots),
        [pltpu.VMEM((depth, width), BF16)] * 2,
        6 * len(slots) * rows * depth * width,
    )


def middle_kernel(who, own, far, w_here, w_there, cot_here, cot_there, *outs):
    act_here, act_there, grad_here, grad_there, g_there = outs
    half = own.shape[1]

    def rows_of(w, which):
        return split(w[pl.ds(pl.multiple_of((who[SIDE] ^ which) * half, half), half), :])

    source = split(own[...]), split(far[...])
    total = None
    for w, cot, act, grad in (
        (w_here, cot_here, act_here, grad_here),
        (w_there, cot_there, act_there, grad_there),
    ):
        pre = mm3(source[0], rows_of(w, 0)) + mm3(source[1], rows_of(w, 1))
        s = 1.0 / (1.0 + jnp.exp(-pre))
        act[...] = pre * s
        pg = cot[...] * (s + pre * s * (1.0 - s))
        grad[...] = pg
        term = mm3(split(pg), rows_of(w, 1), ((1,), (1,)))
        total = term if total is None else total + term
    g_there[...] = total


def middle(who, own, far, w_here, w_there, cot_here, cot_there):
    shape = (cot_there.shape, F32)
    flops = 36 * own.shape[0] * own.shape[1] * w_here.shape[1]
    operands = [own, far, w_here, w_there, cot_here, cot_there]
    return call("middle", middle_kernel, who, operands, [shape] * 5, flops=flops)


def keep_kernel(who, w_here, w_there, grad_here, grad_there, g_here):
    half = g_here.shape[1]
    at = pl.ds(pl.multiple_of(who[SIDE] * half, half), half)
    total = None
    for w, grad in ((w_here, grad_here), (w_there, grad_there)):
        term = mm3(split(grad[...]), split(w[at, :]), ((1,), (1,)))
        total = term if total is None else total + term
    g_here[...] = total


def weight_kernel(scale, who, own, far, grad_here, grad_there, here, there):
    half = own.shape[1]
    grads = split(grad_here[...]), split(grad_there[...])
    for rows, which in ((own, 0), (far, 1)):
        turned = split(rows[...].T)
        at = pl.ds(pl.multiple_of((who[SIDE] ^ which) * half, half), half)
        for grad, out in zip(grads, (here, there)):
            out[at, :] = mm3(turned, grad) * scale


def half_kernel(which, who, whole, out):
    rows = out.shape[0]
    out[...] = whole[pl.ds(pl.multiple_of((who[SIDE] ^ which) * rows, rows), rows), :]


def join_kernel(who, here, there, out):
    rows = here.shape[0]
    for ref, which in ((here, 0), (there, 1)):
        out[pl.ds(pl.multiple_of((who[SIDE] ^ which) * rows, rows), rows), :] = ref[...]


def add_kernel(who, *refs):
    total = refs[0][...]
    for ref in refs[1:-1]:
        total = total + ref[...]
    refs[-1][...] = total


def sum_kernel(copies, who, parts, out):
    total = parts[0]
    for k in range(1, parts.shape[0]):
        total = total + parts[k]
    if copies:
        for k in range(copies):
            out[k] = total
    else:
        out[...] = total


def copies_kernel(who, value, out):
    for k in range(out.shape[0]):
        out[k] = value[...]


def moved(value, axis, even, odd):
    peers = lax.axis_size(axis)
    perm = [(i, (i + (odd if i % 2 else even)) % peers) for i in range(peers)]
    return lax.ppermute(value, axis, perm)


def swapped(value, axis):
    peers = lax.axis_size(axis)
    return lax.ppermute(value, axis, [(i, i ^ 1) for i in range(peers)])


def exchanged(value, axis, groups):
    return lax.all_to_all(value, axis, 0, 0, axis_index_groups=groups)


def after(value, *others):
    return lax.optimization_barrier((value, *others))[0]


def body(features, weight, cotangent, block_rows, block_cols, block_counts, block_values):
    rows, width = features.shape
    hidden = weight.shape[1]
    depth = weight.shape[0]
    parts = lax.axis_size("dom")
    odd = lax.axis_index("dom").astype(jnp.int32) & 1
    side = lax.axis_index("feat").astype(jnp.int32)
    zero = odd * 0
    who = jnp.stack([side, 1 + 2 * odd, 3 - 2 * odd, zero + 2, zero])

    near = moved(features, "dom", 3, 1)
    far = moved(features, "dom", 1, 3)
    w_there = swapped(weight, "feat")
    half_shape = ((rows // 2, hidden), F32)
    cot_here = call("cot_here", functools.partial(half_kernel, 0), who, [cotangent], [half_shape])[0]
    cot_give = call("cot_give", functools.partial(half_kernel, 1), who, [cotangent], [half_shape])[0]
    cot_there = swapped(cot_give, "feat")

    ah, al, th, tl = lay_out(
        block_rows[0], block_cols[0], block_counts, who, block_values[0], rows
    )
    total = forward("agg_own", who, ah, al, [(OWN, features)])
    near = after(near, total, w_there, cot_there)
    two = swapped(near, "dom")
    total = forward("agg_near", who, ah, al, [(NEAR, near)], total)
    far = after(far, total)
    give = forward("agg_far", who, ah, al, [(FAR, far)], total, 1)
    give = forward("agg_two", who, ah, al, [(TWO, two)], give, 1)
    there = swapped(give, "feat")
    keep = forward("agg_keep", who, ah, al, [(FAR, far), (TWO, after(two, give))], total, 0)

    act_here, act_there, grad_here, grad_there, g_give = middle(
        who, keep, there, weight, w_there, cot_here, cot_there
    )
    g_there = swapped(g_give, "feat")
    g_here = call(
        "keep",
        keep_kernel,
        who,
        [weight, w_there, grad_here, grad_there],
        [(keep.shape, F32)],
        flops=12 * rows // 2 * width * hidden,
    )[0]
    firsts = backward("back_here", who, th, tl, [TWO, FAR, NEAR, OWN], g_here, [], 0)
    scale = 1.0 / math.sqrt(rows * parts)
    w_term, w_give = call(
        "weight_term",
        functools.partial(weight_kernel, scale),
        who,
        [after(keep, firsts[0]), there, grad_here, grad_there],
        [(weight.shape, F32)] * 2,
        flops=12 * rows // 2 * depth * hidden,
    )
    w_got = swapped(w_give, "feat")
    act_got = swapped(act_there, "feat")

    g_there = after(g_there, w_term)
    last = backward("back_two", who, th, tl, [TWO], g_there, [firsts[0]], 1)[0]
    two = swapped(last, "dom")
    last = backward("back_far", who, th, tl, [FAR], after(g_there, last), [firsts[1]], 1)[0]
    far = moved(last, "dom", -3, -1)
    last = backward("back_near", who, th, tl, [NEAR], after(g_there, last), [firsts[2], two], 1)[0]
    near = moved(last, "dom", -1, -3)
    mine = backward("back_own", who, th, tl, [OWN], after(g_there, last), [firsts[3]], 1)[0]

    w_sum = call("weight_add", add_kernel, who, [after(w_term, mine), w_got], [(weight.shape, F32)])[0]
    if parts % GROUP == 0 and depth % parts == 0:
        away = parts // GROUP
        groups = [[GROUP * i + j for j in range(GROUP)] for i in range(away)]
        lines = [[GROUP * i + j for i in range(away)] for j in range(GROUP)]
        quarter = (depth // GROUP, hidden)
        sliver = (depth // parts, hidden)
        got = exchanged(w_sum.reshape(GROUP, *quarter), "dom", groups)
        got = call("sum_near", functools.partial(sum_kernel, 0), who, [got], [(quarter, F32)])[0]
        got = exchanged(got.reshape(away, *sliver), "dom", lines)
        got = call(
            "sum_away", functools.partial(sum_kernel, away), who, [got], [((away, *sliver), F32)]
        )[0]
        got = exchanged(got, "dom", lines).reshape(quarter)
        got = call("copies", copies_kernel, who, [got], [((GROUP, *quarter), F32)])[0]
        weight_grad = exchanged(got, "dom", groups).reshape(weight.shape)
    else:
        weight_grad = lax.psum(w_sum, "dom")
    activated = call(
        "activated",
        join_kernel,
        who,
        [after(act_here, weight_grad), act_got],
        [(features.shape, F32)],
        place=jax.ShapeDtypeStruct,
    )[0]
    feature_grad = mine + far + near
    return (activated, feature_grad, weight_grad)


def solution(mesh):
    in_specs = (
        P("dom", "feat"),
        P(None, "feat"),
        P("dom", "feat"),
        P("dom", None, None),
        P("dom", None, None),
        P("dom", None),
        P("dom", None, None, None, None),
    )
    out_specs = (P("dom", "feat"), P("dom", "feat"), P(None, "feat"))
    return jax.shard_map(body, mesh=mesh, in_specs=in_specs, out_specs=out_specs, check_vma=False)
```

```python
import functools
import math

import jax
import jax.numpy as jnp
from jax import lax
from jax.experimental import pallas as pl
from jax.experimental.pallas import tpu as pltpu
from jax.sharding import PartitionSpec as P

F32 = jnp.float32
BF16 = jnp.bfloat16
TILE = 256
GROUP = 4
LIMIT = 12 * 1024 * 1024
IN_VMEM = pl.BlockSpec(memory_space=pltpu.VMEM)
IN_SMEM = pl.BlockSpec(memory_space=pltpu.SMEM)

SIDE, CORE, NEAR, FAR, TWO, OWN = range(6)


def split(value):
    high = value.astype(BF16)
    low = (value - high.astype(F32)).astype(BF16)
    return high, low


def mm(a, b, dims=((1,), (0,))):
    return lax.dot_general(a, b, (dims, ((), ())), preferred_element_type=F32)


def mm3(a, b, dims=((1,), (0,))):
    (ah, al), (bh, bl) = a, b
    return mm(ah, bh, dims) + (mm(ah, bl, dims) + mm(al, bh, dims))


def call(name, kernel, who, operands, shapes, scratch=(), flops=0, place=pltpu.VMEM):
    moved = sum(a.size * a.dtype.itemsize for a in operands)
    pinned = [pltpu.with_memory_space_constraint(a, pltpu.VMEM) for a in operands]
    return pl.pallas_call(
        kernel,
        in_specs=[IN_SMEM] + [IN_VMEM] * len(operands),
        out_specs=[IN_VMEM] * len(shapes),
        out_shape=[place(*shape) for shape in shapes],
        scratch_shapes=list(scratch),
        compiler_params=pltpu.CompilerParams(vmem_limit_bytes=LIMIT),
        cost_estimate=pl.CostEstimate(flops=int(flops), bytes_accessed=moved, transcendentals=0),
        name=name,
    )(who, *pinned)


def lay_out_kernel(rows, cols, counts, who, blocks, ah, al, th, tl):
    slot = pl.program_id(0)
    cap = blocks.shape[1]
    size = blocks.shape[2]
    for out in (ah, al, th, tl):
        out[slot] = jnp.zeros(out.shape[1:], out.dtype)

    def one(k, carry):
        r = pl.multiple_of(rows[slot, k] * size, size)
        c = pl.multiple_of(cols[slot, k] * size, size)
        block = blocks[0, k]
        high, low = split(block)
        ah[slot, pl.ds(r, size), pl.ds(c, size)] = high
        al[slot, pl.ds(r, size), pl.ds(c, size)] = low
        high, low = split(block.T)
        th[slot, pl.ds(c, size), pl.ds(r, size)] = high
        tl[slot, pl.ds(c, size), pl.ds(r, size)] = low
        return carry

    lax.fori_loop(0, jnp.minimum(counts[0, slot], cap), one, 0)


def lay_out(rows, cols, counts, who, blocks, size_all):
    window, cap, size, _ = blocks.shape
    shape = pltpu.VMEM((window, size_all, size_all), BF16)
    return pl.pallas_call(
        lay_out_kernel,
        grid_spec=pltpu.PrefetchScalarGridSpec(
            num_scalar_prefetch=4,
            grid=(window,),
            in_specs=[pl.BlockSpec((1, cap, size, size), lambda s, *_: (s, 0, 0, 0))],
            out_specs=[IN_VMEM] * 4,
        ),
        out_shape=[shape] * 4,
        compiler_params=pltpu.CompilerParams(vmem_limit_bytes=LIMIT),
        cost_estimate=pl.CostEstimate(flops=0, bytes_accessed=20_000_000, transcendentals=0),
        name="lay_out",
    )(rows, cols, counts, who, blocks)


def forward_kernel(slots, part, has_base, who, mh, ml, *refs):
    n = len(slots)
    sources, refs = refs[:n], refs[n:]
    base, refs = (refs[0], refs[1:]) if has_base else (None, refs)
    out, (highs, lows) = refs[0], refs[1:]
    rows = out.shape[0]
    from_row = 0 if part is None else (who[SIDE] ^ part) * rows
    for i, source in enumerate(sources):
        highs[i], lows[i] = split(source[...])

    def tile(k, carry):
        there = pl.ds(pl.multiple_of(k * TILE, TILE), TILE)
        here = pl.ds(pl.multiple_of(from_row + k * TILE, TILE), TILE)
        total = None
        if base is not None:
            total = base[here if base.shape[0] > rows else there, :]
        for i, slot in enumerate(slots):
            at = who[slot]
            term = mm3((mh[at, here, :], ml[at, here, :]), (highs[i], lows[i]))
            total = term if total is None else total + term
        out[there, :] = total
        return carry

    lax.fori_loop(0, rows // TILE, tile, 0)


def forward(name, who, mh, ml, terms, base=None, part=None):
    slots = [slot for slot, _ in terms]
    sources = [source for _, source in terms]
    depth, width = sources[0].shape
    rows = mh.shape[1] // (1 if part is None else 2)
    extra = [] if base is None else [base]
    return call(
        name,
        functools.partial(forward_kernel, slots, part, base is not None),
        who,
        [mh, ml, *sources, *extra],
        [((rows, width), F32)],
        [pltpu.VMEM((len(terms), depth, width), BF16)] * 2,
        6 * len(terms) * rows * depth * width,
    )[0]


def backward_kernel(slots, part, n_add, who, mh, ml, source, *refs):
    addends, outs, (high, low) = refs[:n_add], refs[n_add:-2], refs[-2:]
    depth = source.shape[0]
    rows = outs[0].shape[0]
    high[...], low[...] = split(source[...])
    deep = pl.ds(pl.multiple_of((who[SIDE] ^ part) * depth, depth), depth)

    def tile(k, carry):
        here = pl.ds(pl.multiple_of(k * TILE, TILE), TILE)
        for slot, out in zip(slots, outs):
            at = who[slot]
            total = mm3((mh[at, here, deep], ml[at, here, deep]), (high[...], low[...]))
            for addend in addends:
                total = total + addend[here, :]
            out[here, :] = total
        return carry

    lax.fori_loop(0, rows // TILE, tile, 0)


def backward(name, who, mh, ml, slots, source, addends, part):
    depth, width = source.shape
    rows = mh.shape[1]
    return call(
        name,
        functools.partial(backward_kernel, slots, part, len(addends)),
        who,
        [mh, ml, source, *addends],
        [((rows, width), F32)] * len(slots),
        [pltpu.VMEM((depth, width), BF16)] * 2,
        6 * len(slots) * rows * depth * width,
    )


def middle_kernel(who, own, far, w_here, w_there, cot_here, cot_there, *outs):
    act_here, act_there, grad_here, grad_there, g_there = outs
    half = own.shape[1]

    def rows_of(w, which):
        return split(w[pl.ds(pl.multiple_of((who[SIDE] ^ which) * half, half), half), :])

    source = split(own[...]), split(far[...])
    total = None
    for w, cot, act, grad in (
        (w_here, cot_here, act_here, grad_here),
        (w_there, cot_there, act_there, grad_there),
    ):
        pre = mm3(source[0], rows_of(w, 0)) + mm3(source[1], rows_of(w, 1))
        s = 1.0 / (1.0 + jnp.exp(-pre))
        act[...] = pre * s
        pg = cot[...] * (s + pre * s * (1.0 - s))
        grad[...] = pg
        term = mm3(split(pg), rows_of(w, 1), ((1,), (1,)))
        total = term if total is None else total + term
    g_there[...] = total


def middle(who, own, far, w_here, w_there, cot_here, cot_there):
    shape = (cot_there.shape, F32)
    flops = 36 * own.shape[0] * own.shape[1] * w_here.shape[1]
    operands = [own, far, w_here, w_there, cot_here, cot_there]
    return call("middle", middle_kernel, who, operands, [shape] * 5, flops=flops)


def keep_kernel(who, w_here, w_there, grad_here, grad_there, g_here):
    half = g_here.shape[1]
    at = pl.ds(pl.multiple_of(who[SIDE] * half, half), half)
    total = None
    for w, grad in ((w_here, grad_here), (w_there, grad_there)):
        term = mm3(split(grad[...]), split(w[at, :]), ((1,), (1,)))
        total = term if total is None else total + term
    g_here[...] = total


def weight_kernel(scale, who, own, far, grad_here, grad_there, keep, give, full):
    half = own.shape[1]
    hidden = grad_here.shape[1]
    grads = split(grad_here[...]), split(grad_there[...])
    for rows, which in ((own, 0), (far, 1)):
        turned = split(rows[...].T)
        at = pl.ds(pl.multiple_of((who[SIDE] ^ which) * half, half), half)
        for i, grad in enumerate(grads):
            full[at, i * hidden : (i + 1) * hidden] = mm3(turned, grad) * scale
    rows = keep.shape[0]
    for out, which in ((keep, 0), (give, 1)):
        out[...] = full[pl.ds(pl.multiple_of((who[CORE] ^ which) * rows, rows), rows), :]


def half_kernel(which, who, whole, out):
    rows = out.shape[0]
    out[...] = whole[pl.ds(pl.multiple_of((who[SIDE] ^ which) * rows, rows), rows), :]


def join_kernel(place, who, here, there, out):
    rows = here.shape[0]
    for ref, which in ((here, 0), (there, 1)):
        out[pl.ds(pl.multiple_of((who[place] ^ which) * rows, rows), rows), :] = ref[...]


def add_kernel(who, *refs):
    total = refs[0][...]
    for ref in refs[1:-1]:
        total = total + ref[...]
    refs[-1][...] = total


def sliver_kernel(who, parts, here, there):
    total = parts[0]
    for k in range(1, parts.shape[0]):
        total = total + parts[k]
    half = here.shape[1]
    here[...] = total[:, :half]
    there[...] = total[:, half:]


def copies_kernel(who, here, there, out):
    total = here[...] + there[...]
    for k in range(out.shape[0]):
        out[k] = total


def moved(value, axis, even, odd):
    peers = lax.axis_size(axis)
    perm = [(i, (i + (odd if i % 2 else even)) % peers) for i in range(peers)]
    return lax.ppermute(value, axis, perm)


def swapped(value, axis):
    peers = lax.axis_size(axis)
    return lax.ppermute(value, axis, [(i, i ^ 1) for i in range(peers)])


def exchanged(value, axis, groups):
    return lax.all_to_all(value, axis, 0, 0, axis_index_groups=groups)


def after(value, *others):
    return lax.optimization_barrier((value, *others))[0]


def body(features, weight, cotangent, block_rows, block_cols, block_counts, block_values):
    rows, width = features.shape
    hidden = weight.shape[1]
    depth = weight.shape[0]
    parts = lax.axis_size("dom")
    odd = lax.axis_index("dom").astype(jnp.int32) & 1
    side = lax.axis_index("feat").astype(jnp.int32)
    zero = odd * 0
    who = jnp.stack([side, odd, 1 + 2 * odd, 3 - 2 * odd, zero + 2, zero])

    near = moved(features, "dom", 3, 1)
    far = moved(features, "dom", 1, 3)
    w_there = swapped(weight, "feat")
    half_shape = ((rows // 2, hidden), F32)
    cot_here = call("cot_here", functools.partial(half_kernel, 0), who, [cotangent], [half_shape])[0]
    cot_give = call("cot_give", functools.partial(half_kernel, 1), who, [cotangent], [half_shape])[0]
    cot_there = swapped(cot_give, "feat")

    ah, al, th, tl = lay_out(
        block_rows[0], block_cols[0], block_counts, who, block_values[0], rows
    )
    total = forward("agg_own", who, ah, al, [(OWN, features)])
    near = after(near, total, w_there, cot_there)
    two = swapped(near, "dom")
    total = forward("agg_near", who, ah, al, [(NEAR, near)], total)
    far = after(far, total)
    give = forward("agg_far", who, ah, al, [(FAR, far)], total, 1)
    give = forward("agg_two", who, ah, al, [(TWO, two)], give, 1)
    there = swapped(give, "feat")
    keep = forward("agg_keep", who, ah, al, [(FAR, far), (TWO, after(two, give))], total, 0)

    act_here, act_there, grad_here, grad_there, g_give = middle(
        who, keep, there, weight, w_there, cot_here, cot_there
    )
    g_there = swapped(g_give, "feat")
    g_here = call(
        "keep",
        keep_kernel,
        who,
        [weight, w_there, grad_here, grad_there],
        [(keep.shape, F32)],
        flops=12 * rows // 2 * width * hidden,
    )[0]
    scale = 1.0 / math.sqrt(rows * parts)
    w_half = (depth // 2, 2 * hidden)
    w_keep, w_give = call(
        "weight_term",
        functools.partial(weight_kernel, scale),
        who,
        [keep, there, grad_here, grad_there],
        [(w_half, F32)] * 2,
        [pltpu.VMEM((depth, 2 * hidden), F32)],
        flops=12 * rows // 2 * depth * hidden,
    )
    w_got = swapped(w_give, "dom")
    lines = parts // 2
    groups = [[2 * i + core for i in range(lines)] for core in range(2)]
    w_half_sum = call("core_sum", add_kernel, who, [after(w_keep, g_here), w_got], [(w_half, F32)])[0]
    firsts = backward(
        "back_here", who, th, tl, [TWO, FAR, NEAR, OWN], after(g_here, w_half_sum), [], 0
    )
    sliver = (depth // parts, hidden)
    w_parts = exchanged(w_half_sum.reshape(lines, depth // parts, 2 * hidden), "dom", groups)

    last = backward(
        "back_two", who, th, tl, [TWO], after(g_there, firsts[0]), [firsts[0]], 1
    )[0]
    two = swapped(last, "dom")
    last = backward("back_far", who, th, tl, [FAR], after(g_there, last), [firsts[1]], 1)[0]
    far = moved(last, "dom", -3, -1)
    w_here, w_give = call(
        "slivers", sliver_kernel, who, [after(w_parts, last)], [(sliver, F32)] * 2
    )
    w_got = swapped(w_give, "feat")
    act_got = swapped(after(act_there, w_here), "feat")
    last = backward("back_near", who, th, tl, [NEAR], after(g_there, w_here), [firsts[2], two], 1)[0]
    near = moved(last, "dom", -1, -3)
    mine = backward("back_own", who, th, tl, [OWN], after(g_there, last), [firsts[3]], 1)[0]
    w_all = call(
        "copies", copies_kernel, who, [after(w_here, mine), w_got], [((lines, *sliver), F32)]
    )[0]
    w_own = exchanged(w_all, "dom", groups).reshape(depth // 2, hidden)
    activated = call(
        "activated",
        functools.partial(join_kernel, SIDE),
        who,
        [after(act_here, w_all), act_got],
        [(features.shape, F32)],
        place=jax.ShapeDtypeStruct,
    )[0]
    weight_grad = call(
        "weight_grad",
        functools.partial(join_kernel, CORE),
        who,
        [w_own, swapped(w_own, "dom")],
        [(weight.shape, F32)],
        place=jax.ShapeDtypeStruct,
    )[0]
    feature_grad = mine + far + near
    return (activated, feature_grad, weight_grad)


def solution(mesh):
    in_specs = (
        P("dom", "feat"),
        P(None, "feat"),
        P("dom", "feat"),
        P("dom", None, None),
        P("dom", None, None),
        P("dom", None),
        P("dom", None, None, None, None),
    )
    out_specs = (P("dom", "feat"), P("dom", "feat"), P(None, "feat"))
    return jax.shard_map(body, mesh=mesh, in_specs=in_specs, out_specs=out_specs, check_vma=False)
```

```python
import functools
import math

import jax
import jax.numpy as jnp
from jax import lax
from jax.experimental import pallas as pl
from jax.experimental.pallas import tpu as pltpu
from jax.sharding import PartitionSpec as P

F32 = jnp.float32
BF16 = jnp.bfloat16
TILE = 256
CHUNKS = 2
LIMIT = 8 * 1024 * 1024
IN_VMEM = pl.BlockSpec(memory_space=pltpu.VMEM)
IN_SMEM = pl.BlockSpec(memory_space=pltpu.SMEM)

SIDE, CORE, NEAR, FAR, TWO, OWN, CHIP, LAYER, PAIR = range(9)


def split(value):
    high = value.astype(BF16)
    low = (value - high.astype(F32)).astype(BF16)
    return high, low


def mm(a, b, dims=((1,), (0,))):
    return lax.dot_general(a, b, (dims, ((), ())), preferred_element_type=F32)


def mm3(a, b, dims=((1,), (0,))):
    (ah, al), (bh, bl) = a, b
    return mm(ah, bh, dims) + (mm(ah, bl, dims) + mm(al, bh, dims))


def call(name, kernel, who, operands, shapes, scratch=(), flops=0, place=pltpu.VMEM):
    moved = sum(a.size * a.dtype.itemsize for a in operands)
    pinned = [pltpu.with_memory_space_constraint(a, pltpu.VMEM) for a in operands]
    return pl.pallas_call(
        kernel,
        in_specs=[IN_SMEM] + [IN_VMEM] * len(operands),
        out_specs=[IN_VMEM] * len(shapes),
        out_shape=[place(*shape) for shape in shapes],
        scratch_shapes=list(scratch),
        compiler_params=pltpu.CompilerParams(vmem_limit_bytes=LIMIT),
        cost_estimate=pl.CostEstimate(flops=int(flops), bytes_accessed=moved, transcendentals=0),
        name=name,
    )(who, *pinned)


def lay_out_kernel(rows, cols, counts, who, blocks, ah, al, th, tl):
    slot = pl.program_id(0)
    cap = blocks.shape[1]
    size = blocks.shape[2]
    for out in (ah, al, th, tl):
        out[slot] = jnp.zeros(out.shape[1:], out.dtype)

    def one(k, carry):
        r = pl.multiple_of(rows[slot, k] * size, size)
        c = pl.multiple_of(cols[slot, k] * size, size)
        block = blocks[0, k]
        high, low = split(block)
        ah[slot, pl.ds(r, size), pl.ds(c, size)] = high
        al[slot, pl.ds(r, size), pl.ds(c, size)] = low
        high, low = split(block.T)
        th[slot, pl.ds(c, size), pl.ds(r, size)] = high
        tl[slot, pl.ds(c, size), pl.ds(r, size)] = low
        return carry

    lax.fori_loop(0, jnp.minimum(counts[0, slot], cap), one, 0)


def lay_out(rows, cols, counts, who, blocks, size_all):
    window, cap, size, _ = blocks.shape
    shape = pltpu.VMEM((window, size_all, size_all), BF16)
    return pl.pallas_call(
        lay_out_kernel,
        grid_spec=pltpu.PrefetchScalarGridSpec(
            num_scalar_prefetch=4,
            grid=(window,),
            in_specs=[pl.BlockSpec((1, cap, size, size), lambda s, *_: (s, 0, 0, 0))],
            out_specs=[IN_VMEM] * 4,
        ),
        out_shape=[shape] * 4,
        compiler_params=pltpu.CompilerParams(vmem_limit_bytes=LIMIT),
        cost_estimate=pl.CostEstimate(flops=0, bytes_accessed=20_000_000, transcendentals=0),
        name="lay_out",
    )(rows, cols, counts, who, pltpu.with_memory_space_constraint(blocks, pltpu.HBM))


def forward_kernel(slots, part, has_base, who, mh, ml, *refs):
    n = len(slots)
    sources, refs = refs[:n], refs[n:]
    base, refs = (refs[0], refs[1:]) if has_base else (None, refs)
    out, (highs, lows) = refs[0], refs[1:]
    rows = out.shape[0]
    from_row = 0 if part is None else (who[SIDE] ^ part) * rows
    for i, source in enumerate(sources):
        highs[i], lows[i] = split(source[...])

    def tile(k, carry):
        there = pl.ds(pl.multiple_of(k * TILE, TILE), TILE)
        here = pl.ds(pl.multiple_of(from_row + k * TILE, TILE), TILE)
        total = None
        if base is not None:
            total = base[here if base.shape[0] > rows else there, :]
        for i, slot in enumerate(slots):
            at = who[slot]
            term = mm3((mh[at, here, :], ml[at, here, :]), (highs[i], lows[i]))
            total = term if total is None else total + term
        out[there, :] = total
        return carry

    lax.fori_loop(0, rows // TILE, tile, 0)


def forward(name, who, mh, ml, terms, base=None, part=None):
    slots = [slot for slot, _ in terms]
    sources = [source for _, source in terms]
    depth, width = sources[0].shape
    rows = mh.shape[1] // (1 if part is None else 2)
    extra = [] if base is None else [base]
    return call(
        name,
        functools.partial(forward_kernel, slots, part, base is not None),
        who,
        [mh, ml, *sources, *extra],
        [((rows, width), F32)],
        [pltpu.VMEM((len(terms), depth, width), BF16)] * 2,
        6 * len(terms) * rows * depth * width,
    )[0]


def backward_kernel(slots, part, n_add, column, who, mh, ml, source, *refs):
    addends, outs, (high, low) = refs[:n_add], refs[n_add:-2], refs[-2:]
    depth = source.shape[0]
    rows, width = outs[0].shape
    cols = pl.ds(column, width)
    high[...], low[...] = split(source[:, cols])
    deep = pl.ds(pl.multiple_of((who[SIDE] ^ part) * depth, depth), depth)

    def tile(k, carry):
        here = pl.ds(pl.multiple_of(k * TILE, TILE), TILE)
        for slot, out in zip(slots, outs):
            at = who[slot]
            total = mm3((mh[at, here, deep], ml[at, here, deep]), (high[...], low[...]))
            for addend in addends:
                total = total + addend[here, cols]
            out[here, :] = total
        return carry

    lax.fori_loop(0, rows // TILE, tile, 0)


def backward(name, who, mh, ml, slots, source, addends, part, column=0, width=None):
    depth = source.shape[0]
    width = width or source.shape[1]
    rows = mh.shape[1]
    return call(
        name,
        functools.partial(backward_kernel, slots, part, len(addends), column),
        who,
        [mh, ml, source, *addends],
        [((rows, width), F32)] * len(slots),
        [pltpu.VMEM((depth, width), BF16)] * 2,
        6 * len(slots) * rows * depth * width,
    )


def middle_kernel(who, own, far, w_here, w_there, cot_here, cot_there, *outs):
    act_here, act_there, grad_here, grad_there, g_there = outs
    half = own.shape[1]

    def rows_of(w, which):
        return split(w[pl.ds(pl.multiple_of((who[SIDE] ^ which) * half, half), half), :])

    source = split(own[...]), split(far[...])
    total = None
    for w, cot, act, grad in (
        (w_here, cot_here, act_here, grad_here),
        (w_there, cot_there, act_there, grad_there),
    ):
        pre = mm3(source[0], rows_of(w, 0)) + mm3(source[1], rows_of(w, 1))
        s = 1.0 / (1.0 + jnp.exp(-pre))
        act[...] = pre * s
        pg = cot[...] * (s + pre * s * (1.0 - s))
        grad[...] = pg
        term = mm3(split(pg), rows_of(w, 1), ((1,), (1,)))
        total = term if total is None else total + term
    g_there[...] = total


def middle(who, own, far, w_here, w_there, cot_here, cot_there):
    shape = (cot_there.shape, F32)
    flops = 36 * own.shape[0] * own.shape[1] * w_here.shape[1]
    operands = [own, far, w_here, w_there, cot_here, cot_there]
    return call("middle", middle_kernel, who, operands, [shape] * 5, flops=flops)


def keep_kernel(who, w_here, w_there, grad_here, grad_there, g_here):
    half = g_here.shape[1]
    at = pl.ds(pl.multiple_of(who[SIDE] * half, half), half)
    total = None
    for w, grad in ((w_here, grad_here), (w_there, grad_there)):
        term = mm3(split(grad[...]), split(w[at, :]), ((1,), (1,)))
        total = term if total is None else total + term
    g_here[...] = total


def weight_kernel(scale, who, own, far, grad_here, grad_there, keep, give, full):
    half = own.shape[1]
    hidden = grad_here.shape[1]
    grads = split(grad_here[...]), split(grad_there[...])
    for rows, which in ((own, 0), (far, 1)):
        turned = split(rows[...].T)
        at = pl.ds(pl.multiple_of((who[SIDE] ^ which) * half, half), half)
        for i, grad in enumerate(grads):
            full[at, i * hidden : (i + 1) * hidden] = mm3(turned, grad) * scale
    hand_out(full, (keep, give), who[CORE])


def hand_out(full, outs, place):
    rows = outs[0].shape[0]
    for k, out in enumerate(outs):
        out[...] = full[pl.ds(pl.multiple_of((place ^ k) * rows, rows), rows), :]


def half_kernel(which, who, whole, out):
    rows = out.shape[0]
    out[...] = whole[pl.ds(pl.multiple_of((who[SIDE] ^ which) * rows, rows), rows), :]


def join_kernel(place, who, *refs):
    parts, out = refs[:-1], refs[-1]
    rows = parts[0].shape[0]
    for k, part in enumerate(parts):
        out[pl.ds(pl.multiple_of((who[place] ^ k) * rows, rows), rows), :] = part[...]


def join(name, who, place, parts, kind=pltpu.VMEM):
    rows, cols = parts[0].shape
    shape = (rows * len(parts), cols)
    return call(
        name, functools.partial(join_kernel, place), who, parts, [(shape, F32)], place=kind
    )[0]


def add_kernel(count, place, who, *refs):
    parts, outs, full = refs[:count], refs[count:-1], refs[-1]
    total = parts[0][...]
    for part in parts[1:]:
        total = total + part[...]
    full[...] = total
    if place is None:
        cols = outs[0].shape[1]
        for k, out in enumerate(outs):
            out[...] = full[:, k * cols : (k + 1) * cols]
    else:
        hand_out(full, outs, who[place])


def add(name, who, place, parts, pieces):
    rows, cols = parts[0].shape
    shape = (rows, cols // pieces) if place is None else (rows // pieces, cols)
    return call(
        name,
        functools.partial(add_kernel, len(parts), place),
        who,
        parts,
        [(shape, F32)] * pieces,
        [pltpu.VMEM((rows, cols), F32)],
    )


def last_kernel(who, mine, *refs):
    nears, out = refs[:-1], refs[-1]
    width = nears[0].shape[1]
    for k, near in enumerate(nears):
        cols = pl.ds(k * width, width)
        out[:, cols] = mine[:, cols] + near[...]


def moved(value, axis, even, odd):
    peers = lax.axis_size(axis)
    perm = [(i, (i + (odd if i % 2 else even)) % peers) for i in range(peers)]
    return lax.ppermute(value, axis, perm)


def swapped(value, axis, bit=1):
    peers = lax.axis_size(axis)
    return lax.ppermute(value, axis, [(i, i ^ bit) for i in range(peers)])


def after(value, *others):
    return lax.optimization_barrier((value, *others))[0]


def body(features, weight, cotangent, block_rows, block_cols, block_counts, block_values):
    rows, width = features.shape
    hidden = weight.shape[1]
    depth = weight.shape[0]
    parts = lax.axis_size("dom")
    side = lax.axis_index("feat").astype(jnp.int32)
    place = lax.axis_index("dom").astype(jnp.int32)
    odd = place & 1
    zero = place * 0
    who = jnp.stack(
        [side, odd, 1 + 2 * odd, 3 - 2 * odd, zero + 2, zero, (place >> 1) & 1,
         (place >> 2) & 1, (place >> 3) & 1]
    )

    near = moved(features, "dom", 3, 1)
    far = moved(features, "dom", 1, 3)
    w_there = swapped(weight, "feat")
    half_shape = ((rows // 2, hidden), F32)
    cot_here = call("cot_here", functools.partial(half_kernel, 0), who, [cotangent], [half_shape])[0]
    cot_give = call("cot_give", functools.partial(half_kernel, 1), who, [cotangent], [half_shape])[0]
    cot_there = swapped(cot_give, "feat")

    ah, al, th, tl = lay_out(
        block_rows[0], block_cols[0], block_counts, who, block_values[0], rows
    )
    total = forward("agg_own", who, ah, al, [(OWN, features)])
    near = after(near, total, w_there, cot_there)
    two = swapped(near, "dom")
    total = forward("agg_near", who, ah, al, [(NEAR, near)], total)
    far = after(far, total)
    give = forward("agg_far", who, ah, al, [(FAR, far)], total, 1)
    give = forward("agg_two", who, ah, al, [(TWO, two)], give, 1)
    there = swapped(give, "feat")
    keep = forward("agg_keep", who, ah, al, [(FAR, far), (TWO, after(two, give))], total, 0)

    act_here, act_there, grad_here, grad_there, g_give = middle(
        who, keep, there, weight, w_there, cot_here, cot_there
    )
    g_there = swapped(g_give, "feat")
    g_here = call(
        "keep",
        keep_kernel,
        who,
        [weight, w_there, grad_here, grad_there],
        [(keep.shape, F32)],
        flops=12 * rows // 2 * width * hidden,
    )[0]
    scale = 1.0 / math.sqrt(rows * parts)
    w_keep, w_give = call(
        "weight_term",
        functools.partial(weight_kernel, scale),
        who,
        [keep, there, grad_here, grad_there],
        [((depth // 2, 2 * hidden), F32)] * 2,
        [pltpu.VMEM((depth, 2 * hidden), F32)],
        flops=12 * rows // 2 * depth * hidden,
    )
    quick = parts == 16
    steps = weight_sum(who, w_keep, w_give, quick)

    last = next(steps)(g_here)
    firsts = backward("back_here", who, th, tl, [TWO, FAR, NEAR, OWN], after(g_here, last), [], 0)
    last = next(steps)(firsts[0])
    g_there = after(g_there, last)
    last = backward("back_two", who, th, tl, [TWO], g_there, [firsts[0]], 1)[0]
    two = swapped(last, "dom")
    last = next(steps)(last)
    last = backward("back_far", who, th, tl, [FAR], after(g_there, last), [firsts[1]], 1)[0]
    far = moved(last, "dom", -3, -1)
    last = next(steps)(last)
    nears = []
    for k in range(CHUNKS):
        piece = width // CHUNKS
        last = backward(
            "back_near", who, th, tl, [NEAR], after(g_there, last), [firsts[2], two], 1, k * piece, piece
        )[0]
        nears.append(moved(last, "dom", -1, -3))
        if k == 0:
            last = next(steps)(last)
            act_got = swapped(after(act_there, last), "feat")
    mine = backward("back_own", who, th, tl, [OWN], after(g_there, last), [firsts[3], far], 1)[0]
    last = next(steps)(mine)
    activated = join("activated", who, SIDE, [after(act_here, last), act_got], jax.ShapeDtypeStruct)
    last = next(steps)(activated)
    last = next(steps)(after(last, nears[0]))
    weight_grad = next(steps)(last)
    feature_grad = call(
        "feature_grad",
        last_kernel,
        who,
        [after(mine, weight_grad), *nears],
        [(features.shape, F32)],
        place=jax.ShapeDtypeStruct,
    )[0]
    return (activated, feature_grad, weight_grad)


def weight_sum(who, keep, give, quick):
    if not quick:
        ordered = join("core_join", who, CORE, [keep, give])
        here, there = jnp.split(ordered, 2, axis=1)
        total = lax.psum(here + swapped(there, "feat"), "dom")
        for _ in range(8):
            yield lambda last: last
        yield lambda last: total
        return
    got = swapped(give, "dom")
    box = []

    def step(run):
        def go(last):
            box.append(run(last))
            return box[-1][0]

        return go

    for name, place, bit in (("core", CHIP, 2), ("chip", PAIR, 8), ("pair", LAYER, 4)):
        yield step(lambda last: add(name + "_sum", who, place, [after(keep, last), got], 2))
        keep, give = box[-1]
        got = swapped(give, "dom", bit)
    yield step(lambda last: add("layer_sum", who, None, [after(keep, last), got], 2))
    keep, give = box[-1]
    got = swapped(give, "feat")
    yield step(lambda last: add("side_sum", who, None, [after(keep, last), got], 1))
    for name, place, bit in (("layer", LAYER, 4), ("pair", PAIR, 8), ("chip", CHIP, 2)):
        (keep,) = box[-1]
        got = swapped(keep, "dom", bit)
        yield step(lambda last: [join(name + "_join", who, place, [after(keep, last), got])])
    (keep,) = box[-1]
    got = swapped(keep, "dom")
    yield step(
        lambda last: [
            join("weight_grad", who, CORE, [after(keep, last), got], jax.ShapeDtypeStruct)
        ]
    )


def solution(mesh):
    in_specs = (
        P("dom", "feat"),
        P(None, "feat"),
        P("dom", "feat"),
        P("dom", None, None),
        P("dom", None, None),
        P("dom", None),
        P("dom", None, None, None, None),
    )
    out_specs = (P("dom", "feat"), P("dom", "feat"), P(None, "feat"))
    return jax.shard_map(body, mesh=mesh, in_specs=in_specs, out_specs=out_specs, check_vma=False)
```

```python
import functools
import math

import jax
import jax.numpy as jnp
from jax import lax
from jax.experimental import pallas as pl
from jax.experimental.pallas import tpu as pltpu
from jax.sharding import PartitionSpec as P

F32 = jnp.float32
BF16 = jnp.bfloat16
TILE = 256
PIECES = 4
LIMIT = 8 * 1024 * 1024
IN_VMEM = pl.BlockSpec(memory_space=pltpu.VMEM)
IN_SMEM = pl.BlockSpec(memory_space=pltpu.SMEM)

SIDE, CORE, NEAR, FAR, TWO, OWN, CHIP, LAYER, PAIR = range(9)


def split(value):
    high = value.astype(BF16)
    low = (value - high.astype(F32)).astype(BF16)
    return high, low


def mm(a, b, dims=((1,), (0,))):
    return lax.dot_general(a, b, (dims, ((), ())), preferred_element_type=F32)


def mm3(a, b, dims=((1,), (0,))):
    (ah, al), (bh, bl) = a, b
    return mm(ah, bh, dims) + (mm(ah, bl, dims) + mm(al, bh, dims))


def call(name, kernel, who, operands, shapes, scratch=(), flops=0, place=pltpu.VMEM):
    moved = sum(a.size * a.dtype.itemsize for a in operands)
    pinned = [pltpu.with_memory_space_constraint(a, pltpu.VMEM) for a in operands]
    return pl.pallas_call(
        kernel,
        in_specs=[IN_SMEM] + [IN_VMEM] * len(operands),
        out_specs=[IN_VMEM] * len(shapes),
        out_shape=[place(*shape) for shape in shapes],
        scratch_shapes=list(scratch),
        compiler_params=pltpu.CompilerParams(vmem_limit_bytes=LIMIT),
        cost_estimate=pl.CostEstimate(flops=int(flops), bytes_accessed=moved, transcendentals=0),
        name=name,
    )(who, *pinned)


def lay_out_kernel(rows, cols, counts, who, blocks, a, t):
    slot = pl.program_id(0)
    cap = blocks.shape[1]
    size = blocks.shape[2]
    for out in (a, t):
        for part in range(2):
            out[part, slot] = jnp.zeros(out.shape[2:], out.dtype)

    def one(k, carry):
        r = pl.multiple_of(rows[slot, k] * size, size)
        c = pl.multiple_of(cols[slot, k] * size, size)
        block = blocks[0, k]
        for part, value in enumerate(split(block)):
            a[part, slot, pl.ds(r, size), pl.ds(c, size)] = value
        for part, value in enumerate(split(block.T)):
            t[part, slot, pl.ds(c, size), pl.ds(r, size)] = value
        return carry

    lax.fori_loop(0, jnp.minimum(counts[0, slot], cap), one, 0)


def lay_out(rows, cols, counts, who, blocks, size_all):
    window, cap, size, _ = blocks.shape
    shape = pltpu.VMEM((2, window, size_all, size_all), BF16)
    return pl.pallas_call(
        lay_out_kernel,
        grid_spec=pltpu.PrefetchScalarGridSpec(
            num_scalar_prefetch=4,
            grid=(window,),
            in_specs=[pl.BlockSpec((1, cap, size, size), lambda s, *_: (s, 0, 0, 0))],
            out_specs=[IN_VMEM] * 2,
        ),
        out_shape=[shape] * 2,
        compiler_params=pltpu.CompilerParams(vmem_limit_bytes=LIMIT),
        cost_estimate=pl.CostEstimate(flops=0, bytes_accessed=20_000_000, transcendentals=0),
        name="lay_out",
    )(rows, cols, counts, who, pltpu.with_memory_space_constraint(blocks, pltpu.HBM))


def forward_kernel(slots, part, has_base, who, matrix, *refs):
    n = len(slots)
    sources, refs = refs[:n], refs[n:]
    base, refs = (refs[0], refs[1:]) if has_base else (None, refs)
    out, (highs, lows) = refs[0], refs[1:]
    rows = out.shape[0]
    from_row = 0 if part is None else (who[SIDE] ^ part) * rows
    for i, source in enumerate(sources):
        highs[i], lows[i] = split(source[...])

    def tile(k, carry):
        there = pl.ds(pl.multiple_of(k * TILE, TILE), TILE)
        here = pl.ds(pl.multiple_of(from_row + k * TILE, TILE), TILE)
        total = None
        if base is not None:
            total = base[here if base.shape[0] > rows else there, :]
        for i, slot in enumerate(slots):
            at = who[slot]
            term = mm3((matrix[0, at, here, :], matrix[1, at, here, :]), (highs[i], lows[i]))
            total = term if total is None else total + term
        out[there, :] = total
        return carry

    lax.fori_loop(0, rows // TILE, tile, 0)


def forward(name, who, matrix, terms, base=None, part=None):
    slots = [slot for slot, _ in terms]
    sources = [source for _, source in terms]
    depth, width = sources[0].shape
    rows = matrix.shape[2] // (1 if part is None else 2)
    extra = [] if base is None else [base]
    return call(
        name,
        functools.partial(forward_kernel, slots, part, base is not None),
        who,
        [matrix, *sources, *extra],
        [((rows, width), F32)],
        [pltpu.VMEM((len(terms), depth, width), BF16)] * 2,
        6 * len(terms) * rows * depth * width,
    )[0]


def backward_kernel(slots, part, n_add, first, who, matrix, source, *refs):
    addends, outs = refs[:n_add], refs[n_add:]
    depth = source.shape[0]
    parts = split(source[...])
    deep = pl.ds(pl.multiple_of((who[SIDE] ^ part) * depth, depth), depth)
    here = pl.ds(first, outs[0].shape[0])
    for slot, out in zip(slots, outs):
        at = who[slot]
        total = mm3((matrix[0, at, here, deep], matrix[1, at, here, deep]), parts)
        for addend in addends:
            total = total + addend[here, :]
        out[...] = total


def backward(name, who, matrix, slots, source, addends, part, first=0, rows=None):
    depth, width = source.shape
    rows = rows or matrix.shape[2]
    return call(
        name,
        functools.partial(backward_kernel, slots, part, len(addends), first),
        who,
        [matrix, source, *addends],
        [((rows, width), F32)] * len(slots),
        flops=6 * len(slots) * rows * depth * width,
    )


def middle_kernel(who, own, far, w_here, w_there, cot, cot_there, *outs):
    act_here, act_there, grad_here, grad_there, g_there = outs
    half = own.shape[1]

    def rows_of(w, which):
        return split(w[pl.ds(pl.multiple_of((who[SIDE] ^ which) * half, half), half), :])

    rows = own.shape[0]
    cot_here = cot.at[pl.ds(pl.multiple_of(who[SIDE] * rows, rows), rows), :]
    source = split(own[...]), split(far[...])
    total = None
    for w, cot, act, grad in (
        (w_here, cot_here, act_here, grad_here),
        (w_there, cot_there, act_there, grad_there),
    ):
        pre = mm3(source[0], rows_of(w, 0)) + mm3(source[1], rows_of(w, 1))
        s = 1.0 / (1.0 + jnp.exp(-pre))
        act[...] = pre * s
        pg = cot[...] * (s + pre * s * (1.0 - s))
        grad[...] = pg
        term = mm3(split(pg), rows_of(w, 1), ((1,), (1,)))
        total = term if total is None else total + term
    g_there[...] = total


def middle(who, own, far, w_here, w_there, cot, cot_there):
    shape = (cot_there.shape, F32)
    flops = 36 * own.shape[0] * own.shape[1] * w_here.shape[1]
    operands = [own, far, w_here, w_there, cot, cot_there]
    return call("middle", middle_kernel, who, operands, [shape] * 5, flops=flops)


def keep_kernel(who, w_here, w_there, grad_here, grad_there, g_here):
    half = g_here.shape[1]
    at = pl.ds(pl.multiple_of(who[SIDE] * half, half), half)
    total = None
    for w, grad in ((w_here, grad_here), (w_there, grad_there)):
        term = mm3(split(grad[...]), split(w[at, :]), ((1,), (1,)))
        total = term if total is None else total + term
    g_here[...] = total


def weight_kernel(scale, who, own, far, grad_here, grad_there, keep, give, full):
    half = own.shape[1]
    hidden = grad_here.shape[1]
    grads = split(grad_here[...]), split(grad_there[...])
    for rows, which in ((own, 0), (far, 1)):
        turned = split(rows[...].T)
        at = pl.ds(pl.multiple_of((who[SIDE] ^ which) * half, half), half)
        for i, grad in enumerate(grads):
            full[at, i * hidden : (i + 1) * hidden] = mm3(turned, grad) * scale
    hand_out(full, (keep, give), who[CORE])


def hand_out(full, outs, place):
    rows = outs[0].shape[0]
    for k, out in enumerate(outs):
        out[...] = full[pl.ds(pl.multiple_of((place ^ k) * rows, rows), rows), :]


def half_kernel(which, who, whole, out):
    rows = out.shape[0]
    out[...] = whole[pl.ds(pl.multiple_of((who[SIDE] ^ which) * rows, rows), rows), :]


def join_kernel(place, who, *refs):
    parts, out = refs[:-1], refs[-1]
    rows = parts[0].shape[0]
    for k, part in enumerate(parts):
        out[pl.ds(pl.multiple_of((who[place] ^ k) * rows, rows), rows), :] = part[...]


def join(name, who, place, parts, kind=pltpu.VMEM):
    rows, cols = parts[0].shape
    shape = (rows * len(parts), cols)
    return call(
        name, functools.partial(join_kernel, place), who, parts, [(shape, F32)], place=kind
    )[0]


def add_kernel(count, place, who, *refs):
    parts, outs, full = refs[:count], refs[count:-1], refs[-1]
    total = parts[0][...]
    for part in parts[1:]:
        total = total + part[...]
    full[...] = total
    if place is None:
        cols = outs[0].shape[1]
        for k, out in enumerate(outs):
            out[...] = full[:, k * cols : (k + 1) * cols]
    else:
        hand_out(full, outs, who[place])


def add(name, who, place, parts, pieces):
    rows, cols = parts[0].shape
    shape = (rows, cols // pieces) if place is None else (rows // pieces, cols)
    return call(
        name,
        functools.partial(add_kernel, len(parts), place),
        who,
        parts,
        [(shape, F32)] * pieces,
        [pltpu.VMEM((rows, cols), F32)],
    )


def last_kernel(who, mine, *refs):
    nears, out = refs[:-1], refs[-1]
    rows = nears[0].shape[0]
    for k, near in enumerate(nears):
        here = pl.ds(k * rows, rows)
        out[here, :] = mine[here, :] + near[...]


def moved(value, axis, even, odd):
    peers = lax.axis_size(axis)
    perm = [(i, (i + (odd if i % 2 else even)) % peers) for i in range(peers)]
    return lax.ppermute(value, axis, perm)


def swapped(value, axis, bit=1):
    peers = lax.axis_size(axis)
    return lax.ppermute(value, axis, [(i, i ^ bit) for i in range(peers)])


def after(value, *others):
    return lax.optimization_barrier((value, *others))[0]


def body(features, weight, cotangent, block_rows, block_cols, block_counts, block_values):
    rows, width = features.shape
    hidden = weight.shape[1]
    depth = weight.shape[0]
    parts = lax.axis_size("dom")
    side = lax.axis_index("feat").astype(jnp.int32)
    place = lax.axis_index("dom").astype(jnp.int32)
    odd = place & 1
    zero = place * 0
    who = jnp.stack(
        [side, odd, 1 + 2 * odd, 3 - 2 * odd, zero + 2, zero, (place >> 1) & 1,
         (place >> 2) & 1, (place >> 3) & 1]
    )

    near = moved(features, "dom", 3, 1)
    far = moved(features, "dom", 1, 3)
    w_there = swapped(weight, "feat")
    half_shape = ((rows // 2, hidden), F32)
    cot_give = call("cot_give", functools.partial(half_kernel, 1), who, [cotangent], [half_shape])[0]
    cot_there = swapped(cot_give, "feat")

    a, t = lay_out(
        block_rows[0], block_cols[0], block_counts, who, block_values[0], rows
    )
    total = forward("agg_own", who, a, [(OWN, features)])
    near = after(near, total, w_there, cot_there)
    two = swapped(near, "dom")
    total = forward("agg_near", who, a, [(NEAR, near)], total)
    far = after(far, total)
    give = forward("agg_far", who, a, [(FAR, far)], total, 1)
    give = forward("agg_two", who, a, [(TWO, two)], give, 1)
    there = swapped(give, "feat")
    keep = forward("agg_keep", who, a, [(FAR, far), (TWO, after(two, give))], total, 0)

    act_here, act_there, grad_here, grad_there, g_give = middle(
        who, keep, there, weight, w_there, cotangent, cot_there
    )
    g_there = swapped(g_give, "feat")
    g_here = call(
        "keep",
        keep_kernel,
        who,
        [weight, w_there, grad_here, grad_there],
        [(keep.shape, F32)],
        flops=12 * rows // 2 * width * hidden,
    )[0]
    scale = 1.0 / math.sqrt(rows * parts)
    w_keep, w_give = call(
        "weight_term",
        functools.partial(weight_kernel, scale),
        who,
        [keep, there, grad_here, grad_there],
        [((depth // 2, 2 * hidden), F32)] * 2,
        [pltpu.VMEM((depth, 2 * hidden), F32)],
        flops=12 * rows // 2 * depth * hidden,
    )
    quick = parts == 16
    steps = weight_sum(who, w_keep, w_give, quick)

    last = next(steps)(g_here)
    firsts = backward("back_here", who, t, [TWO, FAR, NEAR, OWN], after(g_here, last), [], 0)
    last = next(steps)(firsts[0])
    g_there = after(g_there, last)
    last = backward("back_two", who, t, [TWO], g_there, [firsts[0]], 1)[0]
    two = swapped(last, "dom")
    last = next(steps)(last)
    last = backward("back_far", who, t, [FAR], after(g_there, last), [firsts[1]], 1)[0]
    far = last
    last = next(steps)(last)
    far = moved(after(far, last), "dom", -3, -1)
    nears = []
    piece = rows // PIECES
    for k in range(PIECES):
        ready = after(g_there, last, *nears[: max(0, k - 1)])
        last = backward(
            "back_near", who, t, [NEAR], ready, [firsts[2], two], 1, k * piece, piece
        )[0]
        nears.append(moved(last, "dom", -1, -3))
        if k == 1:
            act_got = swapped(after(act_there, last), "feat")
            last = next(steps)(last)
        if k == 2:
            mine = backward("back_own", who, t, [OWN], after(g_there, last), [firsts[3], far], 1)[0]
            last = next(steps)(mine)
    last = next(steps)(last, nears[-2])
    activated = join("activated", who, SIDE, [after(act_here, last), act_got], jax.ShapeDtypeStruct)
    last = next(steps)(activated, nears[-1])
    weight_grad = next(steps)(last)
    feature_grad = call(
        "feature_grad",
        last_kernel,
        who,
        [after(mine, weight_grad), *nears],
        [(features.shape, F32)],
        place=jax.ShapeDtypeStruct,
    )[0]
    return (activated, feature_grad, weight_grad)


def weight_sum(who, keep, give, quick):
    if not quick:
        ordered = join("core_join", who, CORE, [keep, give])
        here, there = jnp.split(ordered, 2, axis=1)
        total = lax.psum(here + swapped(there, "feat"), "dom")
        for _ in range(8):
            yield lambda *last: last[0]
        yield lambda *last: total
        return
    got = swapped(give, "dom")
    box = []

    def step(run):
        def go(*last):
            box.append(run(*last))
            return box[-1][0]

        return go

    for name, place, bit in (("core", CHIP, 2), ("chip", LAYER, 4), ("layer", PAIR, 8)):
        yield step(lambda *last: add(name + "_sum", who, place, [after(keep, *last), got], 2))
        keep, give = box[-1]
        got = swapped(give, "dom", bit)
    yield step(lambda *last: add("pair_sum", who, None, [after(keep, *last), got], 2))
    keep, give = box[-1]
    got = swapped(give, "feat")
    yield step(lambda *last: add("side_sum", who, None, [after(keep, *last), got], 1))
    for name, place, bit in (("pair", PAIR, 8), ("layer", LAYER, 4), ("chip", CHIP, 2)):
        (keep,) = box[-1]
        got = swapped(keep, "dom", bit)
        yield step(lambda *last: [join(name + "_join", who, place, [after(keep, *last), got])])
    (keep,) = box[-1]
    got = swapped(keep, "dom")
    yield step(
        lambda *last: [
            join("weight_grad", who, CORE, [after(keep, *last), got], jax.ShapeDtypeStruct)
        ]
    )


def solution(mesh):
    in_specs = (
        P("dom", "feat"),
        P(None, "feat"),
        P("dom", "feat"),
        P("dom", None, None),
        P("dom", None, None),
        P("dom", None),
        P("dom", None, None, None, None),
    )
    out_specs = (P("dom", "feat"), P("dom", "feat"), P(None, "feat"))
    return jax.shard_map(body, mesh=mesh, in_specs=in_specs, out_specs=out_specs, check_vma=False)
```

```python
import functools
import math

import jax
import jax.numpy as jnp
from jax import lax
from jax.experimental import pallas as pl
from jax.experimental.pallas import tpu as pltpu
from jax.sharding import PartitionSpec as P

F32 = jnp.float32
BF16 = jnp.bfloat16
TILE = 256
PIECES = 4
LIMIT = 8 * 1024 * 1024
IN_VMEM = pl.BlockSpec(memory_space=pltpu.VMEM)
IN_SMEM = pl.BlockSpec(memory_space=pltpu.SMEM)

SIDE, CORE, NEAR, FAR, TWO, OWN, CHIP, LAYER, PAIR = range(9)


def split(value):
    high = value.astype(BF16)
    low = (value - high.astype(F32)).astype(BF16)
    return high, low


def mm(a, b, dims=((1,), (0,))):
    return lax.dot_general(a, b, (dims, ((), ())), preferred_element_type=F32)


def mm3(a, b, dims=((1,), (0,))):
    (ah, al), (bh, bl) = a, b
    return mm(ah, bh, dims) + (mm(ah, bl, dims) + mm(al, bh, dims))


def call(name, kernel, who, operands, shapes, scratch=(), flops=0, place=pltpu.VMEM):
    moved = sum(a.size * a.dtype.itemsize for a in operands)
    pinned = [pltpu.with_memory_space_constraint(a, pltpu.VMEM) for a in operands]
    return pl.pallas_call(
        kernel,
        in_specs=[IN_SMEM] + [IN_VMEM] * len(operands),
        out_specs=[IN_VMEM] * len(shapes),
        out_shape=[place(*shape) for shape in shapes],
        scratch_shapes=list(scratch),
        compiler_params=pltpu.CompilerParams(vmem_limit_bytes=LIMIT),
        cost_estimate=pl.CostEstimate(flops=int(flops), bytes_accessed=moved, transcendentals=0),
        name=name,
    )(who, *pinned)


def lay_out_kernel(rows, cols, counts, who, blocks, a, t):
    slot = pl.program_id(0)
    cap = blocks.shape[1]
    size = blocks.shape[2]
    for out in (a, t):
        for part in range(2):
            out[part, slot] = jnp.zeros(out.shape[2:], out.dtype)

    def one(k, carry):
        r = pl.multiple_of(rows[slot, k] * size, size)
        c = pl.multiple_of(cols[slot, k] * size, size)
        block = blocks[0, k]
        for part, value in enumerate(split(block)):
            a[part, slot, pl.ds(r, size), pl.ds(c, size)] = value
        for part, value in enumerate(split(block.T)):
            t[part, slot, pl.ds(c, size), pl.ds(r, size)] = value
        return carry

    lax.fori_loop(0, jnp.minimum(counts[0, slot], cap), one, 0)


def lay_out(rows, cols, counts, who, blocks, size_all):
    window, cap, size, _ = blocks.shape
    shape = pltpu.VMEM((2, window, size_all, size_all), BF16)
    return pl.pallas_call(
        lay_out_kernel,
        grid_spec=pltpu.PrefetchScalarGridSpec(
            num_scalar_prefetch=4,
            grid=(window,),
            in_specs=[pl.BlockSpec((1, cap, size, size), lambda s, *_: (s, 0, 0, 0))],
            out_specs=[IN_VMEM] * 2,
        ),
        out_shape=[shape] * 2,
        compiler_params=pltpu.CompilerParams(vmem_limit_bytes=LIMIT),
        cost_estimate=pl.CostEstimate(flops=0, bytes_accessed=20_000_000, transcendentals=0),
        name="lay_out",
    )(rows, cols, counts, who, pltpu.with_memory_space_constraint(blocks, pltpu.HBM))


def forward_kernel(slots, part, has_base, who, matrix, *refs):
    n = len(slots)
    sources, refs = refs[:n], refs[n:]
    base, refs = (refs[0], refs[1:]) if has_base else (None, refs)
    out, (highs, lows) = refs[0], refs[1:]
    rows = out.shape[0]
    from_row = 0 if part is None else (who[SIDE] ^ part) * rows
    for i, source in enumerate(sources):
        highs[i], lows[i] = split(source[...])

    def tile(k, carry):
        there = pl.ds(pl.multiple_of(k * TILE, TILE), TILE)
        here = pl.ds(pl.multiple_of(from_row + k * TILE, TILE), TILE)
        total = None
        if base is not None:
            total = base[here if base.shape[0] > rows else there, :]
        for i, slot in enumerate(slots):
            at = who[slot]
            term = mm3((matrix[0, at, here, :], matrix[1, at, here, :]), (highs[i], lows[i]))
            total = term if total is None else total + term
        out[there, :] = total
        return carry

    lax.fori_loop(0, rows // TILE, tile, 0)


def forward(name, who, matrix, terms, base=None, part=None):
    slots = [slot for slot, _ in terms]
    sources = [source for _, source in terms]
    depth, width = sources[0].shape
    rows = matrix.shape[2] // (1 if part is None else 2)
    extra = [] if base is None else [base]
    return call(
        name,
        functools.partial(forward_kernel, slots, part, base is not None),
        who,
        [matrix, *sources, *extra],
        [((rows, width), F32)],
        [pltpu.VMEM((len(terms), depth, width), BF16)] * 2,
        6 * len(terms) * rows * depth * width,
    )[0]


def backward_kernel(slots, part, n_add, first, pieces, who, matrix, source, *refs):
    addends, outs = refs[:n_add], refs[n_add:]
    depth = source.shape[0]
    parts = split(source[...])
    deep = pl.ds(pl.multiple_of((who[SIDE] ^ part) * depth, depth), depth)
    size = outs[0].shape[0]
    here = pl.ds(first, size * pieces)
    for i, slot in enumerate(slots):
        at = who[slot]
        total = mm3((matrix[0, at, here, deep], matrix[1, at, here, deep]), parts)
        for addend in addends:
            total = total + addend[here, :]
        for k in range(pieces):
            outs[i * pieces + k][...] = total[k * size : (k + 1) * size, :]


def backward(name, who, matrix, slots, source, addends, part, first=0, rows=None, pieces=1):
    depth, width = source.shape
    rows = rows or matrix.shape[2]
    return call(
        name,
        functools.partial(backward_kernel, slots, part, len(addends), first, pieces),
        who,
        [matrix, source, *addends],
        [((rows // pieces, width), F32)] * (len(slots) * pieces),
        flops=6 * len(slots) * rows * depth * width,
    )


def middle_kernel(who, own, far, w_here, w_there, cot, cot_there, *outs):
    act_here, act_there, grad_here, grad_there, g_there = outs
    half = own.shape[1]

    def rows_of(w, which):
        return split(w[pl.ds(pl.multiple_of((who[SIDE] ^ which) * half, half), half), :])

    rows = own.shape[0]
    cot_here = cot.at[pl.ds(pl.multiple_of(who[SIDE] * rows, rows), rows), :]
    source = split(own[...]), split(far[...])
    total = None
    for w, cot, act, grad in (
        (w_here, cot_here, act_here, grad_here),
        (w_there, cot_there, act_there, grad_there),
    ):
        pre = mm3(source[0], rows_of(w, 0)) + mm3(source[1], rows_of(w, 1))
        s = 1.0 / (1.0 + jnp.exp(-pre))
        act[...] = pre * s
        pg = cot[...] * (s + pre * s * (1.0 - s))
        grad[...] = pg
        term = mm3(split(pg), rows_of(w, 1), ((1,), (1,)))
        total = term if total is None else total + term
    g_there[...] = total


def middle(who, own, far, w_here, w_there, cot, cot_there):
    shape = (cot_there.shape, F32)
    flops = 36 * own.shape[0] * own.shape[1] * w_here.shape[1]
    operands = [own, far, w_here, w_there, cot, cot_there]
    return call("middle", middle_kernel, who, operands, [shape] * 5, flops=flops)


def keep_kernel(who, w_here, w_there, grad_here, grad_there, g_here):
    half = g_here.shape[1]
    at = pl.ds(pl.multiple_of(who[SIDE] * half, half), half)
    total = None
    for w, grad in ((w_here, grad_here), (w_there, grad_there)):
        term = mm3(split(grad[...]), split(w[at, :]), ((1,), (1,)))
        total = term if total is None else total + term
    g_here[...] = total


def weight_kernel(scale, who, own, far, grad_here, grad_there, keep, give, full):
    half = own.shape[1]
    hidden = grad_here.shape[1]
    grads = split(grad_here[...]), split(grad_there[...])
    for rows, which in ((own, 0), (far, 1)):
        turned = split(rows[...].T)
        at = pl.ds(pl.multiple_of((who[SIDE] ^ which) * half, half), half)
        for i, grad in enumerate(grads):
            full[at, i * hidden : (i + 1) * hidden] = mm3(turned, grad) * scale
    hand_out(full, (keep, give), who[CORE])


def hand_out(full, outs, place):
    rows = outs[0].shape[0]
    for k, out in enumerate(outs):
        out[...] = full[pl.ds(pl.multiple_of((place ^ k) * rows, rows), rows), :]


def half_kernel(which, who, whole, out):
    rows = out.shape[0]
    out[...] = whole[pl.ds(pl.multiple_of((who[SIDE] ^ which) * rows, rows), rows), :]


def join_kernel(place, who, *refs):
    parts, out = refs[:-1], refs[-1]
    rows = parts[0].shape[0]
    for k, part in enumerate(parts):
        out[pl.ds(pl.multiple_of((who[place] ^ k) * rows, rows), rows), :] = part[...]


def join(name, who, place, parts, kind=pltpu.VMEM):
    rows, cols = parts[0].shape
    shape = (rows * len(parts), cols)
    return call(
        name, functools.partial(join_kernel, place), who, parts, [(shape, F32)], place=kind
    )[0]


def add_kernel(count, place, who, *refs):
    parts, outs, full = refs[:count], refs[count:-1], refs[-1]
    total = parts[0][...]
    for part in parts[1:]:
        total = total + part[...]
    full[...] = total
    if place is None:
        cols = outs[0].shape[1]
        for k, out in enumerate(outs):
            out[...] = full[:, k * cols : (k + 1) * cols]
    else:
        hand_out(full, outs, who[place])


def add(name, who, place, parts, pieces):
    rows, cols = parts[0].shape
    shape = (rows, cols // pieces) if place is None else (rows // pieces, cols)
    return call(
        name,
        functools.partial(add_kernel, len(parts), place),
        who,
        parts,
        [(shape, F32)] * pieces,
        [pltpu.VMEM((rows, cols), F32)],
    )


def last_kernel(who, mine, *refs):
    out = refs[-1]
    count = len(refs) // 2
    for k, (far, near) in enumerate(zip(refs[:count], refs[count:-1])):
        here = pl.ds(k * far.shape[0], far.shape[0])
        out[here, :] = mine[here, :] + far[...] + near[...]


def moved(value, axis, even, odd):
    peers = lax.axis_size(axis)
    perm = [(i, (i + (odd if i % 2 else even)) % peers) for i in range(peers)]
    return lax.ppermute(value, axis, perm)


def swapped(value, axis, bit=1):
    peers = lax.axis_size(axis)
    return lax.ppermute(value, axis, [(i, i ^ bit) for i in range(peers)])


def after(value, *others):
    return lax.optimization_barrier((value, *others))[0]


def body(features, weight, cotangent, block_rows, block_cols, block_counts, block_values):
    rows, width = features.shape
    hidden = weight.shape[1]
    depth = weight.shape[0]
    parts = lax.axis_size("dom")
    side = lax.axis_index("feat").astype(jnp.int32)
    place = lax.axis_index("dom").astype(jnp.int32)
    odd = place & 1
    zero = place * 0
    who = jnp.stack(
        [side, odd, 1 + 2 * odd, 3 - 2 * odd, zero + 2, zero, (place >> 1) & 1,
         (place >> 2) & 1, (place >> 3) & 1]
    )

    near = moved(features, "dom", 3, 1)
    far = moved(features, "dom", 1, 3)
    w_there = swapped(weight, "feat")
    half_shape = ((rows // 2, hidden), F32)
    cot_give = call("cot_give", functools.partial(half_kernel, 1), who, [cotangent], [half_shape])[0]
    cot_there = swapped(cot_give, "feat")

    a, t = lay_out(
        block_rows[0], block_cols[0], block_counts, who, block_values[0], rows
    )
    total = forward("agg_own", who, a, [(OWN, features)])
    near = after(near, total, w_there, cot_there)
    two = swapped(near, "dom")
    total = forward("agg_near", who, a, [(NEAR, near)], total)
    far = after(far, total)
    give = forward("agg_far", who, a, [(FAR, far)], total, 1)
    give = forward("agg_two", who, a, [(TWO, two)], give, 1)
    there = swapped(give, "feat")
    keep = forward("agg_keep", who, a, [(FAR, far), (TWO, after(two, give))], total, 0)

    act_here, act_there, grad_here, grad_there, g_give = middle(
        who, keep, there, weight, w_there, cotangent, cot_there
    )
    g_there = swapped(g_give, "feat")
    g_here = call(
        "keep",
        keep_kernel,
        who,
        [weight, w_there, grad_here, grad_there],
        [(keep.shape, F32)],
        flops=12 * rows // 2 * width * hidden,
    )[0]
    scale = 1.0 / math.sqrt(rows * parts)
    w_keep, w_give = call(
        "weight_term",
        functools.partial(weight_kernel, scale),
        who,
        [keep, there, grad_here, grad_there],
        [((depth // 2, 2 * hidden), F32)] * 2,
        [pltpu.VMEM((depth, 2 * hidden), F32)],
        flops=12 * rows // 2 * depth * hidden,
    )
    quick = parts == 16
    steps = weight_sum(who, w_keep, w_give, quick)

    last = next(steps)(g_here)
    firsts = backward("back_here", who, t, [TWO, FAR, NEAR, OWN], after(g_here, last), [], 0)
    last = next(steps)(firsts[0])
    g_there = after(g_there, last)
    last = backward("back_two", who, t, [TWO], g_there, [firsts[0]], 1)[0]
    two = swapped(last, "dom")
    sends = backward(
        "back_far", who, t, [FAR], after(g_there, last), [firsts[1]], 1, pieces=PIECES
    )
    last = sends[0]
    fars = []
    nears = []
    piece = rows // PIECES
    for k in range(PIECES):
        done = [*fars[:-1], *nears[:-1]]
        fars.append(moved(after(sends[k], last, *done), "dom", -3, -1))
        ready = after(g_there, last, *fars[:-1], *nears[:-1])
        last = backward(
            "back_near", who, t, [NEAR], ready, [firsts[2], two], 1, k * piece, piece
        )[0]
        nears.append(moved(last, "dom", -1, -3))
        if k == 0:
            last = next(steps)(last)
        if k == 1:
            last = next(steps)(last)
            mine = backward("back_own", who, t, [OWN], after(g_there, last), [firsts[3]], 1)[0]
            last = next(steps)(mine)
            act_got = swapped(after(act_there, last), "feat")
        if k == 2:
            last = next(steps)(last)
    last = next(steps)(last, nears[-2], fars[-2])
    activated = join("activated", who, SIDE, [after(act_here, last), act_got], jax.ShapeDtypeStruct)
    last = next(steps)(activated, nears[-1], fars[-1])
    weight_grad = next(steps)(last)
    feature_grad = call(
        "feature_grad",
        last_kernel,
        who,
        [after(mine, weight_grad), *fars, *nears],
        [(features.shape, F32)],
        place=jax.ShapeDtypeStruct,
    )[0]
    return (activated, feature_grad, weight_grad)


def weight_sum(who, keep, give, quick):
    if not quick:
        ordered = join("core_join", who, CORE, [keep, give])
        here, there = jnp.split(ordered, 2, axis=1)
        total = lax.psum(here + swapped(there, "feat"), "dom")
        for _ in range(8):
            yield lambda *last: last[0]
        yield lambda *last: total
        return
    got = swapped(give, "dom")
    box = []

    def step(run):
        def go(*last):
            box.append(run(*last))
            return box[-1][0]

        return go

    for name, place, bit in (("core", CHIP, 2), ("chip", LAYER, 4), ("layer", PAIR, 8)):
        yield step(lambda *last: add(name + "_sum", who, place, [after(keep, *last), got], 2))
        keep, give = box[-1]
        got = swapped(give, "dom", bit)
    yield step(lambda *last: add("pair_sum", who, None, [after(keep, *last), got], 2))
    keep, give = box[-1]
    got = swapped(give, "feat")
    yield step(lambda *last: add("side_sum", who, None, [after(keep, *last), got], 1))
    for name, place, bit in (("pair", PAIR, 8), ("layer", LAYER, 4), ("chip", CHIP, 2)):
        (keep,) = box[-1]
        got = swapped(keep, "dom", bit)
        yield step(lambda *last: [join(name + "_join", who, place, [after(keep, *last), got])])
    (keep,) = box[-1]
    got = swapped(keep, "dom")
    yield step(
        lambda *last: [
            join("weight_grad", who, CORE, [after(keep, *last), got], jax.ShapeDtypeStruct)
        ]
    )


def solution(mesh):
    in_specs = (
        P("dom", "feat"),
        P(None, "feat"),
        P("dom", "feat"),
        P("dom", None, None),
        P("dom", None, None),
        P("dom", None),
        P("dom", None, None, None, None),
    )
    out_specs = (P("dom", "feat"), P("dom", "feat"), P(None, "feat"))
    return jax.shard_map(body, mesh=mesh, in_specs=in_specs, out_specs=out_specs, check_vma=False)
```

```python
import functools
import math

import jax
import jax.numpy as jnp
from jax import lax
from jax.experimental import pallas as pl
from jax.experimental.pallas import tpu as pltpu
from jax.sharding import PartitionSpec as P

F32 = jnp.float32
BF16 = jnp.bfloat16
TILE = 256
LIMIT = 8 * 1024 * 1024
IN_VMEM = pl.BlockSpec(memory_space=pltpu.VMEM)
IN_SMEM = pl.BlockSpec(memory_space=pltpu.SMEM)

SIDE, CORE, NEAR, FAR, TWO, OWN, CHIP = range(7)


def split(value):
    high = value.astype(BF16)
    low = (value - high.astype(F32)).astype(BF16)
    return high, low


def mm(a, b, dims=((1,), (0,))):
    return lax.dot_general(a, b, (dims, ((), ())), preferred_element_type=F32)


def mm3(a, b, dims=((1,), (0,))):
    (ah, al), (bh, bl) = a, b
    return mm(ah, bh, dims) + (mm(ah, bl, dims) + mm(al, bh, dims))


def call(name, kernel, who, operands, shapes, scratch=(), flops=0, place=pltpu.VMEM):
    moved = sum(a.size * a.dtype.itemsize for a in operands)
    pinned = [pltpu.with_memory_space_constraint(a, pltpu.VMEM) for a in operands]
    return pl.pallas_call(
        kernel,
        in_specs=[IN_SMEM] + [IN_VMEM] * len(operands),
        out_specs=[IN_VMEM] * len(shapes),
        out_shape=[place(*shape) for shape in shapes],
        scratch_shapes=list(scratch),
        compiler_params=pltpu.CompilerParams(vmem_limit_bytes=LIMIT),
        cost_estimate=pl.CostEstimate(flops=int(flops), bytes_accessed=moved, transcendentals=0),
        name=name,
    )(who, *pinned)


def lay_out_kernel(rows, cols, counts, who, blocks, a, t):
    slot = pl.program_id(0)
    cap = blocks.shape[1]
    size = blocks.shape[2]
    for out in (a, t):
        for part in range(2):
            out[part, slot] = jnp.zeros(out.shape[2:], out.dtype)

    def one(k, carry):
        r = pl.multiple_of(rows[slot, k] * size, size)
        c = pl.multiple_of(cols[slot, k] * size, size)
        block = blocks[0, k]
        for part, value in enumerate(split(block)):
            a[part, slot, pl.ds(r, size), pl.ds(c, size)] = value
        for part, value in enumerate(split(block.T)):
            t[part, slot, pl.ds(c, size), pl.ds(r, size)] = value
        return carry

    lax.fori_loop(0, jnp.minimum(counts[0, slot], cap), one, 0)


def lay_out(rows, cols, counts, who, blocks, size_all):
    window, cap, size, _ = blocks.shape
    shape = pltpu.VMEM((2, window, size_all, size_all), BF16)
    return pl.pallas_call(
        lay_out_kernel,
        grid_spec=pltpu.PrefetchScalarGridSpec(
            num_scalar_prefetch=4,
            grid=(window,),
            in_specs=[pl.BlockSpec((1, cap, size, size), lambda s, *_: (s, 0, 0, 0))],
            out_specs=[IN_VMEM] * 2,
        ),
        out_shape=[shape] * 2,
        compiler_params=pltpu.CompilerParams(vmem_limit_bytes=LIMIT),
        cost_estimate=pl.CostEstimate(flops=0, bytes_accessed=20_000_000, transcendentals=0),
        name="lay_out",
    )(rows, cols, counts, who, pltpu.with_memory_space_constraint(blocks, pltpu.HBM))


def forward_kernel(slots, part, has_base, who, matrix, *refs):
    n = len(slots)
    sources, refs = refs[:n], refs[n:]
    base, refs = (refs[0], refs[1:]) if has_base else (None, refs)
    out, (highs, lows) = refs[0], refs[1:]
    rows = out.shape[0]
    from_row = 0 if part is None else (who[SIDE] ^ part) * rows
    for i, source in enumerate(sources):
        highs[i], lows[i] = split(source[...])

    def tile(k, carry):
        there = pl.ds(pl.multiple_of(k * TILE, TILE), TILE)
        here = pl.ds(pl.multiple_of(from_row + k * TILE, TILE), TILE)
        total = None
        if base is not None:
            total = base[here if base.shape[0] > rows else there, :]
        for i, slot in enumerate(slots):
            at = who[slot]
            term = mm3((matrix[0, at, here, :], matrix[1, at, here, :]), (highs[i], lows[i]))
            total = term if total is None else total + term
        out[there, :] = total
        return carry

    lax.fori_loop(0, rows // TILE, tile, 0)


def forward(name, who, matrix, terms, base=None, part=None):
    slots = [slot for slot, _ in terms]
    sources = [source for _, source in terms]
    depth, width = sources[0].shape
    rows = matrix.shape[2] // (1 if part is None else 2)
    extra = [] if base is None else [base]
    return call(
        name,
        functools.partial(forward_kernel, slots, part, base is not None),
        who,
        [matrix, *sources, *extra],
        [((rows, width), F32)],
        [pltpu.VMEM((len(terms), depth, width), BF16)] * 2,
        6 * len(terms) * rows * depth * width,
    )[0]


def backward_kernel(slots, part, n_add, first, pieces, who, matrix, source, *refs):
    addends, outs = refs[:n_add], refs[n_add:]
    depth = source.shape[0]
    parts = split(source[...])
    deep = pl.ds(pl.multiple_of((who[SIDE] ^ part) * depth, depth), depth)
    size = outs[0].shape[0]
    here = pl.ds(first, size * pieces)
    for i, slot in enumerate(slots):
        at = who[slot]
        total = mm3((matrix[0, at, here, deep], matrix[1, at, here, deep]), parts)
        for addend in addends:
            total = total + addend[here, :]
        for k in range(pieces):
            outs[i * pieces + k][...] = total[k * size : (k + 1) * size, :]


def backward(name, who, matrix, slots, source, addends, part, first=0, rows=None, pieces=1):
    depth, width = source.shape
    rows = rows or matrix.shape[2]
    return call(
        name,
        functools.partial(backward_kernel, slots, part, len(addends), first, pieces),
        who,
        [matrix, source, *addends],
        [((rows // pieces, width), F32)] * (len(slots) * pieces),
        flops=6 * len(slots) * rows * depth * width,
    )


def middle_kernel(who, own, far, w_here, w_there, cot, cot_there, *outs):
    act_here, act_there, grad_here, grad_there, g_there = outs
    half = own.shape[1]

    def rows_of(w, which):
        return split(w[pl.ds(pl.multiple_of((who[SIDE] ^ which) * half, half), half), :])

    rows = own.shape[0]
    cot_here = cot.at[pl.ds(pl.multiple_of(who[SIDE] * rows, rows), rows), :]
    source = split(own[...]), split(far[...])
    total = None
    for w, cot, act, grad in (
        (w_here, cot_here, act_here, grad_here),
        (w_there, cot_there, act_there, grad_there),
    ):
        pre = mm3(source[0], rows_of(w, 0)) + mm3(source[1], rows_of(w, 1))
        s = 1.0 / (1.0 + jnp.exp(-pre))
        act[...] = pre * s
        pg = cot[...] * (s + pre * s * (1.0 - s))
        grad[...] = pg
        term = mm3(split(pg), rows_of(w, 1), ((1,), (1,)))
        total = term if total is None else total + term
    g_there[...] = total


def middle(who, own, far, w_here, w_there, cot, cot_there):
    shape = (cot_there.shape, F32)
    flops = 36 * own.shape[0] * own.shape[1] * w_here.shape[1]
    operands = [own, far, w_here, w_there, cot, cot_there]
    return call("middle", middle_kernel, who, operands, [shape] * 5, flops=flops)


def keep_kernel(who, w_here, w_there, grad_here, grad_there, g_here):
    half = g_here.shape[1]
    at = pl.ds(pl.multiple_of(who[SIDE] * half, half), half)
    total = None
    for w, grad in ((w_here, grad_here), (w_there, grad_there)):
        term = mm3(split(grad[...]), split(w[at, :]), ((1,), (1,)))
        total = term if total is None else total + term
    g_here[...] = total


def weight_kernel(scale, who, own, far, grad_here, grad_there, keep, give, full):
    half = own.shape[1]
    hidden = grad_here.shape[1]
    grads = split(grad_here[...]), split(grad_there[...])
    for rows, which in ((own, 0), (far, 1)):
        turned = split(rows[...].T)
        at = pl.ds(pl.multiple_of((who[SIDE] ^ which) * half, half), half)
        for i, grad in enumerate(grads):
            full[at, i * hidden : (i + 1) * hidden] = mm3(turned, grad) * scale
    hand_out(full, (keep, give), who[CORE])


def hand_out(full, outs, place):
    rows = outs[0].shape[0]
    for k, out in enumerate(outs):
        out[...] = full[pl.ds(pl.multiple_of((place ^ k) * rows, rows), rows), :]


def half_kernel(which, who, whole, out):
    rows = out.shape[0]
    out[...] = whole[pl.ds(pl.multiple_of((who[SIDE] ^ which) * rows, rows), rows), :]


def join_kernel(place, who, *refs):
    parts, out = refs[:-1], refs[-1]
    rows = parts[0].shape[0]
    for k, part in enumerate(parts):
        out[pl.ds(pl.multiple_of((who[place] ^ k) * rows, rows), rows), :] = part[...]


def join(name, who, place, parts, kind=pltpu.VMEM):
    rows, cols = parts[0].shape
    shape = (rows * len(parts), cols)
    return call(
        name, functools.partial(join_kernel, place), who, parts, [(shape, F32)], place=kind
    )[0]


def pick_kernel(who, one, other, out):
    out[...] = jnp.where(who[CHIP] == 1, one[...], other[...])


def pick(name, who, one, other):
    return call(name, pick_kernel, who, [one, other], [(one.shape, F32)])[0]


def give_columns_kernel(who, one, other, keep, give):
    cols = keep.shape[1]
    keep[...] = one[:, :cols] + other[:, :cols]
    give[...] = one[:, cols:] + other[:, cols:]


def give_columns(name, who, one, other):
    rows, cols = one.shape
    shape = ((rows, cols // 2), F32)
    return call(name, give_columns_kernel, who, [one, other], [shape] * 2)


def add_kernel(who, *refs):
    total = refs[0][...]
    for ref in refs[1:-1]:
        total = total + ref[...]
    refs[-1][...] = total


def add(name, who, *parts):
    return call(name, add_kernel, who, parts, [(parts[0].shape, F32)])[0]


def moved(value, axis, even, odd):
    peers = lax.axis_size(axis)
    perm = [(i, (i + (odd if i % 2 else even)) % peers) for i in range(peers)]
    return lax.ppermute(value, axis, perm)


def chosen(value, axis, target):
    peers = lax.axis_size(axis)
    pairs = [(i, target(i)) for i in range(peers)]
    return lax.ppermute(value, axis, [pair for pair in pairs if pair[1] is not None])


def swapped(value, axis):
    return chosen(value, axis, lambda i: i ^ 1)


def after(value, *others):
    return lax.optimization_barrier((value, *others))[0]


def body(features, weight, cotangent, block_rows, block_cols, block_counts, block_values):
    rows, width = features.shape
    hidden = weight.shape[1]
    depth = weight.shape[0]
    parts = lax.axis_size("dom")
    side = lax.axis_index("feat").astype(jnp.int32)
    place = lax.axis_index("dom").astype(jnp.int32)
    odd = place & 1
    zero = place * 0
    who = jnp.stack([side, odd, 1 + 2 * odd, 3 - 2 * odd, zero + 2, zero, (place >> 1) & 1])

    near = moved(features, "dom", 3, 1)
    far = moved(features, "dom", 1, 3)
    w_there = swapped(weight, "feat")
    half_shape = ((rows // 2, hidden), F32)
    cot_give = call("cot_give", functools.partial(half_kernel, 1), who, [cotangent], [half_shape])[0]
    cot_there = swapped(cot_give, "feat")

    a, t = lay_out(
        block_rows[0], block_cols[0], block_counts, who, block_values[0], rows
    )
    total = forward("agg_own", who, a, [(OWN, features)])
    near = after(near, total, w_there, cot_there)
    two = swapped(near, "dom")
    total = forward("agg_near", who, a, [(NEAR, near)], total)
    far = after(far, total)
    give = forward("agg_far", who, a, [(FAR, far)], total, 1)
    give = forward("agg_two", who, a, [(TWO, two)], give, 1)
    there = swapped(give, "feat")
    keep = forward("agg_keep", who, a, [(FAR, far), (TWO, after(two, give))], total, 0)

    act_here, act_there, grad_here, grad_there, g_give = middle(
        who, keep, there, weight, w_there, cotangent, cot_there
    )
    g_there = swapped(g_give, "feat")
    scale = 1.0 / math.sqrt(rows * parts)
    w_keep, w_give = call(
        "weight_term",
        functools.partial(weight_kernel, scale),
        who,
        [keep, there, grad_here, grad_there],
        [((depth // 2, 2 * hidden), F32)] * 2,
        [pltpu.VMEM((depth, 2 * hidden), F32)],
        flops=12 * rows // 2 * depth * hidden,
    )
    quick = parts == 16
    steps = weight_sum(who, w_keep, w_give, quick)

    last = next(steps)(grad_here)
    g_here = call(
        "keep",
        keep_kernel,
        who,
        [weight, w_there, after(grad_here, last), grad_there],
        [(keep.shape, F32)],
        flops=12 * rows // 2 * width * hidden,
    )[0]
    firsts = backward("back_here", who, t, [TWO, FAR, NEAR, OWN], after(g_here, last), [], 0)
    last = next(steps)(firsts[0], g_there)
    g_there = after(g_there, last)
    last = backward("back_two", who, t, [TWO], g_there, [firsts[0]], 1)[0]
    two = swapped(last, "dom")
    last = backward("back_far", who, t, [FAR], after(g_there, last), [firsts[1]], 1)[0]
    far = moved(last, "dom", -3, -1)
    last = backward("back_near", who, t, [NEAR], after(g_there, last), [firsts[2], two], 1)[0]
    near = moved(last, "dom", -1, -3)
    last = next(steps)(last)
    act_got = swapped(after(act_there, last), "feat")
    mine = backward("back_own", who, t, [OWN], after(g_there, last), [firsts[3]], 1)[0]
    last = next(steps)(mine, far)
    last = next(steps)(last)
    activated = join("activated", who, SIDE, [after(act_here, last), act_got], jax.ShapeDtypeStruct)
    last = next(steps)(activated)
    weight_grad = next(steps)(last, near)
    feature_grad = call(
        "feature_grad",
        add_kernel,
        who,
        [after(mine, weight_grad), far, near],
        [(features.shape, F32)],
        place=jax.ShapeDtypeStruct,
    )[0]
    return (activated, feature_grad, weight_grad)


def weight_sum(who, keep, give, quick):
    if not quick:
        ordered = join("core_join", who, CORE, [keep, give])
        here, there = jnp.split(ordered, 2, axis=1)
        total = lax.psum(here + swapped(there, "feat"), "dom")
        for _ in range(6):
            yield lambda *last: last[0]
        yield lambda *last: total
        return
    got = swapped(give, "dom")
    box = []

    def step(run):
        def go(*last):
            box.append(run(*last))
            return box[-1][0]

        return go

    yield step(lambda *last: [add("core_sum", who, after(keep, *last), got)])
    (keep,) = box[-1]
    got = chosen(keep, "dom", lambda i: i + 2 if i % 4 < 2 else None)
    yield step(lambda *last: give_columns("chip_sum", who, after(keep, *last), got))
    keep, give = box[-1]
    got = swapped(give, "feat")
    for name, bit in (("side_sum", 4), ("layer_sum", 8), ("pair_sum", None)):
        yield step(lambda *last: [add(name, who, after(keep, *last), got)])
        (keep,) = box[-1]
        if bit is not None:
            got = chosen(keep, "dom", lambda i: i ^ bit if i % 4 >= 2 else None)
    got = chosen(keep, "dom", lambda i: i - 2 if i % 4 >= 2 else None)
    yield step(lambda *last: [pick("chip_pick", who, after(keep, *last), got)])
    (keep,) = box[-1]
    got = swapped(keep, "dom")
    yield step(
        lambda *last: [
            join("weight_grad", who, CORE, [after(keep, *last), got], jax.ShapeDtypeStruct)
        ]
    )


def solution(mesh):
    in_specs = (
        P("dom", "feat"),
        P(None, "feat"),
        P("dom", "feat"),
        P("dom", None, None),
        P("dom", None, None),
        P("dom", None),
        P("dom", None, None, None, None),
    )
    out_specs = (P("dom", "feat"), P("dom", "feat"), P(None, "feat"))
    return jax.shard_map(body, mesh=mesh, in_specs=in_specs, out_specs=out_specs, check_vma=False)
```

```python
import functools
import math

import jax
import jax.numpy as jnp
from jax import lax
from jax.experimental import pallas as pl
from jax.experimental.pallas import tpu as pltpu
from jax.sharding import PartitionSpec as P

F32 = jnp.float32
BF16 = jnp.bfloat16
TILE = 256
LIMIT = 8 * 1024 * 1024
IN_VMEM = pl.BlockSpec(memory_space=pltpu.VMEM)
IN_SMEM = pl.BlockSpec(memory_space=pltpu.SMEM)

SIDE, CORE, NEAR, FAR, TWO, OWN, CHIP = range(7)


def split(value):
    high = value.astype(BF16)
    low = (value - high.astype(F32)).astype(BF16)
    return high, low


def mm(a, b, dims=((1,), (0,))):
    return lax.dot_general(a, b, (dims, ((), ())), preferred_element_type=F32)


def mm3(a, b, dims=((1,), (0,))):
    (ah, al), (bh, bl) = a, b
    return mm(ah, bh, dims) + (mm(ah, bl, dims) + mm(al, bh, dims))


def call(name, kernel, who, operands, shapes, scratch=(), flops=0, place=pltpu.VMEM):
    moved = sum(a.size * a.dtype.itemsize for a in operands)
    pinned = [pltpu.with_memory_space_constraint(a, pltpu.VMEM) for a in operands]
    return pl.pallas_call(
        kernel,
        in_specs=[IN_SMEM] + [IN_VMEM] * len(operands),
        out_specs=[IN_VMEM] * len(shapes),
        out_shape=[place(*shape) for shape in shapes],
        scratch_shapes=list(scratch),
        compiler_params=pltpu.CompilerParams(vmem_limit_bytes=LIMIT),
        cost_estimate=pl.CostEstimate(flops=int(flops), bytes_accessed=moved, transcendentals=0),
        name=name,
    )(who, *pinned)


def lay_out_kernel(rows, cols, counts, who, blocks, a, t):
    slot = pl.program_id(0)
    cap = blocks.shape[1]
    size = blocks.shape[2]
    for out in (a, t):
        for part in range(2):
            out[part, slot] = jnp.zeros(out.shape[2:], out.dtype)

    def one(k, carry):
        r = pl.multiple_of(rows[slot, k] * size, size)
        c = pl.multiple_of(cols[slot, k] * size, size)
        block = blocks[0, k]
        for part, value in enumerate(split(block)):
            a[part, slot, pl.ds(r, size), pl.ds(c, size)] = value
        for part, value in enumerate(split(block.T)):
            t[part, slot, pl.ds(c, size), pl.ds(r, size)] = value
        return carry

    lax.fori_loop(0, jnp.minimum(counts[0, slot], cap), one, 0)


def lay_out(rows, cols, counts, who, blocks, size_all):
    window, cap, size, _ = blocks.shape
    shape = pltpu.VMEM((2, window, size_all, size_all), BF16)
    return pl.pallas_call(
        lay_out_kernel,
        grid_spec=pltpu.PrefetchScalarGridSpec(
            num_scalar_prefetch=4,
            grid=(window,),
            in_specs=[pl.BlockSpec((1, cap, size, size), lambda s, *_: (s, 0, 0, 0))],
            out_specs=[IN_VMEM] * 2,
        ),
        out_shape=[shape] * 2,
        compiler_params=pltpu.CompilerParams(vmem_limit_bytes=LIMIT),
        cost_estimate=pl.CostEstimate(flops=0, bytes_accessed=20_000_000, transcendentals=0),
        name="lay_out",
    )(rows, cols, counts, who, pltpu.with_memory_space_constraint(blocks, pltpu.HBM))


def forward_kernel(slots, part, has_base, who, matrix, *refs):
    n = len(slots)
    sources, refs = refs[:n], refs[n:]
    base, refs = (refs[0], refs[1:]) if has_base else (None, refs)
    out, (highs, lows) = refs[0], refs[1:]
    rows = out.shape[0]
    from_row = 0 if part is None else (who[SIDE] ^ part) * rows
    for i, source in enumerate(sources):
        highs[i], lows[i] = split(source[...])

    def tile(k, carry):
        there = pl.ds(pl.multiple_of(k * TILE, TILE), TILE)
        here = pl.ds(pl.multiple_of(from_row + k * TILE, TILE), TILE)
        total = None
        if base is not None:
            total = base[here if base.shape[0] > rows else there, :]
        for i, slot in enumerate(slots):
            at = who[slot]
            term = mm3((matrix[0, at, here, :], matrix[1, at, here, :]), (highs[i], lows[i]))
            total = term if total is None else total + term
        out[there, :] = total
        return carry

    lax.fori_loop(0, rows // TILE, tile, 0)


def forward(name, who, matrix, terms, base=None, part=None):
    slots = [slot for slot, _ in terms]
    sources = [source for _, source in terms]
    depth, width = sources[0].shape
    rows = matrix.shape[2] // (1 if part is None else 2)
    extra = [] if base is None else [base]
    return call(
        name,
        functools.partial(forward_kernel, slots, part, base is not None),
        who,
        [matrix, *sources, *extra],
        [((rows, width), F32)],
        [pltpu.VMEM((len(terms), depth, width), BF16)] * 2,
        6 * len(terms) * rows * depth * width,
    )[0]


def backward_kernel(slots, part, n_add, first, pieces, who, matrix, source, *refs):
    addends, outs = refs[:n_add], refs[n_add:]
    depth = source.shape[0]
    parts = split(source[...])
    deep = pl.ds(pl.multiple_of((who[SIDE] ^ part) * depth, depth), depth)
    size = outs[0].shape[0]
    here = pl.ds(first, size * pieces)
    for i, slot in enumerate(slots):
        at = who[slot]
        total = mm3((matrix[0, at, here, deep], matrix[1, at, here, deep]), parts)
        for addend in addends:
            total = total + addend[here, :]
        for k in range(pieces):
            outs[i * pieces + k][...] = total[k * size : (k + 1) * size, :]


def backward(name, who, matrix, slots, source, addends, part, first=0, rows=None, pieces=1):
    depth, width = source.shape
    rows = rows or matrix.shape[2]
    return call(
        name,
        functools.partial(backward_kernel, slots, part, len(addends), first, pieces),
        who,
        [matrix, source, *addends],
        [((rows // pieces, width), F32)] * (len(slots) * pieces),
        flops=6 * len(slots) * rows * depth * width,
    )


def middle_kernel(who, own, far, w_here, w_there, cot, cot_there, *outs):
    act_here, act_there, grad_here, grad_there, g_there = outs
    half = own.shape[1]

    def rows_of(w, which):
        return split(w[pl.ds(pl.multiple_of((who[SIDE] ^ which) * half, half), half), :])

    rows = own.shape[0]
    cot_here = cot.at[pl.ds(pl.multiple_of(who[SIDE] * rows, rows), rows), :]
    source = split(own[...]), split(far[...])
    total = None
    for w, cot, act, grad in (
        (w_here, cot_here, act_here, grad_here),
        (w_there, cot_there, act_there, grad_there),
    ):
        pre = mm3(source[0], rows_of(w, 0)) + mm3(source[1], rows_of(w, 1))
        s = 1.0 / (1.0 + jnp.exp(-pre))
        act[...] = pre * s
        pg = cot[...] * (s + pre * s * (1.0 - s))
        grad[...] = pg
        term = mm3(split(pg), rows_of(w, 1), ((1,), (1,)))
        total = term if total is None else total + term
    g_there[...] = total


def middle(who, own, far, w_here, w_there, cot, cot_there):
    shape = (cot_there.shape, F32)
    flops = 36 * own.shape[0] * own.shape[1] * w_here.shape[1]
    operands = [own, far, w_here, w_there, cot, cot_there]
    return call("middle", middle_kernel, who, operands, [shape] * 5, flops=flops)


def keep_kernel(who, w_here, w_there, grad_here, grad_there, g_here):
    half = g_here.shape[1]
    at = pl.ds(pl.multiple_of(who[SIDE] * half, half), half)
    total = None
    for w, grad in ((w_here, grad_here), (w_there, grad_there)):
        term = mm3(split(grad[...]), split(w[at, :]), ((1,), (1,)))
        total = term if total is None else total + term
    g_here[...] = total


def weight_kernel(scale, which, who, own, far, grad_here, grad_there, here, there):
    mine = who[SIDE] == (who[CORE] ^ which)
    turned = split(jnp.where(mine, own[...], far[...]).T)
    for grad, out in ((grad_here, here), (grad_there, there)):
        out[...] = mm3(turned, split(grad[...])) * scale


def weight_term(name, who, scale, which, own, far, grad_here, grad_there):
    rows, half = own.shape
    hidden = grad_here.shape[1]
    return call(
        name,
        functools.partial(weight_kernel, scale, which),
        who,
        [own, far, grad_here, grad_there],
        [((half, hidden), F32)] * 2,
        flops=12 * rows * half * hidden,
    )


def half_kernel(which, who, whole, out):
    rows = out.shape[0]
    out[...] = whole[pl.ds(pl.multiple_of((who[SIDE] ^ which) * rows, rows), rows), :]


def join_kernel(place, who, *refs):
    parts, out = refs[:-1], refs[-1]
    rows = parts[0].shape[0]
    for k, part in enumerate(parts):
        out[pl.ds(pl.multiple_of((who[place] ^ k) * rows, rows), rows), :] = part[...]


def join(name, who, place, parts, kind=pltpu.VMEM):
    rows, cols = parts[0].shape
    shape = (rows * len(parts), cols)
    return call(
        name, functools.partial(join_kernel, place), who, parts, [(shape, F32)], place=kind
    )[0]


def pick_kernel(who, one, other, out):
    out[...] = jnp.where(who[CHIP] == 1, one[...], other[...])


def pick(name, who, one, other):
    return call(name, pick_kernel, who, [one, other], [(one.shape, F32)])[0]


def add_kernel(who, *refs):
    total = refs[0][...]
    for ref in refs[1:-1]:
        total = total + ref[...]
    refs[-1][...] = total


def add(name, who, *parts):
    return call(name, add_kernel, who, parts, [(parts[0].shape, F32)])[0]


def moved(value, axis, even, odd):
    peers = lax.axis_size(axis)
    perm = [(i, (i + (odd if i % 2 else even)) % peers) for i in range(peers)]
    return lax.ppermute(value, axis, perm)


def chosen(value, axis, target):
    peers = lax.axis_size(axis)
    pairs = [(i, target(i)) for i in range(peers)]
    return lax.ppermute(value, axis, [pair for pair in pairs if pair[1] is not None])


def swapped(value, axis):
    return chosen(value, axis, lambda i: i ^ 1)


def after(value, *others):
    return lax.optimization_barrier((value, *others))[0]


def body(features, weight, cotangent, block_rows, block_cols, block_counts, block_values):
    rows, width = features.shape
    hidden = weight.shape[1]
    depth = weight.shape[0]
    parts = lax.axis_size("dom")
    side = lax.axis_index("feat").astype(jnp.int32)
    place = lax.axis_index("dom").astype(jnp.int32)
    odd = place & 1
    zero = place * 0
    who = jnp.stack([side, odd, 1 + 2 * odd, 3 - 2 * odd, zero + 2, zero, (place >> 1) & 1])

    near = moved(features, "dom", 3, 1)
    far = moved(features, "dom", 1, 3)
    w_there = swapped(weight, "feat")
    half_shape = ((rows // 2, hidden), F32)
    cot_give = call("cot_give", functools.partial(half_kernel, 1), who, [cotangent], [half_shape])[0]
    cot_there = swapped(cot_give, "feat")

    a, t = lay_out(
        block_rows[0], block_cols[0], block_counts, who, block_values[0], rows
    )
    total = forward("agg_own", who, a, [(OWN, features)])
    near = after(near, total, w_there, cot_there)
    two = swapped(near, "dom")
    total = forward("agg_near", who, a, [(NEAR, near)], total)
    far = after(far, total)
    give = forward("agg_give", who, a, [(FAR, far), (TWO, two)], total, 1)
    there = swapped(give, "feat")
    keep = forward("agg_keep", who, a, [(FAR, far), (TWO, after(two, give))], total, 0)

    act_here, act_there, grad_here, grad_there, g_give = middle(
        who, keep, there, weight, w_there, cotangent, cot_there
    )
    g_there = swapped(g_give, "feat")
    scale = 1.0 / math.sqrt(rows * parts)
    w_give = weight_term("weight_give", who, scale, 1, keep, there, grad_here, grad_there)
    w_keep = weight_term(
        "weight_keep", who, scale, 0, after(keep, w_give[0]), there, grad_here, grad_there
    )
    quick = parts == 16
    steps = weight_sum(who, w_keep, w_give, quick)

    last = next(steps)(grad_here)
    last = next(steps)(last)
    g_here = call(
        "keep",
        keep_kernel,
        who,
        [weight, w_there, after(grad_here, last), grad_there],
        [(keep.shape, F32)],
        flops=12 * rows // 2 * width * hidden,
    )[0]
    firsts = backward("back_here", who, t, [TWO, FAR, NEAR, OWN], after(g_here, last), [], 0)
    last = next(steps)(firsts[0])
    g_there = after(g_there, last)
    last = backward("back_two", who, t, [TWO], g_there, [firsts[0]], 1)[0]
    two = swapped(last, "dom")
    last = backward("back_far", who, t, [FAR], after(g_there, last), [firsts[1]], 1)[0]
    far = moved(last, "dom", -3, -1)
    last = backward("back_near", who, t, [NEAR], after(g_there, last), [firsts[2], two], 1)[0]
    near = moved(last, "dom", -1, -3)
    last = next(steps)(last)
    act_got = swapped(after(act_there, last), "feat")
    mine = backward("back_own", who, t, [OWN], after(g_there, last), [firsts[3]], 1)[0]
    last = next(steps)(mine, far)
    last = next(steps)(last)
    activated = join("activated", who, SIDE, [after(act_here, last), act_got], jax.ShapeDtypeStruct)
    last = next(steps)(activated, near)
    weight_grad = next(steps)(last)
    feature_grad = call(
        "feature_grad",
        add_kernel,
        who,
        [after(mine, weight_grad), far, near],
        [(features.shape, F32)],
        place=jax.ShapeDtypeStruct,
    )[0]
    return (activated, feature_grad, weight_grad)


def weight_sum(who, keep, give, quick):
    if not quick:
        here, there = (join("core_join", who, CORE, pair) for pair in zip(keep, give))
        total = lax.psum(here + swapped(there, "feat"), "dom")
        for _ in range(7):
            yield lambda *last: last[0]
        yield lambda *last: total
        return
    box = []

    def step(run):
        def go(*last):
            box.append(run(*last))
            return box[-1]

        return go

    def up(value):
        return chosen(value, "dom", lambda i: i + 2 if i % 4 < 2 else None)

    gots = [swapped(value, "dom") for value in give]
    yield step(lambda *last: add("core_there", who, after(keep[1], *last), gots[1]))
    there = box[-1]
    yield step(lambda *last: add("core_here", who, after(keep[0], *last), gots[0]))
    here = box[-1]
    got = up(there)
    yield step(lambda *last: add("chip_there", who, after(there, *last), got))
    got = swapped(box[-1], "feat")
    also = up(here)
    yield step(lambda *last: add("side_sum", who, after(here, *last), also, got))
    for name, bit in (("layer_sum", 4), ("pair_sum", 8)):
        got = chosen(box[-1], "dom", lambda i: i ^ bit if i % 4 >= 2 else None)
        yield step(lambda *last: add(name, who, after(box[-1], *last), got))
    got = chosen(box[-1], "dom", lambda i: i - 2 if i % 4 >= 2 else None)
    yield step(lambda *last: pick("chip_pick", who, after(box[-1], *last), got))
    got = swapped(box[-1], "dom")
    yield step(
        lambda *last: join("weight_grad", who, CORE, [after(box[-1], *last), got], jax.ShapeDtypeStruct)
    )


def solution(mesh):
    in_specs = (
        P("dom", "feat"),
        P(None, "feat"),
        P("dom", "feat"),
        P("dom", None, None),
        P("dom", None, None),
        P("dom", None),
        P("dom", None, None, None, None),
    )
    out_specs = (P("dom", "feat"), P("dom", "feat"), P(None, "feat"))
    return jax.shard_map(body, mesh=mesh, in_specs=in_specs, out_specs=out_specs, check_vma=False)
```

```python
import functools
import math

import jax
import jax.numpy as jnp
from jax import lax
from jax.experimental import pallas as pl
from jax.experimental.pallas import tpu as pltpu
from jax.sharding import PartitionSpec as P

F32 = jnp.float32
BF16 = jnp.bfloat16
TILE = 256
LIMIT = 8 * 1024 * 1024
IN_VMEM = pl.BlockSpec(memory_space=pltpu.VMEM)
IN_SMEM = pl.BlockSpec(memory_space=pltpu.SMEM)

SIDE, CORE, NEAR, FAR, TWO, OWN, CHIP = range(7)


def split(value):
    high = value.astype(BF16)
    low = (value - high.astype(F32)).astype(BF16)
    return high, low


def mm(a, b, dims=((1,), (0,))):
    return lax.dot_general(a, b, (dims, ((), ())), preferred_element_type=F32)


def mm3(a, b, dims=((1,), (0,))):
    (ah, al), (bh, bl) = a, b
    return mm(ah, bh, dims) + (mm(ah, bl, dims) + mm(al, bh, dims))


def call(name, kernel, who, operands, shapes, scratch=(), flops=0, place=pltpu.VMEM):
    moved = sum(a.size * a.dtype.itemsize for a in operands)
    pinned = [pltpu.with_memory_space_constraint(a, pltpu.VMEM) for a in operands]
    return pl.pallas_call(
        kernel,
        in_specs=[IN_SMEM] + [IN_VMEM] * len(operands),
        out_specs=[IN_VMEM] * len(shapes),
        out_shape=[place(*shape) for shape in shapes],
        scratch_shapes=list(scratch),
        compiler_params=pltpu.CompilerParams(vmem_limit_bytes=LIMIT),
        cost_estimate=pl.CostEstimate(flops=int(flops), bytes_accessed=moved, transcendentals=0),
        name=name,
    )(who, *pinned)


def lay_out_kernel(rows, cols, counts, who, blocks, a, t):
    slot = pl.program_id(0)
    cap = blocks.shape[1]
    size = blocks.shape[2]
    for out in (a, t):
        for part in range(2):
            out[part, slot] = jnp.zeros(out.shape[2:], out.dtype)

    def one(k, carry):
        r = pl.multiple_of(rows[slot, k] * size, size)
        c = pl.multiple_of(cols[slot, k] * size, size)
        block = blocks[0, k]
        for part, value in enumerate(split(block)):
            a[part, slot, pl.ds(r, size), pl.ds(c, size)] = value
        for part, value in enumerate(split(block.T)):
            t[part, slot, pl.ds(c, size), pl.ds(r, size)] = value
        return carry

    lax.fori_loop(0, jnp.minimum(counts[0, slot], cap), one, 0)


def lay_out(rows, cols, counts, who, blocks, size_all):
    window, cap, size, _ = blocks.shape
    shape = pltpu.VMEM((2, window, size_all, size_all), BF16)
    return pl.pallas_call(
        lay_out_kernel,
        grid_spec=pltpu.PrefetchScalarGridSpec(
            num_scalar_prefetch=4,
            grid=(window,),
            in_specs=[pl.BlockSpec((1, cap, size, size), lambda s, *_: (s, 0, 0, 0))],
            out_specs=[IN_VMEM] * 2,
        ),
        out_shape=[shape] * 2,
        compiler_params=pltpu.CompilerParams(vmem_limit_bytes=LIMIT),
        cost_estimate=pl.CostEstimate(flops=0, bytes_accessed=20_000_000, transcendentals=0),
        name="lay_out",
    )(rows, cols, counts, who, pltpu.with_memory_space_constraint(blocks, pltpu.HBM))


def forward_kernel(slots, part, has_base, who, matrix, *refs):
    n = len(slots)
    sources, refs = refs[:n], refs[n:]
    base, refs = (refs[0], refs[1:]) if has_base else (None, refs)
    out, (highs, lows) = refs[0], refs[1:]
    rows = out.shape[0]
    from_row = 0 if part is None else (who[SIDE] ^ part) * rows
    for i, source in enumerate(sources):
        highs[i], lows[i] = split(source[...])

    def tile(k, carry):
        there = pl.ds(pl.multiple_of(k * TILE, TILE), TILE)
        here = pl.ds(pl.multiple_of(from_row + k * TILE, TILE), TILE)
        total = None
        if base is not None:
            total = base[here if base.shape[0] > rows else there, :]
        for i, slot in enumerate(slots):
            at = who[slot]
            term = mm3((matrix[0, at, here, :], matrix[1, at, here, :]), (highs[i], lows[i]))
            total = term if total is None else total + term
        out[there, :] = total
        return carry

    lax.fori_loop(0, rows // TILE, tile, 0)


def forward(name, who, matrix, terms, base=None, part=None):
    slots = [slot for slot, _ in terms]
    sources = [source for _, source in terms]
    depth, width = sources[0].shape
    rows = matrix.shape[2] // (1 if part is None else 2)
    extra = [] if base is None else [base]
    return call(
        name,
        functools.partial(forward_kernel, slots, part, base is not None),
        who,
        [matrix, *sources, *extra],
        [((rows, width), F32)],
        [pltpu.VMEM((len(terms), depth, width), BF16)] * 2,
        6 * len(terms) * rows * depth * width,
    )[0]


def backward_kernel(slots, part, n_add, first, pieces, who, matrix, source, *refs):
    addends, outs = refs[:n_add], refs[n_add:]
    depth = source.shape[0]
    parts = split(source[...])
    deep = pl.ds(pl.multiple_of((who[SIDE] ^ part) * depth, depth), depth)
    size = outs[0].shape[0]
    here = pl.ds(first, size * pieces)
    for i, slot in enumerate(slots):
        at = who[slot]
        total = mm3((matrix[0, at, here, deep], matrix[1, at, here, deep]), parts)
        for addend in addends:
            total = total + addend[here, :]
        for k in range(pieces):
            outs[i * pieces + k][...] = total[k * size : (k + 1) * size, :]


def backward(name, who, matrix, slots, source, addends, part, first=0, rows=None, pieces=1):
    depth, width = source.shape
    rows = rows or matrix.shape[2]
    return call(
        name,
        functools.partial(backward_kernel, slots, part, len(addends), first, pieces),
        who,
        [matrix, source, *addends],
        [((rows // pieces, width), F32)] * (len(slots) * pieces),
        flops=6 * len(slots) * rows * depth * width,
    )


def middle_kernel(who, own, far, w_here, w_there, cot, cot_there, *outs):
    act_here, act_there, grad_here, grad_there, g_there = outs
    half = own.shape[1]

    def rows_of(w, which):
        return split(w[pl.ds(pl.multiple_of((who[SIDE] ^ which) * half, half), half), :])

    rows = own.shape[0]
    cot_here = cot.at[pl.ds(pl.multiple_of(who[SIDE] * rows, rows), rows), :]
    source = split(own[...]), split(far[...])
    total = None
    for w, cot, act, grad in (
        (w_here, cot_here, act_here, grad_here),
        (w_there, cot_there, act_there, grad_there),
    ):
        pre = mm3(source[0], rows_of(w, 0)) + mm3(source[1], rows_of(w, 1))
        s = 1.0 / (1.0 + jnp.exp(-pre))
        act[...] = pre * s
        pg = cot[...] * (s + pre * s * (1.0 - s))
        grad[...] = pg
        term = mm3(split(pg), rows_of(w, 1), ((1,), (1,)))
        total = term if total is None else total + term
    g_there[...] = total


def middle(who, own, far, w_here, w_there, cot, cot_there):
    shape = (cot_there.shape, F32)
    flops = 36 * own.shape[0] * own.shape[1] * w_here.shape[1]
    operands = [own, far, w_here, w_there, cot, cot_there]
    return call("middle", middle_kernel, who, operands, [shape] * 5, flops=flops)


def keep_kernel(who, w_here, w_there, grad_here, grad_there, g_here):
    half = g_here.shape[1]
    at = pl.ds(pl.multiple_of(who[SIDE] * half, half), half)
    total = None
    for w, grad in ((w_here, grad_here), (w_there, grad_there)):
        term = mm3(split(grad[...]), split(w[at, :]), ((1,), (1,)))
        total = term if total is None else total + term
    g_here[...] = total


def weight_kernel(scale, which, who, own, far, grad_here, grad_there, here, there):
    mine = who[SIDE] == (who[CORE] ^ which)
    turned = split(jnp.where(mine, own[...], far[...]).T)
    for grad, out in ((grad_here, here), (grad_there, there)):
        out[...] = mm3(turned, split(grad[...])) * scale


def weight_term(name, who, scale, which, own, far, grad_here, grad_there):
    rows, half = own.shape
    hidden = grad_here.shape[1]
    return call(
        name,
        functools.partial(weight_kernel, scale, which),
        who,
        [own, far, grad_here, grad_there],
        [((half, hidden), F32)] * 2,
        flops=12 * rows * half * hidden,
    )


def half_kernel(which, who, whole, out):
    rows = out.shape[0]
    out[...] = whole[pl.ds(pl.multiple_of((who[SIDE] ^ which) * rows, rows), rows), :]


def join_kernel(place, who, *refs):
    parts, out = refs[:-1], refs[-1]
    rows = parts[0].shape[0]
    for k, part in enumerate(parts):
        out[pl.ds(pl.multiple_of((who[place] ^ k) * rows, rows), rows), :] = part[...]


def join(name, who, place, parts, kind=pltpu.VMEM):
    rows, cols = parts[0].shape
    shape = (rows * len(parts), cols)
    return call(
        name, functools.partial(join_kernel, place), who, parts, [(shape, F32)], place=kind
    )[0]


def pick_kernel(who, one, other, out):
    out[...] = jnp.where(who[CHIP] == 1, one[...], other[...])


def pick(name, who, one, other):
    return call(name, pick_kernel, who, [one, other], [(one.shape, F32)])[0]


def add_kernel(who, *refs):
    total = refs[0][...]
    for ref in refs[1:-1]:
        total = total + ref[...]
    refs[-1][...] = total


def add(name, who, *parts):
    return call(name, add_kernel, who, parts, [(parts[0].shape, F32)])[0]


def moved(value, axis, even, odd):
    peers = lax.axis_size(axis)
    perm = [(i, (i + (odd if i % 2 else even)) % peers) for i in range(peers)]
    return lax.ppermute(value, axis, perm)


def chosen(value, axis, target):
    peers = lax.axis_size(axis)
    pairs = [(i, target(i)) for i in range(peers)]
    return lax.ppermute(value, axis, [pair for pair in pairs if pair[1] is not None])


def swapped(value, axis):
    return chosen(value, axis, lambda i: i ^ 1)


def after(value, *others):
    return lax.optimization_barrier((value, *others))[0]


def body(features, weight, cotangent, block_rows, block_cols, block_counts, block_values):
    rows, width = features.shape
    hidden = weight.shape[1]
    depth = weight.shape[0]
    parts = lax.axis_size("dom")
    side = lax.axis_index("feat").astype(jnp.int32)
    place = lax.axis_index("dom").astype(jnp.int32)
    odd = place & 1
    zero = place * 0
    who = jnp.stack([side, odd, 1 + 2 * odd, 3 - 2 * odd, zero + 2, zero, (place >> 1) & 1])

    near = moved(features, "dom", 3, 1)
    far = moved(features, "dom", 1, 3)
    w_there = swapped(weight, "feat")
    half_shape = ((rows // 2, hidden), F32)
    cot_give = call("cot_give", functools.partial(half_kernel, 1), who, [cotangent], [half_shape])[0]
    cot_there = swapped(cot_give, "feat")

    a, t = lay_out(
        block_rows[0], block_cols[0], block_counts, who, block_values[0], rows
    )
    total = forward("agg_own", who, a, [(OWN, features)])
    near = after(near, total, w_there, cot_there)
    two = swapped(near, "dom")
    total = forward("agg_near", who, a, [(NEAR, near)], total)
    far = after(far, total)
    give = forward("agg_give", who, a, [(FAR, far), (TWO, two)], total, 1)
    there = swapped(give, "feat")
    keep = forward("agg_keep", who, a, [(FAR, far), (TWO, after(two, give))], total, 0)

    act_here, act_there, grad_here, grad_there, g_give = middle(
        who, keep, there, weight, w_there, cotangent, cot_there
    )
    g_there = swapped(g_give, "feat")
    scale = 1.0 / math.sqrt(rows * parts)
    w_give = weight_term("weight_give", who, scale, 1, keep, there, grad_here, grad_there)
    w_keep = weight_term(
        "weight_keep", who, scale, 0, after(keep, w_give[0]), there, grad_here, grad_there
    )
    quick = parts == 16
    gate = []
    steps = weight_sum(who, w_keep, w_give, quick, gate)

    last = next(steps)(grad_here)
    last = next(steps)(last)
    g_here = call(
        "keep",
        keep_kernel,
        who,
        [weight, w_there, after(grad_here, last), grad_there],
        [(keep.shape, F32)],
        flops=12 * rows // 2 * width * hidden,
    )[0]
    firsts = backward("back_here", who, t, [TWO, FAR, NEAR, OWN], after(g_here, last), [], 0)
    last = next(steps)(firsts[0])
    g_there = after(g_there, last)
    last = backward("back_two", who, t, [TWO], g_there, [firsts[0]], 1)[0]
    two = swapped(last, "dom")
    last = backward("back_far", who, t, [FAR], after(g_there, last), [firsts[1]], 1)[0]
    far = moved(last, "dom", -3, -1)
    last = backward("back_near", who, t, [NEAR], after(g_there, last), [firsts[2], two], 1)[0]
    near = moved(last, "dom", -1, -3)
    mine = backward("back_own", who, t, [OWN], after(g_there, last), [firsts[3]], 1)[0]
    gate.append(mine)
    last = next(steps)(mine)
    act_got = swapped(after(act_there, last), "feat")
    last = next(steps)(last, far)
    last = next(steps)(last, near)
    activated = join("activated", who, SIDE, [after(act_here, last), act_got], jax.ShapeDtypeStruct)
    last = next(steps)(activated)
    weight_grad = next(steps)(last)
    feature_grad = call(
        "feature_grad",
        add_kernel,
        who,
        [after(mine, weight_grad), far, near],
        [(features.shape, F32)],
        place=jax.ShapeDtypeStruct,
    )[0]
    return (activated, feature_grad, weight_grad)


def weight_sum(who, keep, give, quick, gate):
    if not quick:
        here, there = (join("core_join", who, CORE, pair) for pair in zip(keep, give))
        total = lax.psum(here + swapped(there, "feat"), "dom")
        for _ in range(7):
            yield lambda *last: last[0]
        yield lambda *last: total
        return
    box = []

    def step(run):
        def go(*last):
            box.append(run(*last))
            return box[-1]

        return go

    def up(value):
        return chosen(value, "dom", lambda i: i + 2 if i % 4 < 2 else None)

    gots = [swapped(value, "dom") for value in give]
    yield step(lambda *last: add("core_there", who, after(keep[1], *last), gots[1]))
    there = box[-1]
    yield step(lambda *last: add("core_here", who, after(keep[0], *last), gots[0]))
    here = box[-1]
    got = up(there)
    yield step(lambda *last: add("chip_there", who, after(there, *last), got))
    got = swapped(after(box[-1], *gate), "feat")
    also = up(after(here, *gate))
    yield step(lambda *last: add("side_sum", who, after(here, *last), also, got))
    for name, bit in (("layer_sum", 4), ("pair_sum", 8)):
        got = chosen(box[-1], "dom", lambda i: i ^ bit if i % 4 >= 2 else None)
        yield step(lambda *last: add(name, who, after(box[-1], *last), got))
    got = chosen(box[-1], "dom", lambda i: i - 2 if i % 4 >= 2 else None)
    yield step(lambda *last: pick("chip_pick", who, after(box[-1], *last), got))
    got = swapped(box[-1], "dom")
    yield step(
        lambda *last: join("weight_grad", who, CORE, [after(box[-1], *last), got], jax.ShapeDtypeStruct)
    )


def solution(mesh):
    in_specs = (
        P("dom", "feat"),
        P(None, "feat"),
        P("dom", "feat"),
        P("dom", None, None),
        P("dom", None, None),
        P("dom", None),
        P("dom", None, None, None, None),
    )
    out_specs = (P("dom", "feat"), P("dom", "feat"), P(None, "feat"))
    return jax.shard_map(body, mesh=mesh, in_specs=in_specs, out_specs=out_specs, check_vma=False)
```

```python
import functools
import math

import jax
import jax.numpy as jnp
from jax import lax
from jax.experimental import pallas as pl
from jax.experimental.pallas import tpu as pltpu
from jax.sharding import PartitionSpec as P

F32 = jnp.float32
BF16 = jnp.bfloat16
TILE = 256
LIMIT = 8 * 1024 * 1024
IN_VMEM = pl.BlockSpec(memory_space=pltpu.VMEM)
IN_SMEM = pl.BlockSpec(memory_space=pltpu.SMEM)

SIDE, CORE, NEAR, FAR, TWO, OWN, CHIP = range(7)


def split(value):
    high = value.astype(BF16)
    low = (value - high.astype(F32)).astype(BF16)
    return high, low


def mm(a, b, dims=((1,), (0,))):
    return lax.dot_general(a, b, (dims, ((), ())), preferred_element_type=F32)


def mm3(a, b, dims=((1,), (0,))):
    (ah, al), (bh, bl) = a, b
    return mm(ah, bh, dims) + (mm(ah, bl, dims) + mm(al, bh, dims))


def call(name, kernel, who, operands, shapes, scratch=(), flops=0, place=pltpu.VMEM):
    moved = sum(a.size * a.dtype.itemsize for a in operands)
    pinned = [pltpu.with_memory_space_constraint(a, pltpu.VMEM) for a in operands]
    return pl.pallas_call(
        kernel,
        in_specs=[IN_SMEM] + [IN_VMEM] * len(operands),
        out_specs=[IN_VMEM] * len(shapes),
        out_shape=[place(*shape) for shape in shapes],
        scratch_shapes=list(scratch),
        compiler_params=pltpu.CompilerParams(vmem_limit_bytes=LIMIT),
        cost_estimate=pl.CostEstimate(flops=int(flops), bytes_accessed=moved, transcendentals=0),
        name=name,
    )(who, *pinned)


def lay_out_kernel(turn, rows, cols, counts, blocks, out, mark):
    slot = pl.program_id(0)
    cap = blocks.shape[1]
    size = blocks.shape[2]
    for part in range(2):
        out[part, slot] = jnp.zeros(out.shape[2:], out.dtype)

    def one(k, carry):
        r = pl.multiple_of(rows[slot, k] * size, size)
        c = pl.multiple_of(cols[slot, k] * size, size)
        block = blocks[0, k]
        if turn:
            block, r, c = block.T, c, r
        for part, value in enumerate(split(block)):
            out[part, slot, pl.ds(r, size), pl.ds(c, size)] = value
        return carry

    lax.fori_loop(0, jnp.minimum(counts[0, slot], cap), one, 0)
    mark[...] = jnp.zeros_like(mark)


def lay_out(name, turn, rows, cols, counts, blocks, size_all):
    window, cap, size, _ = blocks.shape
    shapes = [pltpu.VMEM((2, window, size_all, size_all), BF16)]
    shapes += [pltpu.VMEM((8, 128), F32)]
    return pl.pallas_call(
        functools.partial(lay_out_kernel, turn),
        grid_spec=pltpu.PrefetchScalarGridSpec(
            num_scalar_prefetch=3,
            grid=(window,),
            in_specs=[pl.BlockSpec((1, cap, size, size), lambda s, *_: (s, 0, 0, 0))],
            out_specs=[IN_VMEM] * len(shapes),
        ),
        out_shape=shapes,
        compiler_params=pltpu.CompilerParams(vmem_limit_bytes=LIMIT),
        cost_estimate=pl.CostEstimate(flops=0, bytes_accessed=20_000_000, transcendentals=0),
        name=name,
    )(rows, cols, counts, pltpu.with_memory_space_constraint(blocks, pltpu.HBM))


def forward_kernel(slots, part, has_base, who, matrix, *refs):
    n = len(slots)
    sources, refs = refs[:n], refs[n:]
    base, refs = (refs[0], refs[1:]) if has_base else (None, refs)
    out, (highs, lows) = refs[0], refs[1:]
    rows = out.shape[0]
    from_row = 0 if part is None else (who[SIDE] ^ part) * rows
    for i, source in enumerate(sources):
        highs[i], lows[i] = split(source[...])

    def tile(k, carry):
        there = pl.ds(pl.multiple_of(k * TILE, TILE), TILE)
        here = pl.ds(pl.multiple_of(from_row + k * TILE, TILE), TILE)
        total = None
        if base is not None:
            total = base[here if base.shape[0] > rows else there, :]
        for i, slot in enumerate(slots):
            at = who[slot]
            term = mm3((matrix[0, at, here, :], matrix[1, at, here, :]), (highs[i], lows[i]))
            total = term if total is None else total + term
        out[there, :] = total
        return carry

    lax.fori_loop(0, rows // TILE, tile, 0)


def forward(name, who, matrix, terms, base=None, part=None):
    slots = [slot for slot, _ in terms]
    sources = [source for _, source in terms]
    depth, width = sources[0].shape
    rows = matrix.shape[2] // (1 if part is None else 2)
    extra = [] if base is None else [base]
    return call(
        name,
        functools.partial(forward_kernel, slots, part, base is not None),
        who,
        [matrix, *sources, *extra],
        [((rows, width), F32)],
        [pltpu.VMEM((len(terms), depth, width), BF16)] * 2,
        6 * len(terms) * rows * depth * width,
    )[0]


def backward_kernel(slots, part, n_add, who, matrix, source, *refs):
    addends, outs = refs[:n_add], refs[-len(slots) :]
    depth = source.shape[0]
    parts = split(source[...])
    deep = pl.ds(pl.multiple_of((who[SIDE] ^ part) * depth, depth), depth)
    for slot, out in zip(slots, outs):
        at = who[slot]
        total = mm3((matrix[0, at, :, deep], matrix[1, at, :, deep]), parts)
        for addend in addends:
            total = total + addend[...]
        out[...] = total


def backward(name, who, matrix, slots, source, addends, part, *marks):
    depth, width = source.shape
    rows = matrix.shape[2]
    return call(
        name,
        functools.partial(backward_kernel, slots, part, len(addends)),
        who,
        [matrix, source, *addends, *marks],
        [((rows, width), F32)] * len(slots),
        flops=6 * len(slots) * rows * depth * width,
    )


def middle_kernel(who, own, far, w_here, w_there, cot, cot_there, *outs):
    act_here, act_there, grad_here, grad_there, g_there = outs
    half = own.shape[1]

    def rows_of(w, which):
        return split(w[pl.ds(pl.multiple_of((who[SIDE] ^ which) * half, half), half), :])

    rows = own.shape[0]
    cot_here = cot.at[pl.ds(pl.multiple_of(who[SIDE] * rows, rows), rows), :]
    source = split(own[...]), split(far[...])
    total = None
    for w, cot, act, grad in (
        (w_here, cot_here, act_here, grad_here),
        (w_there, cot_there, act_there, grad_there),
    ):
        pre = mm3(source[0], rows_of(w, 0)) + mm3(source[1], rows_of(w, 1))
        s = 1.0 / (1.0 + jnp.exp(-pre))
        act[...] = pre * s
        pg = cot[...] * (s + pre * s * (1.0 - s))
        grad[...] = pg
        term = mm3(split(pg), rows_of(w, 1), ((1,), (1,)))
        total = term if total is None else total + term
    g_there[...] = total


def middle(who, own, far, w_here, w_there, cot, cot_there):
    shape = (cot_there.shape, F32)
    flops = 36 * own.shape[0] * own.shape[1] * w_here.shape[1]
    operands = [own, far, w_here, w_there, cot, cot_there]
    return call("middle", middle_kernel, who, operands, [shape] * 5, flops=flops)


def keep_kernel(who, w_here, w_there, grad_here, grad_there, g_here):
    half = g_here.shape[1]
    at = pl.ds(pl.multiple_of(who[SIDE] * half, half), half)
    total = None
    for w, grad in ((w_here, grad_here), (w_there, grad_there)):
        term = mm3(split(grad[...]), split(w[at, :]), ((1,), (1,)))
        total = term if total is None else total + term
    g_here[...] = total


def weight_kernel(scale, which, who, own, far, grad_here, grad_there, here, there):
    mine = who[SIDE] == (who[CORE] ^ which)
    turned = split(jnp.where(mine, own[...], far[...]).T)
    for grad, out in ((grad_here, here), (grad_there, there)):
        out[...] = mm3(turned, split(grad[...])) * scale


def weight_term(name, who, scale, which, own, far, grad_here, grad_there):
    rows, half = own.shape
    hidden = grad_here.shape[1]
    return call(
        name,
        functools.partial(weight_kernel, scale, which),
        who,
        [own, far, grad_here, grad_there],
        [((half, hidden), F32)] * 2,
        flops=12 * rows * half * hidden,
    )


def half_kernel(which, who, whole, out):
    rows = out.shape[0]
    out[...] = whole[pl.ds(pl.multiple_of((who[SIDE] ^ which) * rows, rows), rows), :]


def join_kernel(place, who, *refs):
    parts, out = refs[:-1], refs[-1]
    rows = parts[0].shape[0]
    for k, part in enumerate(parts):
        out[pl.ds(pl.multiple_of((who[place] ^ k) * rows, rows), rows), :] = part[...]


def join(name, who, place, parts, kind=pltpu.VMEM):
    rows, cols = parts[0].shape
    shape = (rows * len(parts), cols)
    return call(
        name, functools.partial(join_kernel, place), who, parts, [(shape, F32)], place=kind
    )[0]


def pick_kernel(who, one, other, out):
    out[...] = jnp.where(who[CHIP] == 1, one[...], other[...])


def pick(name, who, one, other):
    return call(name, pick_kernel, who, [one, other], [(one.shape, F32)])[0]


def near_kernel(who, straight, relayed, crossed, _, out):
    last = who[CHIP] * who[CORE] == 1
    out[...] = jnp.where(last, crossed[...], straight[...] + relayed[...])


def add_kernel(who, *refs):
    total = refs[0][...]
    for ref in refs[1:-1]:
        total = total + ref[...]
    refs[-1][...] = total


def add(name, who, *parts):
    return call(name, add_kernel, who, parts, [(parts[0].shape, F32)])[0]


def moved(value, axis, even, odd):
    peers = lax.axis_size(axis)
    perm = [(i, (i + (odd if i % 2 else even)) % peers) for i in range(peers)]
    return lax.ppermute(value, axis, perm)


def chosen(value, axis, target):
    peers = lax.axis_size(axis)
    pairs = [(i, target(i)) for i in range(peers)]
    return lax.ppermute(value, axis, [pair for pair in pairs if pair[1] is not None])


def swapped(value, axis):
    return chosen(value, axis, lambda i: i ^ 1)


def after(value, *others):
    return lax.optimization_barrier((value, *others))[0]


def body(features, weight, cotangent, block_rows, block_cols, block_counts, block_values):
    rows, width = features.shape
    hidden = weight.shape[1]
    depth = weight.shape[0]
    parts = lax.axis_size("dom")
    side = lax.axis_index("feat").astype(jnp.int32)
    place = lax.axis_index("dom").astype(jnp.int32)
    odd = place & 1
    zero = place * 0
    who = jnp.stack([side, odd, 1 + 2 * odd, 3 - 2 * odd, zero + 2, zero, (place >> 1) & 1])

    far = moved(features, "dom", 1, 3)
    near_a = chosen(
        features, "dom", lambda i: ((i + 3) % parts, None, i - 1, None)[i % 4]
    )
    w_there = swapped(weight, "feat")
    places = block_rows[0], block_cols[0], block_counts
    a, ready = lay_out("lay_out", False, *places, block_values[0], rows)
    relay = chosen(
        after(near_a, far, w_there, ready), "dom", lambda i: (i + 4) % parts if i % 4 == 1 else None
    )
    near_b = chosen(
        after(features, near_a), "dom", lambda i: (i + 1) % parts if i % 2 else None
    )
    half_shape = ((rows // 2, hidden), F32)
    cot_give = call("cot_give", functools.partial(half_kernel, 1), who, [cotangent], [half_shape])[0]
    cot_there = swapped(cot_give, "feat")

    total = forward("agg_far", who, a, [(OWN, features), (FAR, far)])
    near = call(
        "near",
        near_kernel,
        who,
        [after(near_b, total, cot_there), relay, near_a, ready],
        [(features.shape, F32)],
    )[0]
    two = swapped(near, "dom")
    total = forward("agg_near", who, a, [(NEAR, near)], total)
    give = forward("agg_give", who, a, [(TWO, two)], total, 1)
    there = swapped(give, "feat")
    keep = forward("agg_keep", who, a, [(TWO, after(two, give))], total, 0)
    t, mark = lay_out(
        "lay_out_turned", True, after(places[0], give), *places[1:], block_values[0], rows
    )
    there = after(there, keep, mark)

    act_here, act_there, grad_here, grad_there, g_give = middle(
        who, keep, there, weight, w_there, cotangent, cot_there
    )
    g_there = swapped(g_give, "feat")
    scale = 1.0 / math.sqrt(rows * parts)
    w_give = weight_term("weight_give", who, scale, 1, keep, there, grad_here, grad_there)
    w_keep = weight_term(
        "weight_keep", who, scale, 0, after(keep, w_give[0]), there, grad_here, grad_there
    )
    quick = parts == 16
    steps = weight_sum(who, w_keep, w_give, quick)

    last = next(steps)(grad_here)
    last = next(steps)(last)
    g_here = call(
        "keep",
        keep_kernel,
        who,
        [weight, w_there, after(grad_here, last), grad_there],
        [(keep.shape, F32)],
        flops=12 * rows // 2 * width * hidden,
    )[0]
    firsts = backward("back_here", who, t, [TWO, FAR, NEAR, OWN], after(g_here, last), [], 0, mark)
    last = next(steps)(firsts[0])
    g_there = after(g_there, last)
    last = backward("back_two", who, t, [TWO], g_there, [firsts[0]], 1)[0]
    two = swapped(last, "dom")
    last = backward("back_far", who, t, [FAR], after(g_there, last), [firsts[1]], 1)[0]
    far = moved(last, "dom", -3, -1)
    last = backward("back_near", who, t, [NEAR], after(g_there, last), [firsts[2], two], 1)[0]
    near = moved(last, "dom", -1, -3)
    last = next(steps)(last)
    act_got = swapped(after(act_there, last), "feat")
    mine = backward("back_own", who, t, [OWN], after(g_there, last), [firsts[3]], 1)[0]
    last = next(steps)(mine, far)
    last = next(steps)(last)
    activated = join("activated", who, SIDE, [after(act_here, last), act_got], jax.ShapeDtypeStruct)
    last = next(steps)(activated, near)
    weight_grad = next(steps)(last)
    feature_grad = call(
        "feature_grad",
        add_kernel,
        who,
        [after(mine, weight_grad), far, near],
        [(features.shape, F32)],
        place=jax.ShapeDtypeStruct,
    )[0]
    return (activated, feature_grad, weight_grad)


def weight_sum(who, keep, give, quick):
    if not quick:
        here, there = (join("core_join", who, CORE, pair) for pair in zip(keep, give))
        total = lax.psum(here + swapped(there, "feat"), "dom")
        for _ in range(7):
            yield lambda *last: last[0]
        yield lambda *last: total
        return
    box = []

    def step(run):
        def go(*last):
            box.append(run(*last))
            return box[-1]

        return go

    def up(value):
        return chosen(value, "dom", lambda i: i + 2 if i % 4 < 2 else None)

    gots = [swapped(value, "dom") for value in give]
    yield step(lambda *last: add("core_there", who, after(keep[1], *last), gots[1]))
    there = box[-1]
    yield step(lambda *last: add("core_here", who, after(keep[0], *last), gots[0]))
    here = box[-1]
    got = up(there)
    also = up(here)
    yield step(lambda *last: add("chip_there", who, after(there, *last, also), got))
    got = swapped(box[-1], "feat")
    yield step(lambda *last: add("side_sum", who, after(here, *last), also, got))
    for name, bit in (("layer_sum", 4), ("pair_sum", 8)):
        got = chosen(box[-1], "dom", lambda i: i ^ bit if i % 4 >= 2 else None)
        yield step(lambda *last: add(name, who, after(box[-1], *last), got))
    got = chosen(box[-1], "dom", lambda i: i - 2 if i % 4 >= 2 else None)
    yield step(lambda *last: pick("chip_pick", who, after(box[-1], *last), got))
    got = swapped(box[-1], "dom")
    yield step(
        lambda *last: join("weight_grad", who, CORE, [after(box[-1], *last), got], jax.ShapeDtypeStruct)
    )


def solution(mesh):
    in_specs = (
        P("dom", "feat"),
        P(None, "feat"),
        P("dom", "feat"),
        P("dom", None, None),
        P("dom", None, None),
        P("dom", None),
        P("dom", None, None, None, None),
    )
    out_specs = (P("dom", "feat"), P("dom", "feat"), P(None, "feat"))
    return jax.shard_map(body, mesh=mesh, in_specs=in_specs, out_specs=out_specs, check_vma=False)
```

```python
import functools
import math

import jax
import jax.numpy as jnp
from jax import lax
from jax.experimental import pallas as pl
from jax.experimental.pallas import tpu as pltpu
from jax.sharding import PartitionSpec as P

F32 = jnp.float32
BF16 = jnp.bfloat16
TILE = 256
LIMIT = 8 * 1024 * 1024
IN_VMEM = pl.BlockSpec(memory_space=pltpu.VMEM)
IN_SMEM = pl.BlockSpec(memory_space=pltpu.SMEM)

SIDE, CORE, NEAR, FAR, TWO, OWN, CHIP, LAYER = range(8)


def split(value):
    high = value.astype(BF16)
    low = (value - high.astype(F32)).astype(BF16)
    return high, low


def mm(a, b, dims=((1,), (0,))):
    return lax.dot_general(a, b, (dims, ((), ())), preferred_element_type=F32)


def mm3(a, b, dims=((1,), (0,))):
    (ah, al), (bh, bl) = a, b
    return mm(ah, bh, dims) + (mm(ah, bl, dims) + mm(al, bh, dims))


def call(name, kernel, who, operands, shapes, scratch=(), flops=0, place=pltpu.VMEM):
    moved = sum(a.size * a.dtype.itemsize for a in operands)
    pinned = [pltpu.with_memory_space_constraint(a, pltpu.VMEM) for a in operands]
    return pl.pallas_call(
        kernel,
        in_specs=[IN_SMEM] + [IN_VMEM] * len(operands),
        out_specs=[IN_VMEM] * len(shapes),
        out_shape=[place(*shape) for shape in shapes],
        scratch_shapes=list(scratch),
        compiler_params=pltpu.CompilerParams(vmem_limit_bytes=LIMIT),
        cost_estimate=pl.CostEstimate(flops=int(flops), bytes_accessed=moved, transcendentals=0),
        name=name,
    )(who, *pinned)


def lay_out_kernel(rows, cols, counts, who, blocks, a, t):
    slot = pl.program_id(0)
    cap = blocks.shape[1]
    size = blocks.shape[2]
    for out in (a, t):
        for part in range(2):
            out[part, slot] = jnp.zeros(out.shape[2:], out.dtype)

    def one(k, carry):
        r = pl.multiple_of(rows[slot, k] * size, size)
        c = pl.multiple_of(cols[slot, k] * size, size)
        block = blocks[0, k]
        for part, value in enumerate(split(block)):
            a[part, slot, pl.ds(r, size), pl.ds(c, size)] = value
        for part, value in enumerate(split(block.T)):
            t[part, slot, pl.ds(c, size), pl.ds(r, size)] = value
        return carry

    lax.fori_loop(0, jnp.minimum(counts[0, slot], cap), one, 0)


def lay_out(rows, cols, counts, who, blocks, size_all):
    window, cap, size, _ = blocks.shape
    shape = pltpu.VMEM((2, window, size_all, size_all), BF16)
    return pl.pallas_call(
        lay_out_kernel,
        grid_spec=pltpu.PrefetchScalarGridSpec(
            num_scalar_prefetch=4,
            grid=(window,),
            in_specs=[pl.BlockSpec((1, cap, size, size), lambda s, *_: (s, 0, 0, 0))],
            out_specs=[IN_VMEM] * 2,
        ),
        out_shape=[shape] * 2,
        compiler_params=pltpu.CompilerParams(vmem_limit_bytes=LIMIT),
        cost_estimate=pl.CostEstimate(flops=0, bytes_accessed=20_000_000, transcendentals=0),
        name="lay_out",
    )(rows, cols, counts, who, pltpu.with_memory_space_constraint(blocks, pltpu.HBM))


def forward_kernel(slots, part, has_base, who, matrix, *refs):
    n = len(slots)
    sources, refs = refs[:n], refs[n:]
    base, refs = (refs[0], refs[1:]) if has_base else (None, refs)
    out, (highs, lows) = refs[0], refs[1:]
    rows = out.shape[0]
    from_row = 0 if part is None else (who[SIDE] ^ part) * rows
    for i, source in enumerate(sources):
        highs[i], lows[i] = split(source[...])

    def tile(k, carry):
        there = pl.ds(pl.multiple_of(k * TILE, TILE), TILE)
        here = pl.ds(pl.multiple_of(from_row + k * TILE, TILE), TILE)
        total = None
        if base is not None:
            total = base[here if base.shape[0] > rows else there, :]
        for i, slot in enumerate(slots):
            at = who[slot]
            term = mm3((matrix[0, at, here, :], matrix[1, at, here, :]), (highs[i], lows[i]))
            total = term if total is None else total + term
        out[there, :] = total
        return carry

    lax.fori_loop(0, rows // TILE, tile, 0)


def forward(name, who, matrix, terms, base=None, part=None):
    slots = [slot for slot, _ in terms]
    sources = [source for _, source in terms]
    depth, width = sources[0].shape
    rows = matrix.shape[2] // (1 if part is None else 2)
    extra = [] if base is None else [base]
    return call(
        name,
        functools.partial(forward_kernel, slots, part, base is not None),
        who,
        [matrix, *sources, *extra],
        [((rows, width), F32)],
        [pltpu.VMEM((len(terms), depth, width), BF16)] * 2,
        6 * len(terms) * rows * depth * width,
    )[0]


def backward_kernel(slots, part, n_add, first, pieces, who, matrix, source, *refs):
    addends, outs = refs[:n_add], refs[n_add:]
    depth = source.shape[0]
    parts = split(source[...])
    deep = pl.ds(pl.multiple_of((who[SIDE] ^ part) * depth, depth), depth)
    size = outs[0].shape[0]
    here = pl.ds(first, size * pieces)
    for i, slot in enumerate(slots):
        at = who[slot]
        total = mm3((matrix[0, at, here, deep], matrix[1, at, here, deep]), parts)
        for addend in addends:
            total = total + addend[here, :]
        for k in range(pieces):
            outs[i * pieces + k][...] = total[k * size : (k + 1) * size, :]


def backward(name, who, matrix, slots, source, addends, part, first=0, rows=None, pieces=1):
    depth, width = source.shape
    rows = rows or matrix.shape[2]
    return call(
        name,
        functools.partial(backward_kernel, slots, part, len(addends), first, pieces),
        who,
        [matrix, source, *addends],
        [((rows // pieces, width), F32)] * (len(slots) * pieces),
        flops=6 * len(slots) * rows * depth * width,
    )


def middle_kernel(who, own, far, w_here, w_there, cot, cot_there, *outs):
    act_here, act_there, grad_here, grad_there, g_there = outs
    half = own.shape[1]

    def rows_of(w, which):
        return split(w[pl.ds(pl.multiple_of((who[SIDE] ^ which) * half, half), half), :])

    rows = own.shape[0]
    cot_here = cot.at[pl.ds(pl.multiple_of(who[SIDE] * rows, rows), rows), :]
    source = split(own[...]), split(far[...])
    total = None
    for w, cot, act, grad in (
        (w_here, cot_here, act_here, grad_here),
        (w_there, cot_there, act_there, grad_there),
    ):
        pre = mm3(source[0], rows_of(w, 0)) + mm3(source[1], rows_of(w, 1))
        s = 1.0 / (1.0 + jnp.exp(-pre))
        act[...] = pre * s
        pg = cot[...] * (s + pre * s * (1.0 - s))
        grad[...] = pg
        term = mm3(split(pg), rows_of(w, 1), ((1,), (1,)))
        total = term if total is None else total + term
    g_there[...] = total


def middle(who, own, far, w_here, w_there, cot, cot_there):
    shape = (cot_there.shape, F32)
    flops = 36 * own.shape[0] * own.shape[1] * w_here.shape[1]
    operands = [own, far, w_here, w_there, cot, cot_there]
    return call("middle", middle_kernel, who, operands, [shape] * 5, flops=flops)


def keep_kernel(who, w_here, w_there, grad_here, grad_there, g_here):
    half = g_here.shape[1]
    at = pl.ds(pl.multiple_of(who[SIDE] * half, half), half)
    total = None
    for w, grad in ((w_here, grad_here), (w_there, grad_there)):
        term = mm3(split(grad[...]), split(w[at, :]), ((1,), (1,)))
        total = term if total is None else total + term
    g_here[...] = total


def weight_kernel(scale, which, who, own, far, grad_here, grad_there, here, there):
    mine = who[SIDE] == (who[CORE] ^ which)
    turned = split(jnp.where(mine, own[...], far[...]).T)
    for grad, out in ((grad_here, here), (grad_there, there)):
        out[...] = mm3(turned, split(grad[...])) * scale


def weight_term(name, who, scale, which, own, far, grad_here, grad_there):
    rows, half = own.shape
    hidden = grad_here.shape[1]
    return call(
        name,
        functools.partial(weight_kernel, scale, which),
        who,
        [own, far, grad_here, grad_there],
        [((half, hidden), F32)] * 2,
        flops=12 * rows * half * hidden,
    )


def half_kernel(which, who, whole, out):
    rows = out.shape[0]
    out[...] = whole[pl.ds(pl.multiple_of((who[SIDE] ^ which) * rows, rows), rows), :]


def join_kernel(place, who, *refs):
    parts, out = refs[:-1], refs[-1]
    rows = parts[0].shape[0]
    for k, part in enumerate(parts):
        out[pl.ds(pl.multiple_of((who[place] ^ k) * rows, rows), rows), :] = part[...]


def join(name, who, place, parts, kind=pltpu.VMEM):
    rows, cols = parts[0].shape
    shape = (rows * len(parts), cols)
    return call(
        name, functools.partial(join_kernel, place), who, parts, [(shape, F32)], place=kind
    )[0]


def pick_kernel(who, ready, later, ready_sent, later_sent, out):
    rows = ready.shape[0]
    odd = who[CHIP] == 1
    for which, one, other in ((0, ready, ready_sent), (1, later, later_sent)):
        at = pl.ds(pl.multiple_of((who[LAYER] ^ which) * rows, rows), rows)
        out[at, :] = jnp.where(odd, one[...], other[...])


def pick(name, who, *parts):
    rows, cols = parts[0].shape
    return call(name, pick_kernel, who, parts, [((2 * rows, cols), F32)])[0]


def hand_out(full, outs, place):
    rows = outs[0].shape[0]
    for k, out in enumerate(outs):
        out[...] = full[pl.ds(pl.multiple_of((place ^ k) * rows, rows), rows), :]


def side_kernel(who, one, two, three, keep, give, full):
    full[...] = one[...] + two[...] + three[...]
    hand_out(full, (keep, give), who[LAYER])


def side_sum(name, who, *parts):
    rows, cols = parts[0].shape
    shape = ((rows // 2, cols), F32)
    return call(name, side_kernel, who, parts, [shape] * 2, [pltpu.VMEM((rows, cols), F32)])


def add_kernel(who, *refs):
    total = refs[0][...]
    for ref in refs[1:-1]:
        total = total + ref[...]
    refs[-1][...] = total


def add(name, who, *parts):
    return call(name, add_kernel, who, parts, [(parts[0].shape, F32)])[0]


def moved(value, axis, even, odd):
    peers = lax.axis_size(axis)
    perm = [(i, (i + (odd if i % 2 else even)) % peers) for i in range(peers)]
    return lax.ppermute(value, axis, perm)


def chosen(value, axis, target):
    peers = lax.axis_size(axis)
    pairs = [(i, target(i)) for i in range(peers)]
    return lax.ppermute(value, axis, [pair for pair in pairs if pair[1] is not None])


def swapped(value, axis):
    return chosen(value, axis, lambda i: i ^ 1)


def after(value, *others):
    return lax.optimization_barrier((value, *others))[0]


def body(features, weight, cotangent, block_rows, block_cols, block_counts, block_values):
    rows, width = features.shape
    hidden = weight.shape[1]
    depth = weight.shape[0]
    parts = lax.axis_size("dom")
    side = lax.axis_index("feat").astype(jnp.int32)
    place = lax.axis_index("dom").astype(jnp.int32)
    odd = place & 1
    zero = place * 0
    who = jnp.stack([side, odd, 1 + 2 * odd, 3 - 2 * odd, zero + 2, zero, (place >> 1) & 1,
                     (place >> 2) & 1])

    near = moved(features, "dom", 3, 1)
    far = moved(features, "dom", 1, 3)
    w_there = swapped(weight, "feat")
    half_shape = ((rows // 2, hidden), F32)
    cot_give = call("cot_give", functools.partial(half_kernel, 1), who, [cotangent], [half_shape])[0]
    cot_there = swapped(cot_give, "feat")

    a, t = lay_out(
        block_rows[0], block_cols[0], block_counts, who, block_values[0], rows
    )
    total = forward("agg_own", who, a, [(OWN, features)])
    near = after(near, total, w_there, cot_there)
    two = swapped(near, "dom")
    total = forward("agg_near", who, a, [(NEAR, near)], total)
    far = after(far, total)
    give = forward("agg_give", who, a, [(FAR, far), (TWO, two)], total, 1)
    there = swapped(give, "feat")
    keep = forward("agg_keep", who, a, [(FAR, far), (TWO, after(two, give))], total, 0)

    act_here, act_there, grad_here, grad_there, g_give = middle(
        who, keep, there, weight, w_there, cotangent, cot_there
    )
    g_there = swapped(g_give, "feat")
    scale = 1.0 / math.sqrt(rows * parts)
    w_give = weight_term("weight_give", who, scale, 1, keep, there, grad_here, grad_there)
    w_keep = weight_term(
        "weight_keep", who, scale, 0, after(keep, w_give[0]), there, grad_here, grad_there
    )
    quick = parts == 16
    steps = weight_sum(who, w_keep, w_give, quick)

    last = next(steps)(grad_here)
    last = next(steps)(last)
    g_here = call(
        "keep",
        keep_kernel,
        who,
        [weight, w_there, after(grad_here, last), grad_there],
        [(keep.shape, F32)],
        flops=12 * rows // 2 * width * hidden,
    )[0]
    firsts = backward("back_here", who, t, [TWO, FAR, NEAR, OWN], after(g_here, last), [], 0)
    last = next(steps)(firsts[0])
    g_there = after(g_there, last)
    last = backward("back_two", who, t, [TWO], g_there, [firsts[0]], 1)[0]
    two = swapped(last, "dom")
    last = backward("back_far", who, t, [FAR], after(g_there, last), [firsts[1]], 1)[0]
    far = moved(last, "dom", -3, -1)
    last = backward("back_near", who, t, [NEAR], after(g_there, last), [firsts[2], two], 1)[0]
    near = moved(last, "dom", -1, -3)
    last = next(steps)(last)
    act_got = swapped(after(act_there, last), "feat")
    mine = backward("back_own", who, t, [OWN], after(g_there, last), [firsts[3]], 1)[0]
    last = next(steps)(mine, far)
    last = next(steps)(last)
    activated = join("activated", who, SIDE, [after(act_here, last), act_got], jax.ShapeDtypeStruct)
    last = next(steps)(activated)
    feature_grad = call(
        "feature_grad",
        add_kernel,
        who,
        [after(mine, last), far, near],
        [(features.shape, F32)],
        place=jax.ShapeDtypeStruct,
    )[0]
    weight_grad = next(steps)(feature_grad)
    return (activated, feature_grad, weight_grad)


def weight_sum(who, keep, give, quick):
    if not quick:
        here, there = (join("core_join", who, CORE, pair) for pair in zip(keep, give))
        total = lax.psum(here + swapped(there, "feat"), "dom")
        for _ in range(7):
            yield lambda *last: last[0]
        yield lambda *last: total
        return
    box = []

    def step(run):
        def go(*last):
            box.append(run(*last))
            return box[-1][0] if isinstance(box[-1], (list, tuple)) else box[-1]

        return go

    def up(value):
        return chosen(value, "dom", lambda i: i + 2 if i % 4 < 2 else None)

    gots = [swapped(value, "dom") for value in give]
    yield step(lambda *last: add("core_there", who, after(keep[1], *last), gots[1]))
    there = box[-1]
    yield step(lambda *last: add("core_here", who, after(keep[0], *last), gots[0]))
    here = box[-1]
    got = up(there)
    yield step(lambda *last: add("chip_there", who, after(there, *last), got))
    got = swapped(box[-1], "feat")
    also = up(here)
    yield step(lambda *last: side_sum("side_sum", who, after(here, *last), also, got)[::-1])
    give, keep = box[-1]
    for name, bit in (("layer_sum", 4), ("pair_sum", 8)):
        got = chosen(give, "dom", lambda i: i ^ bit if i % 4 >= 2 else None)
        yield step(lambda *last: add(name, who, after(keep, *last), got))
        keep = give = box[-1]
    ready_sent = chosen(keep, "dom", lambda i: i - 2 if i % 4 >= 2 else None)
    later = chosen(keep, "dom", lambda i: i ^ 4 if i % 4 >= 2 else None)
    later_sent = chosen(after(later, ready_sent), "dom", lambda i: i - 2 if i % 4 >= 2 else None)
    yield step(
        lambda *last: pick("chip_pick", who, after(keep, *last), later, ready_sent, later_sent)
    )
    got = swapped(box[-1], "dom")
    yield step(
        lambda *last: join("weight_grad", who, CORE, [after(box[-1], *last), got], jax.ShapeDtypeStruct)
    )


def solution(mesh):
    in_specs = (
        P("dom", "feat"),
        P(None, "feat"),
        P("dom", "feat"),
        P("dom", None, None),
        P("dom", None, None),
        P("dom", None),
        P("dom", None, None, None, None),
    )
    out_specs = (P("dom", "feat"), P("dom", "feat"), P(None, "feat"))
    return jax.shard_map(body, mesh=mesh, in_specs=in_specs, out_specs=out_specs, check_vma=False)
```

```python
import functools
import math

import jax
import jax.numpy as jnp
from jax import lax
from jax.experimental import pallas as pl
from jax.experimental.pallas import tpu as pltpu
from jax.sharding import PartitionSpec as P

F32 = jnp.float32
BF16 = jnp.bfloat16
TILE = 256
LIMIT = 8 * 1024 * 1024
IN_VMEM = pl.BlockSpec(memory_space=pltpu.VMEM)
IN_SMEM = pl.BlockSpec(memory_space=pltpu.SMEM)

SIDE, CORE, NEAR, FAR, TWO, OWN, CHIP, LAYER = range(8)


def split(value):
    high = value.astype(BF16)
    low = (value - high.astype(F32)).astype(BF16)
    return high, low


def mm(a, b, dims=((1,), (0,))):
    return lax.dot_general(a, b, (dims, ((), ())), preferred_element_type=F32)


def mm3(a, b, dims=((1,), (0,))):
    (ah, al), (bh, bl) = a, b
    return mm(ah, bh, dims) + (mm(ah, bl, dims) + mm(al, bh, dims))


def call(name, kernel, who, operands, shapes, scratch=(), flops=0, place=pltpu.VMEM):
    moved = sum(a.size * a.dtype.itemsize for a in operands)
    pinned = [pltpu.with_memory_space_constraint(a, pltpu.VMEM) for a in operands]
    return pl.pallas_call(
        kernel,
        in_specs=[IN_SMEM] + [IN_VMEM] * len(operands),
        out_specs=[IN_VMEM] * len(shapes),
        out_shape=[place(*shape) for shape in shapes],
        scratch_shapes=list(scratch),
        compiler_params=pltpu.CompilerParams(vmem_limit_bytes=LIMIT),
        cost_estimate=pl.CostEstimate(flops=int(flops), bytes_accessed=moved, transcendentals=0),
        name=name,
    )(who, *pinned)


def lay_out_kernel(turn, first, step, rows, cols, counts, who, blocks, out, mark):
    here = pl.program_id(0)
    slot = first + step * here
    cap = blocks.shape[1]
    size = blocks.shape[2]
    for part in range(2):
        out[part, here] = jnp.zeros(out.shape[2:], out.dtype)

    def one(k, carry):
        r = pl.multiple_of(rows[slot, k] * size, size)
        c = pl.multiple_of(cols[slot, k] * size, size)
        block = blocks[0, k]
        if turn:
            block, r, c = block.T, c, r
        for part, value in enumerate(split(block)):
            out[part, here, pl.ds(r, size), pl.ds(c, size)] = value
        return carry

    lax.fori_loop(0, jnp.minimum(counts[0, slot], cap), one, 0)
    mark[...] = jnp.full(mark.shape, who[SIDE].astype(F32))


def lay_out(name, who, turn, slots, rows, cols, counts, blocks, size_all):
    cap, size = blocks.shape[1:3]
    first, step = slots[0], slots[1] - slots[0]
    return pl.pallas_call(
        functools.partial(lay_out_kernel, turn, first, step),
        grid_spec=pltpu.PrefetchScalarGridSpec(
            num_scalar_prefetch=4,
            grid=(len(slots),),
            in_specs=[
                pl.BlockSpec((1, cap, size, size), lambda s, *_: (first + step * s, 0, 0, 0))
            ],
            out_specs=[IN_VMEM] * 2,
        ),
        out_shape=[
            pltpu.VMEM((2, len(slots), size_all, size_all), BF16),
            pltpu.VMEM((8, 128), F32),
        ],
        compiler_params=pltpu.CompilerParams(vmem_limit_bytes=LIMIT),
        cost_estimate=pl.CostEstimate(flops=0, bytes_accessed=20_000_000, transcendentals=0),
        name=name,
    )(rows, cols, counts, who, pltpu.with_memory_space_constraint(blocks, pltpu.HBM))


def forward_kernel(slots, part, has_base, who, matrix, *refs):
    n = len(slots)
    sources, refs = refs[:n], refs[n:]
    base, refs = (refs[0], refs[1:]) if has_base else (None, refs)
    out, (highs, lows) = refs[0], refs[1:]
    rows = out.shape[0]
    from_row = 0 if part is None else (who[SIDE] ^ part) * rows
    for i, source in enumerate(sources):
        highs[i], lows[i] = split(source[...])

    def tile(k, carry):
        there = pl.ds(pl.multiple_of(k * TILE, TILE), TILE)
        here = pl.ds(pl.multiple_of(from_row + k * TILE, TILE), TILE)
        total = None
        if base is not None:
            total = base[here if base.shape[0] > rows else there, :]
        for i, slot in enumerate(slots):
            at = who[slot]
            term = mm3((matrix[0, at, here, :], matrix[1, at, here, :]), (highs[i], lows[i]))
            total = term if total is None else total + term
        out[there, :] = total
        return carry

    lax.fori_loop(0, rows // TILE, tile, 0)


def forward(name, who, matrix, terms, base=None, part=None):
    slots = [slot for slot, _ in terms]
    sources = [source for _, source in terms]
    depth, width = sources[0].shape
    rows = matrix.shape[2] // (1 if part is None else 2)
    extra = [] if base is None else [base]
    return call(
        name,
        functools.partial(forward_kernel, slots, part, base is not None),
        who,
        [matrix, *sources, *extra],
        [((rows, width), F32)],
        [pltpu.VMEM((len(terms), depth, width), BF16)] * 2,
        6 * len(terms) * rows * depth * width,
    )[0]


def backward_kernel(slots, part, n_add, who, even, uneven, source, *refs):
    addends, outs = refs[:n_add], refs[-len(slots) :]
    depth = source.shape[0]
    parts = split(source[...])
    deep = pl.ds(pl.multiple_of((who[SIDE] ^ part) * depth, depth), depth)
    for slot, out in zip(slots, outs):
        matrix = uneven if slot in (NEAR, FAR) else even
        at = who[slot] >> 1
        total = mm3((matrix[0, at, :, deep], matrix[1, at, :, deep]), parts)
        for addend in addends:
            total = total + addend[...]
        out[...] = total


def backward(name, who, matrices, slots, source, addends, part, *marks):
    depth, width = source.shape
    rows = matrices[0].shape[2]
    return call(
        name,
        functools.partial(backward_kernel, slots, part, len(addends)),
        who,
        [*matrices, source, *addends, *marks],
        [((rows, width), F32)] * len(slots),
        flops=6 * len(slots) * rows * depth * width,
    )


def middle_kernel(who, own, far, w_here, w_there, cot, cot_there, *outs):
    act_here, act_there, grad_here, grad_there, g_there = outs
    half = own.shape[1]

    def rows_of(w, which):
        return split(w[pl.ds(pl.multiple_of((who[SIDE] ^ which) * half, half), half), :])

    rows = own.shape[0]
    cot_here = cot.at[pl.ds(pl.multiple_of(who[SIDE] * rows, rows), rows), :]
    source = split(own[...]), split(far[...])
    total = None
    for w, cot, act, grad in (
        (w_here, cot_here, act_here, grad_here),
        (w_there, cot_there, act_there, grad_there),
    ):
        pre = mm3(source[0], rows_of(w, 0)) + mm3(source[1], rows_of(w, 1))
        s = 1.0 / (1.0 + jnp.exp(-pre))
        act[...] = pre * s
        pg = cot[...] * (s + pre * s * (1.0 - s))
        grad[...] = pg
        term = mm3(split(pg), rows_of(w, 1), ((1,), (1,)))
        total = term if total is None else total + term
    g_there[...] = total


def middle(who, own, far, w_here, w_there, cot, cot_there):
    shape = (cot_there.shape, F32)
    flops = 36 * own.shape[0] * own.shape[1] * w_here.shape[1]
    operands = [own, far, w_here, w_there, cot, cot_there]
    return call("middle", middle_kernel, who, operands, [shape] * 5, flops=flops)


def keep_kernel(who, w_here, w_there, grad_here, grad_there, g_here):
    half = g_here.shape[1]
    at = pl.ds(pl.multiple_of(who[SIDE] * half, half), half)
    total = None
    for w, grad in ((w_here, grad_here), (w_there, grad_there)):
        term = mm3(split(grad[...]), split(w[at, :]), ((1,), (1,)))
        total = term if total is None else total + term
    g_here[...] = total


def weight_kernel(scale, which, who, own, far, grad_here, grad_there, here, there):
    mine = who[SIDE] == (who[CORE] ^ which)
    turned = split(jnp.where(mine, own[...], far[...]).T)
    for grad, out in ((grad_here, here), (grad_there, there)):
        out[...] = mm3(turned, split(grad[...])) * scale


def weight_term(name, who, scale, which, own, far, grad_here, grad_there):
    rows, half = own.shape
    hidden = grad_here.shape[1]
    return call(
        name,
        functools.partial(weight_kernel, scale, which),
        who,
        [own, far, grad_here, grad_there],
        [((half, hidden), F32)] * 2,
        flops=12 * rows * half * hidden,
    )


def half_kernel(which, who, whole, out):
    rows = out.shape[0]
    out[...] = whole[pl.ds(pl.multiple_of((who[SIDE] ^ which) * rows, rows), rows), :]


def join_kernel(place, who, *refs):
    parts, out = refs[:-1], refs[-1]
    rows = parts[0].shape[0]
    for k, part in enumerate(parts):
        out[pl.ds(pl.multiple_of((who[place] ^ k) * rows, rows), rows), :] = part[...]


def join(name, who, place, parts, kind=pltpu.VMEM):
    rows, cols = parts[0].shape
    shape = (rows * len(parts), cols)
    return call(
        name, functools.partial(join_kernel, place), who, parts, [(shape, F32)], place=kind
    )[0]


def pick_kernel(who, ready, later, ready_sent, later_sent, out):
    rows = ready.shape[0]
    odd = who[CHIP] == 1
    for which, one, other in ((0, ready, ready_sent), (1, later, later_sent)):
        at = pl.ds(pl.multiple_of((who[LAYER] ^ which) * rows, rows), rows)
        out[at, :] = jnp.where(odd, one[...], other[...])


def pick(name, who, *parts):
    rows, cols = parts[0].shape
    return call(name, pick_kernel, who, parts, [((2 * rows, cols), F32)])[0]


def hand_out(full, outs, place):
    rows = outs[0].shape[0]
    for k, out in enumerate(outs):
        out[...] = full[pl.ds(pl.multiple_of((place ^ k) * rows, rows), rows), :]


def side_kernel(who, one, two, three, keep, give, full):
    full[...] = one[...] + two[...] + three[...]
    hand_out(full, (keep, give), who[LAYER])


def side_sum(name, who, *parts):
    rows, cols = parts[0].shape
    shape = ((rows // 2, cols), F32)
    return call(name, side_kernel, who, parts, [shape] * 2, [pltpu.VMEM((rows, cols), F32)])


def near_kernel(who, straight, relayed, crossed, _, out):
    last = who[CHIP] * who[CORE] == 1
    out[...] = jnp.where(last, crossed[...], straight[...] + relayed[...])


def add_kernel(who, *refs):
    total = refs[0][...]
    for ref in refs[1:-1]:
        total = total + ref[...]
    refs[-1][...] = total


def add(name, who, *parts):
    return call(name, add_kernel, who, parts, [(parts[0].shape, F32)])[0]


def moved(value, axis, even, odd):
    peers = lax.axis_size(axis)
    perm = [(i, (i + (odd if i % 2 else even)) % peers) for i in range(peers)]
    return lax.ppermute(value, axis, perm)


def chosen(value, axis, target):
    peers = lax.axis_size(axis)
    pairs = [(i, target(i)) for i in range(peers)]
    return lax.ppermute(value, axis, [pair for pair in pairs if pair[1] is not None])


def swapped(value, axis):
    return chosen(value, axis, lambda i: i ^ 1)


def after(value, *others):
    return lax.optimization_barrier((value, *others))[0]


def body(features, weight, cotangent, block_rows, block_cols, block_counts, block_values):
    rows, width = features.shape
    hidden = weight.shape[1]
    depth = weight.shape[0]
    parts = lax.axis_size("dom")
    side = lax.axis_index("feat").astype(jnp.int32)
    place = lax.axis_index("dom").astype(jnp.int32)
    odd = place & 1
    zero = place * 0
    who = jnp.stack([side, odd, 1 + 2 * odd, 3 - 2 * odd, zero + 2, zero, (place >> 1) & 1,
                     (place >> 2) & 1])

    far = moved(features, "dom", 1, 3)
    near_a = chosen(features, "dom", lambda i: ((i + 3) % parts, None, i - 1, None)[i % 4])
    w_there = swapped(weight, "feat")
    places = block_rows[0], block_cols[0], block_counts
    blocks = block_values[0]
    a, ready = lay_out("lay_out", who, False, range(blocks.shape[0]), *places, blocks, rows)
    relay = chosen(
        after(near_a, far, w_there, ready), "dom", lambda i: (i + 4) % parts if i % 4 == 1 else None
    )
    near_b = chosen(
        after(features, near_a), "dom", lambda i: (i + 1) % parts if i % 2 else None
    )
    half_shape = ((rows // 2, hidden), F32)
    cot_give = call("cot_give", functools.partial(half_kernel, 1), who, [cotangent], [half_shape])[0]
    cot_there = swapped(cot_give, "feat")

    total = forward("agg_far", who, a, [(OWN, features), (FAR, far)])
    t_even, mark_even = lay_out(
        "lay_out_even", who, True, (0, 2), after(places[0], total), *places[1:], blocks, rows
    )
    near = call(
        "near",
        near_kernel,
        who,
        [after(near_b, total, cot_there, mark_even), relay, near_a, ready],
        [(features.shape, F32)],
    )[0]
    two = swapped(near, "dom")
    total = forward("agg_near", who, a, [(NEAR, near)], total)
    give = forward("agg_give", who, a, [(TWO, two)], total, 1)
    there = swapped(give, "feat")
    keep = forward("agg_keep", who, a, [(TWO, after(two, give))], total, 0)
    t_uneven, mark_uneven = lay_out(
        "lay_out_uneven", who, True, (1, 3), after(places[0], give), *places[1:], blocks, rows
    )
    t = t_even, t_uneven
    there = after(there, keep, mark_uneven)

    act_here, act_there, grad_here, grad_there, g_give = middle(
        who, keep, there, weight, w_there, cotangent, cot_there
    )
    g_there = swapped(g_give, "feat")
    scale = 1.0 / math.sqrt(rows * parts)
    w_give = weight_term("weight_give", who, scale, 1, keep, there, grad_here, grad_there)
    w_keep = weight_term(
        "weight_keep", who, scale, 0, after(keep, w_give[0]), there, grad_here, grad_there
    )
    quick = parts == 16
    steps = weight_sum(who, w_keep, w_give, quick)

    last = next(steps)(grad_here)
    last = next(steps)(last)
    g_here = call(
        "keep",
        keep_kernel,
        who,
        [weight, w_there, after(grad_here, last), grad_there],
        [(keep.shape, F32)],
        flops=12 * rows // 2 * width * hidden,
    )[0]
    firsts = backward("back_here", who, t, [TWO, FAR, NEAR, OWN], after(g_here, last), [], 0, mark_even, mark_uneven)
    last = next(steps)(firsts[0])
    g_there = after(g_there, last)
    last = backward("back_two", who, t, [TWO], g_there, [firsts[0]], 1)[0]
    two = swapped(last, "dom")
    last = backward("back_far", who, t, [FAR], after(g_there, last), [firsts[1]], 1)[0]
    far = moved(last, "dom", -3, -1)
    last = backward("back_near", who, t, [NEAR], after(g_there, last), [firsts[2], two], 1)[0]
    near = moved(last, "dom", -1, -3)
    last = next(steps)(last)
    act_got = swapped(after(act_there, last), "feat")
    mine = backward("back_own", who, t, [OWN], after(g_there, last), [firsts[3]], 1)[0]
    last = next(steps)(mine, far)
    last = next(steps)(last)
    activated = join("activated", who, SIDE, [after(act_here, last), act_got], jax.ShapeDtypeStruct)
    last = next(steps)(activated)
    feature_grad = call(
        "feature_grad",
        add_kernel,
        who,
        [after(mine, last), far, near],
        [(features.shape, F32)],
        place=jax.ShapeDtypeStruct,
    )[0]
    weight_grad = next(steps)(feature_grad)
    return (activated, feature_grad, weight_grad)


def weight_sum(who, keep, give, quick):
    if not quick:
        here, there = (join("core_join", who, CORE, pair) for pair in zip(keep, give))
        total = lax.psum(here + swapped(there, "feat"), "dom")
        for _ in range(7):
            yield lambda *last: last[0]
        yield lambda *last: total
        return
    box = []

    def step(run):
        def go(*last):
            box.append(run(*last))
            return box[-1][0] if isinstance(box[-1], (list, tuple)) else box[-1]

        return go

    def up(value):
        return chosen(value, "dom", lambda i: i + 2 if i % 4 < 2 else None)

    gots = [swapped(value, "dom") for value in give]
    yield step(lambda *last: add("core_there", who, after(keep[1], *last), gots[1]))
    there = box[-1]
    yield step(lambda *last: add("core_here", who, after(keep[0], *last), gots[0]))
    here = box[-1]
    got = up(there)
    yield step(lambda *last: add("chip_there", who, after(there, *last), got))
    got = swapped(box[-1], "feat")
    also = up(here)
    yield step(lambda *last: side_sum("side_sum", who, after(here, *last), also, got)[::-1])
    give, keep = box[-1]
    for name, bit in (("layer_sum", 4), ("pair_sum", 8)):
        got = chosen(give, "dom", lambda i: i ^ bit if i % 4 >= 2 else None)
        yield step(lambda *last: add(name, who, after(keep, *last), got))
        keep = give = box[-1]
    ready_sent = chosen(keep, "dom", lambda i: i - 2 if i % 4 >= 2 else None)
    later = chosen(keep, "dom", lambda i: i ^ 4 if i % 4 >= 2 else None)
    later_sent = chosen(after(later, ready_sent), "dom", lambda i: i - 2 if i % 4 >= 2 else None)
    yield step(
        lambda *last: pick("chip_pick", who, after(keep, *last), later, ready_sent, later_sent)
    )
    got = swapped(box[-1], "dom")
    yield step(
        lambda *last: join("weight_grad", who, CORE, [after(box[-1], *last), got], jax.ShapeDtypeStruct)
    )


def solution(mesh):
    in_specs = (
        P("dom", "feat"),
        P(None, "feat"),
        P("dom", "feat"),
        P("dom", None, None),
        P("dom", None, None),
        P("dom", None),
        P("dom", None, None, None, None),
    )
    out_specs = (P("dom", "feat"), P("dom", "feat"), P(None, "feat"))
    return jax.shard_map(body, mesh=mesh, in_specs=in_specs, out_specs=out_specs, check_vma=False)
```

```python
import functools
import math

import jax
import jax.numpy as jnp
from jax import lax
from jax.experimental import pallas as pl
from jax.experimental.pallas import tpu as pltpu
from jax.sharding import PartitionSpec as P

F32 = jnp.float32
BF16 = jnp.bfloat16
TILE = 256
LIMIT = 8 * 1024 * 1024
IN_VMEM = pl.BlockSpec(memory_space=pltpu.VMEM)
IN_SMEM = pl.BlockSpec(memory_space=pltpu.SMEM)

SIDE, CORE, NEAR, FAR, TWO, OWN, CHIP, LAYER = range(8)


def split(value):
    high = value.astype(BF16)
    low = (value - high.astype(F32)).astype(BF16)
    return high, low


def mm(a, b, dims=((1,), (0,))):
    return lax.dot_general(a, b, (dims, ((), ())), preferred_element_type=F32)


def mm3(a, b, dims=((1,), (0,))):
    (ah, al), (bh, bl) = a, b
    return mm(ah, bh, dims) + (mm(ah, bl, dims) + mm(al, bh, dims))


def call(name, kernel, who, operands, shapes, scratch=(), flops=0, place=pltpu.VMEM):
    moved = sum(a.size * a.dtype.itemsize for a in operands)
    pinned = [pltpu.with_memory_space_constraint(a, pltpu.VMEM) for a in operands]
    return pl.pallas_call(
        kernel,
        in_specs=[IN_SMEM] + [IN_VMEM] * len(operands),
        out_specs=[IN_VMEM] * len(shapes),
        out_shape=[place(*shape) for shape in shapes],
        scratch_shapes=list(scratch),
        compiler_params=pltpu.CompilerParams(vmem_limit_bytes=LIMIT),
        cost_estimate=pl.CostEstimate(flops=int(flops), bytes_accessed=moved, transcendentals=0),
        name=name,
    )(who, *pinned)


def lay_out_kernel(rows, cols, counts, who, blocks, a, t):
    slot = pl.program_id(0)
    cap = blocks.shape[1]
    size = blocks.shape[2]
    for out in (a, t):
        for part in range(2):
            out[part, slot] = jnp.zeros(out.shape[2:], out.dtype)

    def one(k, carry):
        r = pl.multiple_of(rows[slot, k] * size, size)
        c = pl.multiple_of(cols[slot, k] * size, size)
        block = blocks[0, k]
        for part, value in enumerate(split(block)):
            a[part, slot, pl.ds(r, size), pl.ds(c, size)] = value
        for part, value in enumerate(split(block.T)):
            t[part, slot, pl.ds(c, size), pl.ds(r, size)] = value
        return carry

    lax.fori_loop(0, jnp.minimum(counts[0, slot], cap), one, 0)


def lay_out(rows, cols, counts, who, blocks, size_all):
    window, cap, size, _ = blocks.shape
    shape = pltpu.VMEM((2, window, size_all, size_all), BF16)
    return pl.pallas_call(
        lay_out_kernel,
        grid_spec=pltpu.PrefetchScalarGridSpec(
            num_scalar_prefetch=4,
            grid=(window,),
            in_specs=[pl.BlockSpec((1, cap, size, size), lambda s, *_: (s, 0, 0, 0))],
            out_specs=[IN_VMEM] * 2,
        ),
        out_shape=[shape] * 2,
        compiler_params=pltpu.CompilerParams(vmem_limit_bytes=LIMIT),
        cost_estimate=pl.CostEstimate(flops=0, bytes_accessed=20_000_000, transcendentals=0),
        name="lay_out",
    )(rows, cols, counts, who, pltpu.with_memory_space_constraint(blocks, pltpu.HBM))


def forward_kernel(slots, part, has_base, who, matrix, *refs):
    n = len(slots)
    sources, refs = refs[:n], refs[n:]
    base, refs = (refs[0], refs[1:]) if has_base else (None, refs)
    out, (highs, lows) = refs[0], refs[1:]
    rows = out.shape[0]
    from_row = 0 if part is None else (who[SIDE] ^ part) * rows
    for i, source in enumerate(sources):
        highs[i], lows[i] = split(source[...])

    def tile(k, carry):
        there = pl.ds(pl.multiple_of(k * TILE, TILE), TILE)
        here = pl.ds(pl.multiple_of(from_row + k * TILE, TILE), TILE)
        total = None
        if base is not None:
            total = base[here if base.shape[0] > rows else there, :]
        for i, slot in enumerate(slots):
            at = who[slot]
            term = mm3((matrix[0, at, here, :], matrix[1, at, here, :]), (highs[i], lows[i]))
            total = term if total is None else total + term
        out[there, :] = total
        return carry

    lax.fori_loop(0, rows // TILE, tile, 0)


def forward(name, who, matrix, terms, base=None, part=None):
    slots = [slot for slot, _ in terms]
    sources = [source for _, source in terms]
    depth, width = sources[0].shape
    rows = matrix.shape[2] // (1 if part is None else 2)
    extra = [] if base is None else [base]
    return call(
        name,
        functools.partial(forward_kernel, slots, part, base is not None),
        who,
        [matrix, *sources, *extra],
        [((rows, width), F32)],
        [pltpu.VMEM((len(terms), depth, width), BF16)] * 2,
        6 * len(terms) * rows * depth * width,
    )[0]


def backward_kernel(slots, part, n_add, first, pieces, who, matrix, source, *refs):
    addends, outs = refs[:n_add], refs[n_add:]
    depth = source.shape[0]
    parts = split(source[...])
    deep = pl.ds(pl.multiple_of((who[SIDE] ^ part) * depth, depth), depth)
    size = outs[0].shape[0]
    here = pl.ds(first, size * pieces)
    for i, slot in enumerate(slots):
        at = who[slot]
        total = mm3((matrix[0, at, here, deep], matrix[1, at, here, deep]), parts)
        for addend in addends:
            total = total + addend[here, :]
        for k in range(pieces):
            outs[i * pieces + k][...] = total[k * size : (k + 1) * size, :]


def backward(name, who, matrix, slots, source, addends, part, first=0, rows=None, pieces=1):
    depth, width = source.shape
    rows = rows or matrix.shape[2]
    return call(
        name,
        functools.partial(backward_kernel, slots, part, len(addends), first, pieces),
        who,
        [matrix, source, *addends],
        [((rows // pieces, width), F32)] * (len(slots) * pieces),
        flops=6 * len(slots) * rows * depth * width,
    )


def middle_kernel(who, own, far, w_here, w_there, cot, cot_there, *outs):
    act_here, act_there, grad_here, grad_there, g_there = outs
    half = own.shape[1]

    def rows_of(w, which):
        return split(w[pl.ds(pl.multiple_of((who[SIDE] ^ which) * half, half), half), :])

    rows = own.shape[0]
    cot_here = cot.at[pl.ds(pl.multiple_of(who[SIDE] * rows, rows), rows), :]
    source = split(own[...]), split(far[...])
    total = None
    for w, cot, act, grad in (
        (w_here, cot_here, act_here, grad_here),
        (w_there, cot_there, act_there, grad_there),
    ):
        pre = mm3(source[0], rows_of(w, 0)) + mm3(source[1], rows_of(w, 1))
        s = 1.0 / (1.0 + jnp.exp(-pre))
        act[...] = pre * s
        pg = cot[...] * (s + pre * s * (1.0 - s))
        grad[...] = pg
        term = mm3(split(pg), rows_of(w, 1), ((1,), (1,)))
        total = term if total is None else total + term
    g_there[...] = total


def middle(who, own, far, w_here, w_there, cot, cot_there):
    shape = (cot_there.shape, F32)
    flops = 36 * own.shape[0] * own.shape[1] * w_here.shape[1]
    operands = [own, far, w_here, w_there, cot, cot_there]
    return call("middle", middle_kernel, who, operands, [shape] * 5, flops=flops)


def keep_kernel(who, w_here, w_there, grad_here, grad_there, g_here):
    half = g_here.shape[1]
    at = pl.ds(pl.multiple_of(who[SIDE] * half, half), half)
    total = None
    for w, grad in ((w_here, grad_here), (w_there, grad_there)):
        term = mm3(split(grad[...]), split(w[at, :]), ((1,), (1,)))
        total = term if total is None else total + term
    g_here[...] = total


def weight_kernel(scale, which, who, own, far, grad_here, grad_there, here, there):
    mine = who[SIDE] == (who[CORE] ^ which)
    turned = split(jnp.where(mine, own[...], far[...]).T)
    for grad, out in ((grad_here, here), (grad_there, there)):
        out[...] = mm3(turned, split(grad[...])) * scale


def weight_term(name, who, scale, which, own, far, grad_here, grad_there):
    rows, half = own.shape
    hidden = grad_here.shape[1]
    return call(
        name,
        functools.partial(weight_kernel, scale, which),
        who,
        [own, far, grad_here, grad_there],
        [((half, hidden), F32)] * 2,
        flops=12 * rows * half * hidden,
    )


def half_kernel(which, who, whole, out):
    rows = out.shape[0]
    out[...] = whole[pl.ds(pl.multiple_of((who[SIDE] ^ which) * rows, rows), rows), :]


def join_kernel(place, who, *refs):
    parts, out = refs[:-1], refs[-1]
    rows = parts[0].shape[0]
    for k, part in enumerate(parts):
        out[pl.ds(pl.multiple_of((who[place] ^ k) * rows, rows), rows), :] = part[...]


def join(name, who, place, parts, kind=pltpu.VMEM):
    rows, cols = parts[0].shape
    shape = (rows * len(parts), cols)
    return call(
        name, functools.partial(join_kernel, place), who, parts, [(shape, F32)], place=kind
    )[0]


def pick_kernel(who, ready, later, ready_sent, later_sent, out):
    rows = ready.shape[0]
    odd = who[CHIP] == 1
    for which, one, other in ((0, ready, ready_sent), (1, later, later_sent)):
        at = pl.ds(pl.multiple_of((who[LAYER] ^ which) * rows, rows), rows)
        out[at, :] = jnp.where(odd, one[...], other[...])


def pick(name, who, *parts):
    rows, cols = parts[0].shape
    return call(name, pick_kernel, who, parts, [((2 * rows, cols), F32)])[0]


def hand_out(full, outs, place):
    rows = outs[0].shape[0]
    for k, out in enumerate(outs):
        out[...] = full[pl.ds(pl.multiple_of((place ^ k) * rows, rows), rows), :]


def side_kernel(who, one, two, three, keep, give, full):
    full[...] = one[...] + two[...] + three[...]
    hand_out(full, (keep, give), who[LAYER])


def side_sum(name, who, *parts):
    rows, cols = parts[0].shape
    shape = ((rows // 2, cols), F32)
    return call(name, side_kernel, who, parts, [shape] * 2, [pltpu.VMEM((rows, cols), F32)])


def add_kernel(who, *refs):
    total = refs[0][...]
    for ref in refs[1:-1]:
        total = total + ref[...]
    refs[-1][...] = total


def add(name, who, *parts):
    return call(name, add_kernel, who, parts, [(parts[0].shape, F32)])[0]


def moved(value, axis, even, odd):
    peers = lax.axis_size(axis)
    perm = [(i, (i + (odd if i % 2 else even)) % peers) for i in range(peers)]
    return lax.ppermute(value, axis, perm)


def chosen(value, axis, target):
    peers = lax.axis_size(axis)
    pairs = [(i, target(i)) for i in range(peers)]
    return lax.ppermute(value, axis, [pair for pair in pairs if pair[1] is not None])


def swapped(value, axis):
    return chosen(value, axis, lambda i: i ^ 1)


def after(value, *others):
    return lax.optimization_barrier((value, *others))[0]


def body(features, weight, cotangent, block_rows, block_cols, block_counts, block_values):
    rows, width = features.shape
    hidden = weight.shape[1]
    depth = weight.shape[0]
    parts = lax.axis_size("dom")
    side = lax.axis_index("feat").astype(jnp.int32)
    place = lax.axis_index("dom").astype(jnp.int32)
    odd = place & 1
    zero = place * 0
    who = jnp.stack([side, odd, 1 + 2 * odd, 3 - 2 * odd, zero + 2, zero, (place >> 1) & 1,
                     (place >> 2) & 1])

    near = moved(features, "dom", 3, 1)
    far = moved(features, "dom", 1, 3)
    w_there = swapped(weight, "feat")
    half_shape = ((rows // 2, hidden), F32)
    cot_give = call("cot_give", functools.partial(half_kernel, 1), who, [cotangent], [half_shape])[0]
    cot_there = swapped(cot_give, "feat")

    a, t = lay_out(
        block_rows[0], block_cols[0], block_counts, who, block_values[0], rows
    )
    total = forward("agg_own", who, a, [(OWN, features)])
    near = after(near, total, w_there, cot_there)
    two = swapped(near, "dom")
    total = forward("agg_near", who, a, [(NEAR, near)], total)
    far = after(far, total)
    give = forward("agg_give", who, a, [(FAR, far), (TWO, two)], total, 1)
    there = swapped(give, "feat")
    keep = forward("agg_keep", who, a, [(FAR, far), (TWO, after(two, give))], total, 0)

    act_here, act_there, grad_here, grad_there, g_give = middle(
        who, keep, there, weight, w_there, cotangent, cot_there
    )
    g_there = swapped(g_give, "feat")
    scale = 1.0 / math.sqrt(rows * parts)
    w_give = weight_term("weight_give", who, scale, 1, keep, there, grad_here, grad_there)
    w_keep = weight_term(
        "weight_keep", who, scale, 0, after(keep, w_give[0]), there, grad_here, grad_there
    )
    quick = parts == 16
    steps = weight_sum(who, w_keep, w_give, quick)

    last = next(steps)(grad_here)
    last = next(steps)(last)
    g_here = call(
        "keep",
        keep_kernel,
        who,
        [weight, w_there, after(grad_here, last), grad_there],
        [(keep.shape, F32)],
        flops=12 * rows // 2 * width * hidden,
    )[0]
    firsts = backward("back_here", who, t, [TWO, FAR, NEAR, OWN], after(g_here, last), [], 0)
    last = next(steps)(firsts[0])
    g_there = after(g_there, last)
    last = backward("back_two", who, t, [TWO], g_there, [firsts[0]], 1)[0]
    two = swapped(last, "dom")
    last = backward("back_far", who, t, [FAR], after(g_there, last), [firsts[1]], 1)[0]
    far = moved(last, "dom", -3, -1)
    last = backward("back_near", who, t, [NEAR], after(g_there, last), [firsts[2], two], 1)[0]
    near = moved(last, "dom", -1, -3)
    last = next(steps)(last)
    act_got = swapped(after(act_there, last), "feat")
    mine = backward("back_own", who, t, [OWN], after(g_there, last), [firsts[3]], 1)[0]
    last = next(steps)(mine, far)
    last = next(steps)(last)
    activated = join("activated", who, SIDE, [after(act_here, last), act_got], jax.ShapeDtypeStruct)
    last = next(steps)(activated)
    feature_grad = call(
        "feature_grad",
        add_kernel,
        who,
        [after(mine, last), far, near],
        [(features.shape, F32)],
        place=jax.ShapeDtypeStruct,
    )[0]
    weight_grad = next(steps)(feature_grad)
    return (activated, feature_grad, weight_grad)


def weight_sum(who, keep, give, quick):
    if not quick:
        here, there = (join("core_join", who, CORE, pair) for pair in zip(keep, give))
        total = lax.psum(here + swapped(there, "feat"), "dom")
        for _ in range(7):
            yield lambda *last: last[0]
        yield lambda *last: total
        return
    box = []

    def step(run):
        def go(*last):
            box.append(run(*last))
            return box[-1][0] if isinstance(box[-1], (list, tuple)) else box[-1]

        return go

    def up(value):
        return chosen(value, "dom", lambda i: i + 2 if i % 4 < 2 else None)

    gots = [swapped(value, "dom") for value in give]
    yield step(lambda *last: add("core_there", who, after(keep[1], *last), gots[1]))
    there = box[-1]
    yield step(lambda *last: add("core_here", who, after(keep[0], *last), gots[0]))
    here = box[-1]
    got = up(there)
    yield step(lambda *last: add("chip_there", who, after(there, *last), got))
    got = swapped(box[-1], "feat")
    also = up(here)
    yield step(lambda *last: side_sum("side_sum", who, after(here, *last), also, got)[::-1])
    give, keep = box[-1]
    for name, bit in (("layer_sum", 4), ("pair_sum", 8)):
        got = chosen(give, "dom", lambda i: i ^ bit if i % 4 >= 2 else None)
        yield step(lambda *last: add(name, who, after(keep, *last), got))
        keep = give = box[-1]
    later_sent = chosen(keep, "dom", lambda i: (i ^ 4) - 2 if i % 4 >= 2 else None)
    later = chosen(keep, "dom", lambda i: i ^ 4 if i % 4 >= 2 else None)
    ready_sent = chosen(keep, "dom", lambda i: i - 2 if i % 4 >= 2 else None)
    yield step(
        lambda *last: pick("chip_pick", who, after(keep, *last), later, ready_sent, later_sent)
    )
    got = swapped(box[-1], "dom")
    yield step(
        lambda *last: join("weight_grad", who, CORE, [after(box[-1], *last), got], jax.ShapeDtypeStruct)
    )


def solution(mesh):
    in_specs = (
        P("dom", "feat"),
        P(None, "feat"),
        P("dom", "feat"),
        P("dom", None, None),
        P("dom", None, None),
        P("dom", None),
        P("dom", None, None, None, None),
    )
    out_specs = (P("dom", "feat"), P("dom", "feat"), P(None, "feat"))
    return jax.shard_map(body, mesh=mesh, in_specs=in_specs, out_specs=out_specs, check_vma=False)
```

```python
import functools
import math

import jax
import jax.numpy as jnp
from jax import lax
from jax.experimental import pallas as pl
from jax.experimental.pallas import tpu as pltpu
from jax.sharding import PartitionSpec as P

F32 = jnp.float32
BF16 = jnp.bfloat16
TILE = 256
LIMIT = 8 * 1024 * 1024
IN_VMEM = pl.BlockSpec(memory_space=pltpu.VMEM)
IN_SMEM = pl.BlockSpec(memory_space=pltpu.SMEM)

SIDE, CORE, NEAR, FAR, TWO, OWN, CHIP, LAYER = range(8)


def split(value):
    high = value.astype(BF16)
    low = (value - high.astype(F32)).astype(BF16)
    return high, low


def mm(a, b, dims=((1,), (0,))):
    return lax.dot_general(a, b, (dims, ((), ())), preferred_element_type=F32)


def mm3(a, b, dims=((1,), (0,))):
    (ah, al), (bh, bl) = a, b
    return mm(ah, bh, dims) + (mm(ah, bl, dims) + mm(al, bh, dims))


def call(name, kernel, who, operands, shapes, scratch=(), flops=0, place=pltpu.VMEM):
    moved = sum(a.size * a.dtype.itemsize for a in operands)
    pinned = [pltpu.with_memory_space_constraint(a, pltpu.VMEM) for a in operands]
    return pl.pallas_call(
        kernel,
        in_specs=[IN_SMEM] + [IN_VMEM] * len(operands),
        out_specs=[IN_VMEM] * len(shapes),
        out_shape=[place(*shape) for shape in shapes],
        scratch_shapes=list(scratch),
        compiler_params=pltpu.CompilerParams(vmem_limit_bytes=LIMIT),
        cost_estimate=pl.CostEstimate(flops=int(flops), bytes_accessed=moved, transcendentals=0),
        name=name,
    )(who, *pinned)


def lay_out_kernel(rows, cols, counts, who, blocks, a, t):
    slot = pl.program_id(0)
    cap = blocks.shape[1]
    size = blocks.shape[2]
    for out in (a, t):
        for part in range(2):
            out[part, slot] = jnp.zeros(out.shape[2:], out.dtype)

    def one(k, carry):
        r = pl.multiple_of(rows[slot, k] * size, size)
        c = pl.multiple_of(cols[slot, k] * size, size)
        block = blocks[0, k]
        for part, value in enumerate(split(block)):
            a[part, slot, pl.ds(r, size), pl.ds(c, size)] = value
        for part, value in enumerate(split(block.T)):
            t[part, slot, pl.ds(c, size), pl.ds(r, size)] = value
        return carry

    lax.fori_loop(0, jnp.minimum(counts[0, slot], cap), one, 0)


def lay_out(rows, cols, counts, who, blocks, size_all):
    window, cap, size, _ = blocks.shape
    shape = pltpu.VMEM((2, window, size_all, size_all), BF16)
    return pl.pallas_call(
        lay_out_kernel,
        grid_spec=pltpu.PrefetchScalarGridSpec(
            num_scalar_prefetch=4,
            grid=(window,),
            in_specs=[pl.BlockSpec((1, cap, size, size), lambda s, *_: (s, 0, 0, 0))],
            out_specs=[IN_VMEM] * 2,
        ),
        out_shape=[shape] * 2,
        compiler_params=pltpu.CompilerParams(vmem_limit_bytes=LIMIT),
        cost_estimate=pl.CostEstimate(flops=0, bytes_accessed=20_000_000, transcendentals=0),
        name="lay_out",
    )(rows, cols, counts, who, pltpu.with_memory_space_constraint(blocks, pltpu.HBM))


def forward_kernel(slots, part, has_base, who, matrix, *refs):
    n = len(slots)
    sources, refs = refs[:n], refs[n:]
    base, refs = (refs[0], refs[1:]) if has_base else (None, refs)
    out, (highs, lows) = refs[0], refs[1:]
    rows = out.shape[0]
    from_row = 0 if part is None else (who[SIDE] ^ part) * rows
    for i, source in enumerate(sources):
        highs[i], lows[i] = split(source[...])

    def tile(k, carry):
        there = pl.ds(pl.multiple_of(k * TILE, TILE), TILE)
        here = pl.ds(pl.multiple_of(from_row + k * TILE, TILE), TILE)
        total = None
        if base is not None:
            total = base[here if base.shape[0] > rows else there, :]
        for i, slot in enumerate(slots):
            at = who[slot]
            term = mm3((matrix[0, at, here, :], matrix[1, at, here, :]), (highs[i], lows[i]))
            total = term if total is None else total + term
        out[there, :] = total
        return carry

    lax.fori_loop(0, rows // TILE, tile, 0)


def forward(name, who, matrix, terms, base=None, part=None):
    slots = [slot for slot, _ in terms]
    sources = [source for _, source in terms]
    depth, width = sources[0].shape
    rows = matrix.shape[2] // (1 if part is None else 2)
    extra = [] if base is None else [base]
    return call(
        name,
        functools.partial(forward_kernel, slots, part, base is not None),
        who,
        [matrix, *sources, *extra],
        [((rows, width), F32)],
        [pltpu.VMEM((len(terms), depth, width), BF16)] * 2,
        6 * len(terms) * rows * depth * width,
    )[0]


def backward_kernel(slots, part, n_add, first, pieces, who, matrix, source, *refs):
    addends, outs = refs[:n_add], refs[n_add:]
    depth = source.shape[0]
    parts = split(source[...])
    deep = pl.ds(pl.multiple_of((who[SIDE] ^ part) * depth, depth), depth)
    size = outs[0].shape[0]
    here = pl.ds(first, size * pieces)
    for i, slot in enumerate(slots):
        at = who[slot]
        total = mm3((matrix[0, at, here, deep], matrix[1, at, here, deep]), parts)
        for addend in addends:
            total = total + addend[here, :]
        for k in range(pieces):
            outs[i * pieces + k][...] = total[k * size : (k + 1) * size, :]


def backward(name, who, matrix, slots, source, addends, part, first=0, rows=None, pieces=1):
    depth, width = source.shape
    rows = rows or matrix.shape[2]
    return call(
        name,
        functools.partial(backward_kernel, slots, part, len(addends), first, pieces),
        who,
        [matrix, source, *addends],
        [((rows // pieces, width), F32)] * (len(slots) * pieces),
        flops=6 * len(slots) * rows * depth * width,
    )


def middle_kernel(who, own, far, w_here, w_there, cot, cot_there, *outs):
    act_here, act_there, grad_here, grad_there, g_there = outs
    half = own.shape[1]

    def rows_of(w, which):
        return split(w[pl.ds(pl.multiple_of((who[SIDE] ^ which) * half, half), half), :])

    rows = own.shape[0]
    cot_here = cot.at[pl.ds(pl.multiple_of(who[SIDE] * rows, rows), rows), :]
    source = split(own[...]), split(far[...])
    total = None
    for w, cot, act, grad in (
        (w_here, cot_here, act_here, grad_here),
        (w_there, cot_there, act_there, grad_there),
    ):
        pre = mm3(source[0], rows_of(w, 0)) + mm3(source[1], rows_of(w, 1))
        s = 1.0 / (1.0 + jnp.exp(-pre))
        act[...] = pre * s
        pg = cot[...] * (s + pre * s * (1.0 - s))
        grad[...] = pg
        term = mm3(split(pg), rows_of(w, 1), ((1,), (1,)))
        total = term if total is None else total + term
    g_there[...] = total


def middle(who, own, far, w_here, w_there, cot, cot_there):
    shape = (cot_there.shape, F32)
    flops = 36 * own.shape[0] * own.shape[1] * w_here.shape[1]
    operands = [own, far, w_here, w_there, cot, cot_there]
    return call("middle", middle_kernel, who, operands, [shape] * 5, flops=flops)


def keep_kernel(who, w_here, w_there, grad_here, grad_there, g_here):
    half = g_here.shape[1]
    at = pl.ds(pl.multiple_of(who[SIDE] * half, half), half)
    total = None
    for w, grad in ((w_here, grad_here), (w_there, grad_there)):
        term = mm3(split(grad[...]), split(w[at, :]), ((1,), (1,)))
        total = term if total is None else total + term
    g_here[...] = total


def weight_kernel(scale, which, who, own, far, grad_here, grad_there, here, there):
    mine = who[SIDE] == (who[CORE] ^ which)
    turned = split(jnp.where(mine, own[...], far[...]).T)
    for grad, out in ((grad_here, here), (grad_there, there)):
        out[...] = mm3(turned, split(grad[...])) * scale


def weight_term(name, who, scale, which, own, far, grad_here, grad_there):
    rows, half = own.shape
    hidden = grad_here.shape[1]
    return call(
        name,
        functools.partial(weight_kernel, scale, which),
        who,
        [own, far, grad_here, grad_there],
        [((half, hidden), F32)] * 2,
        flops=12 * rows * half * hidden,
    )


def half_kernel(which, who, whole, out):
    rows = out.shape[0]
    out[...] = whole[pl.ds(pl.multiple_of((who[SIDE] ^ which) * rows, rows), rows), :]


def join_kernel(place, who, *refs):
    parts, out = refs[:-1], refs[-1]
    rows = parts[0].shape[0]
    for k, part in enumerate(parts):
        out[pl.ds(pl.multiple_of((who[place] ^ k) * rows, rows), rows), :] = part[...]


def join(name, who, place, parts, kind=pltpu.VMEM):
    rows, cols = parts[0].shape
    shape = (rows * len(parts), cols)
    return call(
        name, functools.partial(join_kernel, place), who, parts, [(shape, F32)], place=kind
    )[0]


def pick_kernel(who, ready, ready_sent, later, later_sent, out):
    rows = ready.shape[0]
    odd = who[CHIP] == 1
    for which, one, other in ((0, ready, ready_sent), (1, later, later_sent)):
        at = pl.ds(pl.multiple_of((who[LAYER] ^ which) * rows, rows), rows)
        out[at, :] = jnp.where(odd, one[...], other[...])


def pick(name, who, *parts):
    rows, cols = parts[0].shape
    return call(name, pick_kernel, who, parts, [((2 * rows, cols), F32)])[0]


def hand_out(full, outs, place):
    rows = outs[0].shape[0]
    for k, out in enumerate(outs):
        out[...] = full[pl.ds(pl.multiple_of((place ^ k) * rows, rows), rows), :]


def side_kernel(who, one, two, three, keep, give, full):
    full[...] = one[...] + two[...] + three[...]
    hand_out(full, (keep, give), who[LAYER])


def side_sum(name, who, *parts):
    rows, cols = parts[0].shape
    shape = ((rows // 2, cols), F32)
    return call(name, side_kernel, who, parts, [shape] * 2, [pltpu.VMEM((rows, cols), F32)])


def line_kernel(who, here, one, two, three, out):
    out[...] = (here[...] + one[...]) + (two[...] + three[...])


def line_sum(name, who, *parts):
    return call(name, line_kernel, who, parts, [(parts[0].shape, F32)])[0]


def add_kernel(who, *refs):
    total = refs[0][...]
    for ref in refs[1:-1]:
        total = total + ref[...]
    refs[-1][...] = total


def add(name, who, *parts):
    return call(name, add_kernel, who, parts, [(parts[0].shape, F32)])[0]


def moved(value, axis, even, odd):
    peers = lax.axis_size(axis)
    perm = [(i, (i + (odd if i % 2 else even)) % peers) for i in range(peers)]
    return lax.ppermute(value, axis, perm)


def chosen(value, axis, target):
    peers = lax.axis_size(axis)
    pairs = [(i, target(i)) for i in range(peers)]
    return lax.ppermute(value, axis, [pair for pair in pairs if pair[1] is not None])


def swapped(value, axis):
    return chosen(value, axis, lambda i: i ^ 1)


def after(value, *others):
    return lax.optimization_barrier((value, *others))[0]


def body(features, weight, cotangent, block_rows, block_cols, block_counts, block_values):
    rows, width = features.shape
    hidden = weight.shape[1]
    depth = weight.shape[0]
    parts = lax.axis_size("dom")
    side = lax.axis_index("feat").astype(jnp.int32)
    place = lax.axis_index("dom").astype(jnp.int32)
    odd = place & 1
    zero = place * 0
    who = jnp.stack([side, odd, 1 + 2 * odd, 3 - 2 * odd, zero + 2, zero, (place >> 1) & 1,
                     (place >> 2) & 1])

    near = moved(features, "dom", 3, 1)
    far = moved(features, "dom", 1, 3)
    w_there = swapped(weight, "feat")
    half_shape = ((rows // 2, hidden), F32)
    cot_give = call("cot_give", functools.partial(half_kernel, 1), who, [cotangent], [half_shape])[0]
    cot_there = swapped(cot_give, "feat")

    a, t = lay_out(
        block_rows[0], block_cols[0], block_counts, who, block_values[0], rows
    )
    total = forward("agg_own", who, a, [(OWN, features)])
    near = after(near, total, w_there, cot_there)
    two = swapped(near, "dom")
    total = forward("agg_near", who, a, [(NEAR, near)], total)
    far = after(far, total)
    give = forward("agg_give", who, a, [(FAR, far), (TWO, two)], total, 1)
    there = swapped(give, "feat")
    keep = forward("agg_keep", who, a, [(FAR, far), (TWO, after(two, give))], total, 0)

    act_here, act_there, grad_here, grad_there, g_give = middle(
        who, keep, there, weight, w_there, cotangent, cot_there
    )
    g_there = swapped(g_give, "feat")
    scale = 1.0 / math.sqrt(rows * parts)
    w_give = weight_term("weight_give", who, scale, 1, keep, there, grad_here, grad_there)
    w_keep = weight_term(
        "weight_keep", who, scale, 0, after(keep, w_give[0]), there, grad_here, grad_there
    )
    quick = parts == 16
    steps = weight_sum(who, w_keep, w_give, quick)

    last = next(steps)(grad_here)
    last = next(steps)(last)
    g_here = call(
        "keep",
        keep_kernel,
        who,
        [weight, w_there, after(grad_here, last), grad_there],
        [(keep.shape, F32)],
        flops=12 * rows // 2 * width * hidden,
    )[0]
    firsts = backward("back_here", who, t, [TWO, FAR, NEAR, OWN], after(g_here, last), [], 0)
    last = next(steps)(firsts[0])
    g_there = after(g_there, last)
    last = backward("back_two", who, t, [TWO], g_there, [firsts[0]], 1)[0]
    two = swapped(last, "dom")
    last = backward("back_far", who, t, [FAR], after(g_there, last), [firsts[1]], 1)[0]
    far = moved(last, "dom", -3, -1)
    last = backward("back_near", who, t, [NEAR], after(g_there, last), [firsts[2], two], 1)[0]
    near = moved(last, "dom", -1, -3)
    last = next(steps)(last)
    act_got = swapped(after(act_there, last), "feat")
    last = next(steps)(last, far)
    mine = backward("back_own", who, t, [OWN], after(g_there, last), [firsts[3]], 1)[0]
    activated = join("activated", who, SIDE, [after(act_here, last), act_got], jax.ShapeDtypeStruct)
    last = next(steps)(activated, mine)
    feature_grad = call(
        "feature_grad",
        add_kernel,
        who,
        [after(mine, last), far, near],
        [(features.shape, F32)],
        place=jax.ShapeDtypeStruct,
    )[0]
    weight_grad = next(steps)(feature_grad)
    return (activated, feature_grad, weight_grad)


def weight_sum(who, keep, give, quick):
    if not quick:
        here, there = (join("core_join", who, CORE, pair) for pair in zip(keep, give))
        total = lax.psum(here + swapped(there, "feat"), "dom")
        for _ in range(6):
            yield lambda *last: last[0]
        yield lambda *last: total
        return
    box = []

    def step(run):
        def go(*last):
            box.append(run(*last))
            return box[-1][0] if isinstance(box[-1], (list, tuple)) else box[-1]

        return go

    def up(value):
        return chosen(value, "dom", lambda i: i + 2 if i % 4 < 2 else None)

    gots = [swapped(value, "dom") for value in give]
    yield step(lambda *last: add("core_there", who, after(keep[1], *last), gots[1]))
    there = box[-1]
    yield step(lambda *last: add("core_here", who, after(keep[0], *last), gots[0]))
    here = box[-1]
    got = up(there)
    yield step(lambda *last: add("chip_there", who, after(there, *last), got))
    got = swapped(box[-1], "feat")
    also = up(here)
    yield step(lambda *last: side_sum("side_sum", who, after(here, *last), also, got)[::-1])
    give, keep = box[-1]
    gots = [
        chosen(value, "dom", lambda i: i ^ bits if i % 4 >= 2 else None)
        for value, bits in ((give, 4), (keep, 8), (give, 12))
    ]
    yield step(lambda *last: line_sum("line_sum", who, after(keep, *last), *gots))
    keep = box[-1]
    later_sent = chosen(keep, "dom", lambda i: (i ^ 4) - 2 if i % 4 >= 2 else None)
    later = chosen(keep, "dom", lambda i: i ^ 4 if i % 4 >= 2 else None)
    ready_sent = chosen(keep, "dom", lambda i: i - 2 if i % 4 >= 2 else None)
    yield step(
        lambda *last: pick("chip_pick", who, after(keep, *last), ready_sent, later, later_sent)
    )
    got = swapped(box[-1], "dom")
    yield step(
        lambda *last: join("weight_grad", who, CORE, [after(box[-1], *last), got], jax.ShapeDtypeStruct)
    )


def solution(mesh):
    in_specs = (
        P("dom", "feat"),
        P(None, "feat"),
        P("dom", "feat"),
        P("dom", None, None),
        P("dom", None, None),
        P("dom", None),
        P("dom", None, None, None, None),
    )
    out_specs = (P("dom", "feat"), P("dom", "feat"), P(None, "feat"))
    return jax.shard_map(body, mesh=mesh, in_specs=in_specs, out_specs=out_specs, check_vma=False)
```

```python
import functools
import math

import jax
import jax.numpy as jnp
from jax import lax
from jax.experimental import pallas as pl
from jax.experimental.pallas import tpu as pltpu
from jax.sharding import PartitionSpec as P

F32 = jnp.float32
BF16 = jnp.bfloat16
TILE = 256
LIMIT = 8 * 1024 * 1024
IN_VMEM = pl.BlockSpec(memory_space=pltpu.VMEM)
IN_SMEM = pl.BlockSpec(memory_space=pltpu.SMEM)

SIDE, CORE, NEAR, FAR, TWO, OWN, CHIP, LAYER = range(8)


def split(value):
    high = value.astype(BF16)
    low = (value - high.astype(F32)).astype(BF16)
    return high, low


def mm(a, b, dims=((1,), (0,))):
    return lax.dot_general(a, b, (dims, ((), ())), preferred_element_type=F32)


def mm3(a, b, dims=((1,), (0,))):
    (ah, al), (bh, bl) = a, b
    return mm(ah, bh, dims) + (mm(ah, bl, dims) + mm(al, bh, dims))


def call(name, kernel, who, operands, shapes, scratch=(), flops=0, place=pltpu.VMEM):
    moved = sum(a.size * a.dtype.itemsize for a in operands)
    pinned = [pltpu.with_memory_space_constraint(a, pltpu.VMEM) for a in operands]
    return pl.pallas_call(
        kernel,
        in_specs=[IN_SMEM] + [IN_VMEM] * len(operands),
        out_specs=[IN_VMEM] * len(shapes),
        out_shape=[place(*shape) for shape in shapes],
        scratch_shapes=list(scratch),
        compiler_params=pltpu.CompilerParams(vmem_limit_bytes=LIMIT),
        cost_estimate=pl.CostEstimate(flops=int(flops), bytes_accessed=moved, transcendentals=0),
        name=name,
    )(who, *pinned)


def lay_out_kernel(rows, cols, counts, who, blocks, a, t):
    slot = pl.program_id(0)
    cap = blocks.shape[1]
    size = blocks.shape[2]
    for out in (a, t):
        for part in range(2):
            out[part, slot] = jnp.zeros(out.shape[2:], out.dtype)

    def one(k, carry):
        r = pl.multiple_of(rows[slot, k] * size, size)
        c = pl.multiple_of(cols[slot, k] * size, size)
        block = blocks[0, k]
        for part, value in enumerate(split(block)):
            a[part, slot, pl.ds(r, size), pl.ds(c, size)] = value
        for part, value in enumerate(split(block.T)):
            t[part, slot, pl.ds(c, size), pl.ds(r, size)] = value
        return carry

    lax.fori_loop(0, jnp.minimum(counts[0, slot], cap), one, 0)


def lay_out(rows, cols, counts, who, blocks, size_all):
    window, cap, size, _ = blocks.shape
    shape = pltpu.VMEM((2, window, size_all, size_all), BF16)
    return pl.pallas_call(
        lay_out_kernel,
        grid_spec=pltpu.PrefetchScalarGridSpec(
            num_scalar_prefetch=4,
            grid=(window,),
            in_specs=[pl.BlockSpec((1, cap, size, size), lambda s, *_: (s, 0, 0, 0))],
            out_specs=[IN_VMEM] * 2,
        ),
        out_shape=[shape] * 2,
        compiler_params=pltpu.CompilerParams(vmem_limit_bytes=LIMIT),
        cost_estimate=pl.CostEstimate(flops=0, bytes_accessed=20_000_000, transcendentals=0),
        name="lay_out",
    )(rows, cols, counts, who, pltpu.with_memory_space_constraint(blocks, pltpu.HBM))


def forward_kernel(slots, part, has_base, who, matrix, *refs):
    n = len(slots)
    sources, refs = refs[:n], refs[n:]
    base, refs = (refs[0], refs[1:]) if has_base else (None, refs)
    out, (highs, lows) = refs[0], refs[1:]
    rows = out.shape[0]
    from_row = 0 if part is None else (who[SIDE] ^ part) * rows
    for i, source in enumerate(sources):
        highs[i], lows[i] = split(source[...])

    def tile(k, carry):
        there = pl.ds(pl.multiple_of(k * TILE, TILE), TILE)
        here = pl.ds(pl.multiple_of(from_row + k * TILE, TILE), TILE)
        total = None
        if base is not None:
            total = base[here if base.shape[0] > rows else there, :]
        for i, slot in enumerate(slots):
            at = who[slot]
            term = mm3((matrix[0, at, here, :], matrix[1, at, here, :]), (highs[i], lows[i]))
            total = term if total is None else total + term
        out[there, :] = total
        return carry

    lax.fori_loop(0, rows // TILE, tile, 0)


def forward(name, who, matrix, terms, base=None, part=None):
    slots = [slot for slot, _ in terms]
    sources = [source for _, source in terms]
    depth, width = sources[0].shape
    rows = matrix.shape[2] // (1 if part is None else 2)
    extra = [] if base is None else [base]
    return call(
        name,
        functools.partial(forward_kernel, slots, part, base is not None),
        who,
        [matrix, *sources, *extra],
        [((rows, width), F32)],
        [pltpu.VMEM((len(terms), depth, width), BF16)] * 2,
        6 * len(terms) * rows * depth * width,
    )[0]


def backward_kernel(slots, part, n_add, first, pieces, who, matrix, source, *refs):
    addends, outs = refs[:n_add], refs[n_add:]
    depth = source.shape[0]
    parts = split(source[...])
    deep = pl.ds(pl.multiple_of((who[SIDE] ^ part) * depth, depth), depth)
    size = outs[0].shape[0]
    here = pl.ds(first, size * pieces)
    for i, slot in enumerate(slots):
        at = who[slot]
        total = mm3((matrix[0, at, here, deep], matrix[1, at, here, deep]), parts)
        for addend in addends:
            total = total + addend[here, :]
        for k in range(pieces):
            outs[i * pieces + k][...] = total[k * size : (k + 1) * size, :]


def backward(name, who, matrix, slots, source, addends, part, first=0, rows=None, pieces=1):
    depth, width = source.shape
    rows = rows or matrix.shape[2]
    return call(
        name,
        functools.partial(backward_kernel, slots, part, len(addends), first, pieces),
        who,
        [matrix, source, *addends],
        [((rows // pieces, width), F32)] * (len(slots) * pieces),
        flops=6 * len(slots) * rows * depth * width,
    )


def middle_kernel(who, own, far, w_here, w_there, cot, cot_there, *outs):
    act_here, act_there, grad_here, grad_there, g_there = outs
    half = own.shape[1]

    def rows_of(w, which):
        return split(w[pl.ds(pl.multiple_of((who[SIDE] ^ which) * half, half), half), :])

    rows = own.shape[0]
    cot_here = cot.at[pl.ds(pl.multiple_of(who[SIDE] * rows, rows), rows), :]
    source = split(own[...]), split(far[...])
    total = None
    for w, cot, act, grad in (
        (w_here, cot_here, act_here, grad_here),
        (w_there, cot_there, act_there, grad_there),
    ):
        pre = mm3(source[0], rows_of(w, 0)) + mm3(source[1], rows_of(w, 1))
        s = 1.0 / (1.0 + jnp.exp(-pre))
        act[...] = pre * s
        pg = cot[...] * (s + pre * s * (1.0 - s))
        grad[...] = pg
        term = mm3(split(pg), rows_of(w, 1), ((1,), (1,)))
        total = term if total is None else total + term
    g_there[...] = total


def middle(who, own, far, w_here, w_there, cot, cot_there):
    shape = (cot_there.shape, F32)
    flops = 36 * own.shape[0] * own.shape[1] * w_here.shape[1]
    operands = [own, far, w_here, w_there, cot, cot_there]
    return call("middle", middle_kernel, who, operands, [shape] * 5, flops=flops)


def keep_kernel(who, w_here, w_there, grad_here, grad_there, g_here):
    half = g_here.shape[1]
    at = pl.ds(pl.multiple_of(who[SIDE] * half, half), half)
    total = None
    for w, grad in ((w_here, grad_here), (w_there, grad_there)):
        term = mm3(split(grad[...]), split(w[at, :]), ((1,), (1,)))
        total = term if total is None else total + term
    g_here[...] = total


def weight_kernel(scale, which, who, own, far, grad_here, grad_there, here, there):
    mine = who[SIDE] == (who[CORE] ^ which)
    turned = split(jnp.where(mine, own[...], far[...]).T)
    for grad, out in ((grad_here, here), (grad_there, there)):
        out[...] = mm3(turned, split(grad[...])) * scale


def weight_term(name, who, scale, which, own, far, grad_here, grad_there):
    rows, half = own.shape
    hidden = grad_here.shape[1]
    return call(
        name,
        functools.partial(weight_kernel, scale, which),
        who,
        [own, far, grad_here, grad_there],
        [((half, hidden), F32)] * 2,
        flops=12 * rows * half * hidden,
    )


def half_kernel(which, who, whole, out):
    rows = out.shape[0]
    out[...] = whole[pl.ds(pl.multiple_of((who[SIDE] ^ which) * rows, rows), rows), :]


def join_kernel(place, who, *refs):
    parts, out = refs[:-1], refs[-1]
    rows = parts[0].shape[0]
    for k, part in enumerate(parts):
        out[pl.ds(pl.multiple_of((who[place] ^ k) * rows, rows), rows), :] = part[...]


def join(name, who, place, parts, kind=pltpu.VMEM):
    rows, cols = parts[0].shape
    shape = (rows * len(parts), cols)
    return call(
        name, functools.partial(join_kernel, place), who, parts, [(shape, F32)], place=kind
    )[0]


def pick_kernel(who, ready, later, ready_sent, later_sent, out):
    rows = ready.shape[0]
    odd = who[CHIP] == 1
    for which, one, other in ((0, ready, ready_sent), (1, later, later_sent)):
        at = pl.ds(pl.multiple_of((who[LAYER] ^ which) * rows, rows), rows)
        out[at, :] = jnp.where(odd, one[...], other[...])


def pick(name, who, *parts):
    rows, cols = parts[0].shape
    return call(name, pick_kernel, who, parts, [((2 * rows, cols), F32)])[0]


def hand_out(full, outs, place):
    rows = outs[0].shape[0]
    for k, out in enumerate(outs):
        out[...] = full[pl.ds(pl.multiple_of((place ^ k) * rows, rows), rows), :]


def side_kernel(who, one, two, three, keep, give, full):
    full[...] = one[...] + two[...] + three[...]
    hand_out(full, (keep, give), who[LAYER])


def side_sum(name, who, *parts):
    rows, cols = parts[0].shape
    shape = ((rows // 2, cols), F32)
    return call(name, side_kernel, who, parts, [shape] * 2, [pltpu.VMEM((rows, cols), F32)])


def line_kernel(who, here, one, two, three, out):
    out[...] = (here[...] + one[...]) + (two[...] + three[...])


def line_sum(name, who, *parts):
    return call(name, line_kernel, who, parts, [(parts[0].shape, F32)])[0]


def add_kernel(who, *refs):
    total = refs[0][...]
    for ref in refs[1:-1]:
        total = total + ref[...]
    refs[-1][...] = total


def add(name, who, *parts):
    return call(name, add_kernel, who, parts, [(parts[0].shape, F32)])[0]


def moved(value, axis, even, odd):
    peers = lax.axis_size(axis)
    perm = [(i, (i + (odd if i % 2 else even)) % peers) for i in range(peers)]
    return lax.ppermute(value, axis, perm)


def chosen(value, axis, target):
    peers = lax.axis_size(axis)
    pairs = [(i, target(i)) for i in range(peers)]
    return lax.ppermute(value, axis, [pair for pair in pairs if pair[1] is not None])


def swapped(value, axis):
    return chosen(value, axis, lambda i: i ^ 1)


def after(value, *others):
    return lax.optimization_barrier((value, *others))[0]


def body(features, weight, cotangent, block_rows, block_cols, block_counts, block_values):
    rows, width = features.shape
    hidden = weight.shape[1]
    depth = weight.shape[0]
    parts = lax.axis_size("dom")
    side = lax.axis_index("feat").astype(jnp.int32)
    place = lax.axis_index("dom").astype(jnp.int32)
    odd = place & 1
    zero = place * 0
    who = jnp.stack([side, odd, 1 + 2 * odd, 3 - 2 * odd, zero + 2, zero, (place >> 1) & 1,
                     (place >> 2) & 1])

    near = moved(features, "dom", 3, 1)
    far = moved(features, "dom", 1, 3)
    w_there = swapped(weight, "feat")
    half_shape = ((rows // 2, hidden), F32)
    cot_give = call("cot_give", functools.partial(half_kernel, 1), who, [cotangent], [half_shape])[0]
    cot_there = swapped(cot_give, "feat")

    a, t = lay_out(
        block_rows[0], block_cols[0], block_counts, who, block_values[0], rows
    )
    total = forward("agg_own", who, a, [(OWN, features)])
    near = after(near, total, w_there, cot_there)
    two = swapped(near, "dom")
    total = forward("agg_near", who, a, [(NEAR, near)], total)
    far = after(far, total)
    give = forward("agg_give", who, a, [(FAR, far), (TWO, two)], total, 1)
    there = swapped(give, "feat")
    keep = forward("agg_keep", who, a, [(FAR, far), (TWO, after(two, give))], total, 0)

    act_here, act_there, grad_here, grad_there, g_give = middle(
        who, keep, there, weight, w_there, cotangent, cot_there
    )
    g_there = swapped(g_give, "feat")
    scale = 1.0 / math.sqrt(rows * parts)
    w_give = weight_term("weight_give", who, scale, 1, keep, there, grad_here, grad_there)
    w_keep = weight_term(
        "weight_keep", who, scale, 0, after(keep, w_give[0]), there, grad_here, grad_there
    )
    quick = parts == 16
    steps = weight_sum(who, w_keep, w_give, quick)

    last = next(steps)(grad_here)
    last = next(steps)(last)
    g_here = call(
        "keep",
        keep_kernel,
        who,
        [weight, w_there, after(grad_here, last), grad_there],
        [(keep.shape, F32)],
        flops=12 * rows // 2 * width * hidden,
    )[0]
    firsts = backward("back_here", who, t, [TWO, FAR, NEAR, OWN], after(g_here, last), [], 0)
    last = next(steps)(firsts[0])
    g_there = after(g_there, last)
    last = backward("back_two", who, t, [TWO], g_there, [firsts[0]], 1)[0]
    two = swapped(last, "dom")
    last = backward("back_far", who, t, [FAR], after(g_there, last), [firsts[1]], 1)[0]
    far = moved(last, "dom", -3, -1)
    last = backward("back_near", who, t, [NEAR], after(g_there, last), [firsts[2], two], 1)[0]
    near = moved(last, "dom", -1, -3)
    last = next(steps)(last)
    act_got = swapped(after(act_there, last), "feat")
    mine = backward("back_own", who, t, [OWN], after(g_there, last), [firsts[3]], 1)[0]
    last = next(steps)(mine, far)
    activated = join("activated", who, SIDE, [after(act_here, last), act_got], jax.ShapeDtypeStruct)
    last = next(steps)(activated)
    feature_grad = call(
        "feature_grad",
        add_kernel,
        who,
        [after(mine, last), far, near],
        [(features.shape, F32)],
        place=jax.ShapeDtypeStruct,
    )[0]
    weight_grad = next(steps)(feature_grad)
    return (activated, feature_grad, weight_grad)


def weight_sum(who, keep, give, quick):
    if not quick:
        here, there = (join("core_join", who, CORE, pair) for pair in zip(keep, give))
        total = lax.psum(here + swapped(there, "feat"), "dom")
        for _ in range(6):
            yield lambda *last: last[0]
        yield lambda *last: total
        return
    box = []

    def step(run):
        def go(*last):
            box.append(run(*last))
            return box[-1][0] if isinstance(box[-1], (list, tuple)) else box[-1]

        return go

    def up(value):
        return chosen(value, "dom", lambda i: i + 2 if i % 4 < 2 else None)

    gots = [swapped(value, "dom") for value in give]
    yield step(lambda *last: add("core_there", who, after(keep[1], *last), gots[1]))
    there = box[-1]
    yield step(lambda *last: add("core_here", who, after(keep[0], *last), gots[0]))
    here = box[-1]
    got = up(there)
    yield step(lambda *last: add("chip_there", who, after(there, *last), got))
    got = swapped(box[-1], "feat")
    also = up(here)
    yield step(lambda *last: side_sum("side_sum", who, after(here, *last), also, got)[::-1])
    give, keep = box[-1]
    gots = [
        chosen(value, "dom", lambda i: i ^ bits if i % 4 >= 2 else None)
        for value, bits in ((give, 4), (keep, 8), (give, 12))
    ]
    yield step(lambda *last: line_sum("line_sum", who, after(keep, *last), *gots))
    keep = box[-1]
    later_sent = chosen(keep, "dom", lambda i: (i ^ 4) - 2 if i % 4 >= 2 else None)
    later = chosen(keep, "dom", lambda i: i ^ 4 if i % 4 >= 2 else None)
    ready_sent = chosen(keep, "dom", lambda i: i - 2 if i % 4 >= 2 else None)
    yield step(
        lambda *last: pick("chip_pick", who, after(keep, *last), later, ready_sent, later_sent)
    )
    got = swapped(box[-1], "dom")
    yield step(
        lambda *last: join("weight_grad", who, CORE, [after(box[-1], *last), got], jax.ShapeDtypeStruct)
    )


def solution(mesh):
    in_specs = (
        P("dom", "feat"),
        P(None, "feat"),
        P("dom", "feat"),
        P("dom", None, None),
        P("dom", None, None),
        P("dom", None),
        P("dom", None, None, None, None),
    )
    out_specs = (P("dom", "feat"), P("dom", "feat"), P(None, "feat"))
    return jax.shard_map(body, mesh=mesh, in_specs=in_specs, out_specs=out_specs, check_vma=False)
```

```python
import functools
import math

import jax
import jax.numpy as jnp
from jax import lax
from jax.experimental import pallas as pl
from jax.experimental.pallas import tpu as pltpu
from jax.sharding import PartitionSpec as P

F32 = jnp.float32
BF16 = jnp.bfloat16
TILE = 256
LIMIT = 8 * 1024 * 1024
IN_VMEM = pl.BlockSpec(memory_space=pltpu.VMEM)
IN_SMEM = pl.BlockSpec(memory_space=pltpu.SMEM)

SIDE, CORE, NEAR, FAR, TWO, OWN, CHIP, LAYER = range(8)


def split(value):
    high = value.astype(BF16)
    low = (value - high.astype(F32)).astype(BF16)
    return high, low


def mm(a, b, dims=((1,), (0,))):
    return lax.dot_general(a, b, (dims, ((), ())), preferred_element_type=F32)


def mm3(a, b, dims=((1,), (0,))):
    (ah, al), (bh, bl) = a, b
    return mm(ah, bh, dims) + (mm(ah, bl, dims) + mm(al, bh, dims))


def call(name, kernel, who, operands, shapes, scratch=(), flops=0, place=pltpu.VMEM):
    moved = sum(a.size * a.dtype.itemsize for a in operands)
    pinned = [pltpu.with_memory_space_constraint(a, pltpu.VMEM) for a in operands]
    return pl.pallas_call(
        kernel,
        in_specs=[IN_SMEM] + [IN_VMEM] * len(operands),
        out_specs=[IN_VMEM] * len(shapes),
        out_shape=[place(*shape) for shape in shapes],
        scratch_shapes=list(scratch),
        compiler_params=pltpu.CompilerParams(vmem_limit_bytes=LIMIT),
        cost_estimate=pl.CostEstimate(flops=int(flops), bytes_accessed=moved, transcendentals=0),
        name=name,
    )(who, *pinned)


def lay_out_kernel(rows, cols, counts, who, blocks, a, t):
    slot = pl.program_id(0)
    cap = blocks.shape[1]
    size = blocks.shape[2]
    for out in (a, t):
        for part in range(2):
            out[part, slot] = jnp.zeros(out.shape[2:], out.dtype)

    def one(k, carry):
        r = pl.multiple_of(rows[slot, k] * size, size)
        c = pl.multiple_of(cols[slot, k] * size, size)
        block = blocks[0, k]
        for part, value in enumerate(split(block)):
            a[part, slot, pl.ds(r, size), pl.ds(c, size)] = value
        for part, value in enumerate(split(block.T)):
            t[part, slot, pl.ds(c, size), pl.ds(r, size)] = value
        return carry

    lax.fori_loop(0, jnp.minimum(counts[0, slot], cap), one, 0)


def lay_out(rows, cols, counts, who, blocks, size_all):
    window, cap, size, _ = blocks.shape
    shape = pltpu.VMEM((2, window, size_all, size_all), BF16)
    return pl.pallas_call(
        lay_out_kernel,
        grid_spec=pltpu.PrefetchScalarGridSpec(
            num_scalar_prefetch=4,
            grid=(window,),
            in_specs=[pl.BlockSpec((1, cap, size, size), lambda s, *_: (s, 0, 0, 0))],
            out_specs=[IN_VMEM] * 2,
        ),
        out_shape=[shape] * 2,
        compiler_params=pltpu.CompilerParams(vmem_limit_bytes=LIMIT),
        cost_estimate=pl.CostEstimate(flops=0, bytes_accessed=20_000_000, transcendentals=0),
        name="lay_out",
    )(rows, cols, counts, who, pltpu.with_memory_space_constraint(blocks, pltpu.HBM))


def forward_kernel(slots, halves, part, has_base, who, matrix, *refs):
    n = len(slots)
    sources, refs = list(refs[: sum(halves)]), refs[sum(halves) :]
    base, refs = (refs[0], refs[1:]) if has_base else (None, refs)
    out, (highs, lows) = refs[0], refs[1:]
    rows = out.shape[0]
    from_row = 0 if part is None else (who[SIDE] ^ part) * rows
    for i in range(n):
        depth = highs.shape[1] // halves[i]
        for k in range(halves[i]):
            at = pl.ds(k * depth, depth)
            highs[i, at, :], lows[i, at, :] = split(sources.pop(0)[...])

    def tile(k, carry):
        there = pl.ds(pl.multiple_of(k * TILE, TILE), TILE)
        here = pl.ds(pl.multiple_of(from_row + k * TILE, TILE), TILE)
        total = None
        if base is not None:
            total = base[here if base.shape[0] > rows else there, :]
        for i, slot in enumerate(slots):
            at = who[slot]
            term = mm3((matrix[0, at, here, :], matrix[1, at, here, :]), (highs[i], lows[i]))
            total = term if total is None else total + term
        out[there, :] = total
        return carry

    lax.fori_loop(0, rows // TILE, tile, 0)


def forward(name, who, matrix, terms, base=None, part=None):
    slots = [slot for slot, _ in terms]
    groups = [group if isinstance(group, tuple) else (group,) for _, group in terms]
    sources = [source for group in groups for source in group]
    width = sources[0].shape[1]
    depth = matrix.shape[3]
    rows = matrix.shape[2] // (1 if part is None else 2)
    extra = [] if base is None else [base]
    return call(
        name,
        functools.partial(
            forward_kernel, slots, [len(group) for group in groups], part, base is not None
        ),
        who,
        [matrix, *sources, *extra],
        [((rows, width), F32)],
        [pltpu.VMEM((len(terms), depth, width), BF16)] * 2,
        6 * len(terms) * rows * depth * width,
    )[0]


def backward_kernel(slots, part, n_add, first, pieces, who, matrix, source, *refs):
    addends, outs = refs[:n_add], refs[n_add:]
    depth = source.shape[0]
    parts = split(source[...])
    deep = pl.ds(pl.multiple_of((who[SIDE] ^ part) * depth, depth), depth)
    size = outs[0].shape[0]
    here = pl.ds(first, size * pieces)
    for i, slot in enumerate(slots):
        at = who[slot]
        total = mm3((matrix[0, at, here, deep], matrix[1, at, here, deep]), parts)
        for addend in addends:
            total = total + addend[here, :]
        for k in range(pieces):
            outs[i * pieces + k][...] = total[k * size : (k + 1) * size, :]


def backward(name, who, matrix, slots, source, addends, part, first=0, rows=None, pieces=1):
    depth, width = source.shape
    rows = rows or matrix.shape[2]
    return call(
        name,
        functools.partial(backward_kernel, slots, part, len(addends), first, pieces),
        who,
        [matrix, source, *addends],
        [((rows // pieces, width), F32)] * (len(slots) * pieces),
        flops=6 * len(slots) * rows * depth * width,
    )


def middle_kernel(who, own, far, w_here, w_there, cot, cot_there, *outs):
    act_here, act_there, grad_here, grad_there, g_there = outs
    half = own.shape[1]

    def rows_of(w, which):
        return split(w[pl.ds(pl.multiple_of((who[SIDE] ^ which) * half, half), half), :])

    rows = own.shape[0]
    cot_here = cot.at[pl.ds(pl.multiple_of(who[SIDE] * rows, rows), rows), :]
    source = split(own[...]), split(far[...])
    total = None
    for w, cot, act, grad in (
        (w_here, cot_here, act_here, grad_here),
        (w_there, cot_there, act_there, grad_there),
    ):
        pre = mm3(source[0], rows_of(w, 0)) + mm3(source[1], rows_of(w, 1))
        s = 1.0 / (1.0 + jnp.exp(-pre))
        act[...] = pre * s
        pg = cot[...] * (s + pre * s * (1.0 - s))
        grad[...] = pg
        term = mm3(split(pg), rows_of(w, 1), ((1,), (1,)))
        total = term if total is None else total + term
    g_there[...] = total


def middle(who, own, far, w_here, w_there, cot, cot_there):
    shape = (cot_there.shape, F32)
    flops = 36 * own.shape[0] * own.shape[1] * w_here.shape[1]
    operands = [own, far, w_here, w_there, cot, cot_there]
    return call("middle", middle_kernel, who, operands, [shape] * 5, flops=flops)


def keep_kernel(who, w_here, w_there, grad_here, grad_there, g_here):
    half = g_here.shape[1]
    at = pl.ds(pl.multiple_of(who[SIDE] * half, half), half)
    total = None
    for w, grad in ((w_here, grad_here), (w_there, grad_there)):
        term = mm3(split(grad[...]), split(w[at, :]), ((1,), (1,)))
        total = term if total is None else total + term
    g_here[...] = total


def weight_kernel(scale, which, who, own, far, grad_here, grad_there, out):
    mine = who[SIDE] == (who[CORE] ^ which)
    turned = split(jnp.where(mine, own[...], far[...]).T)
    hidden = grad_here.shape[1]
    for k, grad in enumerate((grad_here, grad_there)):
        out[:, k * hidden : (k + 1) * hidden] = mm3(turned, split(grad[...])) * scale


def weight_term(name, who, scale, which, own, far, grad_here, grad_there):
    rows, half = own.shape
    hidden = grad_here.shape[1]
    return call(
        name,
        functools.partial(weight_kernel, scale, which),
        who,
        [own, far, grad_here, grad_there],
        [((half, 2 * hidden), F32)],
        flops=12 * rows * half * hidden,
    )[0]


def half_kernel(which, who, whole, out):
    rows = out.shape[0]
    out[...] = whole[pl.ds(pl.multiple_of((who[SIDE] ^ which) * rows, rows), rows), :]


def join_kernel(place, who, *refs):
    parts, out = refs[:-1], refs[-1]
    rows = parts[0].shape[0]
    for k, part in enumerate(parts):
        out[pl.ds(pl.multiple_of((who[place] ^ k) * rows, rows), rows), :] = part[...]


def join(name, who, place, parts, kind=pltpu.VMEM):
    rows, cols = parts[0].shape
    shape = (rows * len(parts), cols)
    return call(
        name, functools.partial(join_kernel, place), who, parts, [(shape, F32)], place=kind
    )[0]


def pick_kernel(who, ready, later, ready_sent, later_sent, out):
    rows = ready.shape[0]
    odd = who[CHIP] == 1
    for which, one, other in ((0, ready, ready_sent), (1, later, later_sent)):
        at = pl.ds(pl.multiple_of((who[LAYER] ^ which) * rows, rows), rows)
        out[at, :] = jnp.where(odd, one[...], other[...])


def pick(name, who, *parts):
    rows, cols = parts[0].shape
    return call(name, pick_kernel, who, parts, [((2 * rows, cols), F32)])[0]


def hand_out(full, outs, place):
    rows = outs[0].shape[0]
    for k, out in enumerate(outs):
        out[...] = full[pl.ds(pl.multiple_of((place ^ k) * rows, rows), rows), :]


def side_kernel(who, one, two, three, keep, give, full):
    full[...] = one[...] + two[...] + three[...]
    hand_out(full, (keep, give), who[LAYER])


def side_sum(name, who, *parts):
    rows, cols = parts[0].shape
    shape = ((rows // 2, cols), F32)
    return call(name, side_kernel, who, parts, [shape] * 2, [pltpu.VMEM((rows, cols), F32)])


def core_kernel(who, one, other, here, there):
    cols = here.shape[1]
    here[...] = one[:, :cols] + other[:, :cols]
    there[...] = one[:, cols:] + other[:, cols:]


def core_sum(name, who, one, other):
    rows, cols = one.shape
    return call(name, core_kernel, who, [one, other], [((rows, cols // 2), F32)] * 2)


def add_kernel(who, *refs):
    total = refs[0][...]
    for ref in refs[1:-1]:
        total = total + ref[...]
    refs[-1][...] = total


def add(name, who, *parts):
    return call(name, add_kernel, who, parts, [(parts[0].shape, F32)])[0]


def moved(value, axis, even, odd):
    peers = lax.axis_size(axis)
    perm = [(i, (i + (odd if i % 2 else even)) % peers) for i in range(peers)]
    return lax.ppermute(value, axis, perm)


def chosen(value, axis, target):
    peers = lax.axis_size(axis)
    pairs = [(i, target(i)) for i in range(peers)]
    return lax.ppermute(value, axis, [pair for pair in pairs if pair[1] is not None])


def swapped(value, axis):
    return chosen(value, axis, lambda i: i ^ 1)


def after(value, *others):
    return lax.optimization_barrier((value, *others))[0]


def body(features, weight, cotangent, block_rows, block_cols, block_counts, block_values):
    rows, width = features.shape
    hidden = weight.shape[1]
    depth = weight.shape[0]
    parts = lax.axis_size("dom")
    side = lax.axis_index("feat").astype(jnp.int32)
    place = lax.axis_index("dom").astype(jnp.int32)
    odd = place & 1
    zero = place * 0
    who = jnp.stack([side, odd, 1 + 2 * odd, 3 - 2 * odd, zero + 2, zero, (place >> 1) & 1,
                     (place >> 2) & 1])

    near = moved(features, "dom", 3, 1)
    far = moved(features, "dom", 1, 3)
    w_there = swapped(weight, "feat")
    half_shape = ((rows // 2, hidden), F32)
    cot_give = call("cot_give", functools.partial(half_kernel, 1), who, [cotangent], [half_shape])[0]
    cot_there = swapped(cot_give, "feat")

    a, t = lay_out(
        block_rows[0], block_cols[0], block_counts, who, block_values[0], rows
    )
    total = forward("agg_own", who, a, [(OWN, features)])
    near = after(near, total, w_there, cot_there)
    two = tuple(swapped(near[k * rows // 2 : (k + 1) * rows // 2], "dom") for k in range(2))
    total = forward("agg_near", who, a, [(NEAR, near)], total)
    give = forward("agg_two", who, a, [(TWO, two)], total, 1)
    far = after(far, give)
    give = forward("agg_give", who, a, [(FAR, far)], give, 1)
    there = swapped(give, "feat")
    keep = forward("agg_keep", who, a, [(FAR, far), (TWO, (after(two[0], give), two[1]))], total, 0)

    act_here, act_there, grad_here, grad_there, g_give = middle(
        who, keep, there, weight, w_there, cotangent, cot_there
    )
    g_there = swapped(g_give, "feat")
    scale = 1.0 / math.sqrt(rows * parts)
    w_give = weight_term("weight_give", who, scale, 1, keep, there, grad_here, grad_there)
    w_keep = weight_term(
        "weight_keep", who, scale, 0, after(keep, w_give), there, grad_here, grad_there
    )
    quick = parts == 16
    steps = weight_sum(who, w_keep, w_give, quick)

    last = next(steps)(grad_here)
    g_here = call(
        "keep",
        keep_kernel,
        who,
        [weight, w_there, after(grad_here, last), grad_there],
        [(keep.shape, F32)],
        flops=12 * rows // 2 * width * hidden,
    )[0]
    firsts = backward("back_here", who, t, [TWO, FAR, NEAR, OWN], after(g_here, last), [], 0)
    last = next(steps)(firsts[0])
    g_there = after(g_there, last)
    last = backward("back_two", who, t, [TWO], g_there, [firsts[0]], 1)[0]
    two = swapped(last, "dom")
    last = backward("back_far", who, t, [FAR], after(g_there, last), [firsts[1]], 1)[0]
    far = moved(last, "dom", -3, -1)
    last = backward("back_near", who, t, [NEAR], after(g_there, last), [firsts[2], two], 1)[0]
    near = moved(last, "dom", -1, -3)
    last = next(steps)(last)
    act_got = swapped(after(act_there, last), "feat")
    mine = backward("back_own", who, t, [OWN], after(g_there, last), [firsts[3]], 1)[0]
    last = next(steps)(mine, far)
    last = next(steps)(last)
    activated = join("activated", who, SIDE, [after(act_here, last), act_got], jax.ShapeDtypeStruct)
    last = next(steps)(activated)
    feature_grad = call(
        "feature_grad",
        add_kernel,
        who,
        [after(mine, last), far, near],
        [(features.shape, F32)],
        place=jax.ShapeDtypeStruct,
    )[0]
    weight_grad = next(steps)(feature_grad)
    return (activated, feature_grad, weight_grad)


def weight_sum(who, keep, give, quick):
    if not quick:
        here, there = jnp.split(join("core_join", who, CORE, (keep, give)), 2, axis=1)
        total = lax.psum(here + swapped(there, "feat"), "dom")
        for _ in range(6):
            yield lambda *last: last[0]
        yield lambda *last: total
        return
    box = []

    def step(run):
        def go(*last):
            box.append(run(*last))
            return box[-1][0] if isinstance(box[-1], (list, tuple)) else box[-1]

        return go

    def up(value):
        return chosen(value, "dom", lambda i: i + 2 if i % 4 < 2 else None)

    got = swapped(give, "dom")
    yield step(lambda *last: core_sum("core_sum", who, after(keep, *last), got)[::-1])
    there, here = box[-1]
    got = up(there)
    yield step(lambda *last: add("chip_there", who, after(there, *last), got))
    got = swapped(box[-1], "feat")
    also = up(here)
    yield step(lambda *last: side_sum("side_sum", who, after(here, *last), also, got)[::-1])
    give, keep = box[-1]
    for name, bit in (("layer_sum", 4), ("pair_sum", 8)):
        got = chosen(give, "dom", lambda i: i ^ bit if i % 4 >= 2 else None)
        yield step(lambda *last: add(name, who, after(keep, *last), got))
        keep = give = box[-1]
    later_sent = chosen(keep, "dom", lambda i: (i ^ 4) - 2 if i % 4 >= 2 else None)
    later = chosen(keep, "dom", lambda i: i ^ 4 if i % 4 >= 2 else None)
    ready_sent = chosen(keep, "dom", lambda i: i - 2 if i % 4 >= 2 else None)
    yield step(
        lambda *last: pick("chip_pick", who, after(keep, *last), later, ready_sent, later_sent)
    )
    got = swapped(box[-1], "dom")
    yield step(
        lambda *last: join("weight_grad", who, CORE, [after(box[-1], *last), got], jax.ShapeDtypeStruct)
    )


def solution(mesh):
    in_specs = (
        P("dom", "feat"),
        P(None, "feat"),
        P("dom", "feat"),
        P("dom", None, None),
        P("dom", None, None),
        P("dom", None),
        P("dom", None, None, None, None),
    )
    out_specs = (P("dom", "feat"), P("dom", "feat"), P(None, "feat"))
    return jax.shard_map(body, mesh=mesh, in_specs=in_specs, out_specs=out_specs, check_vma=False)
```

```python
import functools
import math

import jax
import jax.numpy as jnp
from jax import lax
from jax.experimental import pallas as pl
from jax.experimental.pallas import tpu as pltpu
from jax.sharding import PartitionSpec as P

F32 = jnp.float32
BF16 = jnp.bfloat16
TILE = 256
LIMIT = 8 * 1024 * 1024
IN_VMEM = pl.BlockSpec(memory_space=pltpu.VMEM)
IN_SMEM = pl.BlockSpec(memory_space=pltpu.SMEM)

SIDE, CORE, NEAR, FAR, TWO, OWN, CHIP, LAYER = range(8)


def split(value):
    high = value.astype(BF16)
    low = (value - high.astype(F32)).astype(BF16)
    return high, low


def mm(a, b, dims=((1,), (0,))):
    return lax.dot_general(a, b, (dims, ((), ())), preferred_element_type=F32)


def mm3(a, b, dims=((1,), (0,))):
    (ah, al), (bh, bl) = a, b
    return mm(ah, bh, dims) + (mm(ah, bl, dims) + mm(al, bh, dims))


def call(name, kernel, who, operands, shapes, scratch=(), flops=0, place=pltpu.VMEM):
    moved = sum(a.size * a.dtype.itemsize for a in operands)
    pinned = [pltpu.with_memory_space_constraint(a, pltpu.VMEM) for a in operands]
    return pl.pallas_call(
        kernel,
        in_specs=[IN_SMEM] + [IN_VMEM] * len(operands),
        out_specs=[IN_VMEM] * len(shapes),
        out_shape=[place(*shape) for shape in shapes],
        scratch_shapes=list(scratch),
        compiler_params=pltpu.CompilerParams(vmem_limit_bytes=LIMIT),
        cost_estimate=pl.CostEstimate(flops=int(flops), bytes_accessed=moved, transcendentals=0),
        name=name,
    )(who, *pinned)


def lay_out_kernel(rows, cols, counts, who, blocks, a, t):
    slot = pl.program_id(0)
    cap = blocks.shape[1]
    size = blocks.shape[2]
    for out in (a, t):
        for part in range(2):
            out[part, slot] = jnp.zeros(out.shape[2:], out.dtype)

    def one(k, carry):
        r = pl.multiple_of(rows[slot, k] * size, size)
        c = pl.multiple_of(cols[slot, k] * size, size)
        block = blocks[0, k]
        for part, value in enumerate(split(block)):
            a[part, slot, pl.ds(r, size), pl.ds(c, size)] = value
        for part, value in enumerate(split(block.T)):
            t[part, slot, pl.ds(c, size), pl.ds(r, size)] = value
        return carry

    lax.fori_loop(0, jnp.minimum(counts[0, slot], cap), one, 0)


def lay_out(rows, cols, counts, who, blocks, size_all):
    window, cap, size, _ = blocks.shape
    shape = pltpu.VMEM((2, window, size_all, size_all), BF16)
    return pl.pallas_call(
        lay_out_kernel,
        grid_spec=pltpu.PrefetchScalarGridSpec(
            num_scalar_prefetch=4,
            grid=(window,),
            in_specs=[pl.BlockSpec((1, cap, size, size), lambda s, *_: (s, 0, 0, 0))],
            out_specs=[IN_VMEM] * 2,
        ),
        out_shape=[shape] * 2,
        compiler_params=pltpu.CompilerParams(vmem_limit_bytes=LIMIT),
        cost_estimate=pl.CostEstimate(flops=0, bytes_accessed=20_000_000, transcendentals=0),
        name="lay_out",
    )(rows, cols, counts, who, pltpu.with_memory_space_constraint(blocks, pltpu.HBM))


def forward_kernel(slots, halves, part, has_base, who, matrix, *refs):
    n = len(slots)
    sources, refs = list(refs[: sum(halves)]), refs[sum(halves) :]
    base, refs = (refs[0], refs[1:]) if has_base else (None, refs)
    out, (highs, lows) = refs[0], refs[1:]
    rows = out.shape[0]
    from_row = 0 if part is None else (who[SIDE] ^ part) * rows
    for i in range(n):
        depth = highs.shape[1] // halves[i]
        for k in range(halves[i]):
            at = pl.ds(k * depth, depth)
            highs[i, at, :], lows[i, at, :] = split(sources.pop(0)[...])

    def tile(k, carry):
        there = pl.ds(pl.multiple_of(k * TILE, TILE), TILE)
        here = pl.ds(pl.multiple_of(from_row + k * TILE, TILE), TILE)
        total = None
        if base is not None:
            total = base[here if base.shape[0] > rows else there, :]
        for i, slot in enumerate(slots):
            at = who[slot]
            term = mm3((matrix[0, at, here, :], matrix[1, at, here, :]), (highs[i], lows[i]))
            total = term if total is None else total + term
        out[there, :] = total
        return carry

    lax.fori_loop(0, rows // TILE, tile, 0)


def forward(name, who, matrix, terms, base=None, part=None):
    slots = [slot for slot, _ in terms]
    groups = [group if isinstance(group, tuple) else (group,) for _, group in terms]
    sources = [source for group in groups for source in group]
    width = sources[0].shape[1]
    depth = matrix.shape[3]
    rows = matrix.shape[2] // (1 if part is None else 2)
    extra = [] if base is None else [base]
    return call(
        name,
        functools.partial(
            forward_kernel, slots, [len(group) for group in groups], part, base is not None
        ),
        who,
        [matrix, *sources, *extra],
        [((rows, width), F32)],
        [pltpu.VMEM((len(terms), depth, width), BF16)] * 2,
        6 * len(terms) * rows * depth * width,
    )[0]


def backward_kernel(slots, part, n_add, first, pieces, who, matrix, source, *refs):
    addends, outs = refs[:n_add], refs[n_add:]
    depth = source.shape[0]
    parts = split(source[...])
    deep = pl.ds(pl.multiple_of((who[SIDE] ^ part) * depth, depth), depth)
    size = outs[0].shape[0]
    here = pl.ds(first, size * pieces)
    for i, slot in enumerate(slots):
        at = who[slot]
        total = mm3((matrix[0, at, here, deep], matrix[1, at, here, deep]), parts)
        for addend in addends:
            total = total + addend[here, :]
        for k in range(pieces):
            outs[i * pieces + k][...] = total[k * size : (k + 1) * size, :]


def backward(name, who, matrix, slots, source, addends, part, first=0, rows=None, pieces=1):
    depth, width = source.shape
    rows = rows or matrix.shape[2]
    return call(
        name,
        functools.partial(backward_kernel, slots, part, len(addends), first, pieces),
        who,
        [matrix, source, *addends],
        [((rows // pieces, width), F32)] * (len(slots) * pieces),
        flops=6 * len(slots) * rows * depth * width,
    )


def middle_kernel(who, own, far, w_here, w_there, cot, cot_there, *outs):
    act_here, act_there, grad_here, grad_there, g_there = outs
    half = own.shape[1]

    def rows_of(w, which):
        return split(w[pl.ds(pl.multiple_of((who[SIDE] ^ which) * half, half), half), :])

    rows = own.shape[0]
    cot_here = cot.at[pl.ds(pl.multiple_of(who[SIDE] * rows, rows), rows), :]
    source = split(own[...]), split(far[...])
    total = None
    for w, cot, act, grad in (
        (w_here, cot_here, act_here, grad_here),
        (w_there, cot_there, act_there, grad_there),
    ):
        pre = mm3(source[0], rows_of(w, 0)) + mm3(source[1], rows_of(w, 1))
        s = 1.0 / (1.0 + jnp.exp(-pre))
        act[...] = pre * s
        pg = cot[...] * (s + pre * s * (1.0 - s))
        grad[...] = pg
        term = mm3(split(pg), rows_of(w, 1), ((1,), (1,)))
        total = term if total is None else total + term
    g_there[...] = total


def middle(who, own, far, w_here, w_there, cot, cot_there):
    shape = (cot_there.shape, F32)
    flops = 36 * own.shape[0] * own.shape[1] * w_here.shape[1]
    operands = [own, far, w_here, w_there, cot, cot_there]
    return call("middle", middle_kernel, who, operands, [shape] * 5, flops=flops)


def keep_kernel(who, w_here, w_there, grad_here, grad_there, g_here):
    half = g_here.shape[1]
    at = pl.ds(pl.multiple_of(who[SIDE] * half, half), half)
    total = None
    for w, grad in ((w_here, grad_here), (w_there, grad_there)):
        term = mm3(split(grad[...]), split(w[at, :]), ((1,), (1,)))
        total = term if total is None else total + term
    g_here[...] = total


def weight_kernel(scale, which, who, own, far, grad_here, grad_there, out):
    mine = who[SIDE] == (who[CORE] ^ which)
    turned = split(jnp.where(mine, own[...], far[...]).T)
    hidden = grad_here.shape[1]
    for k, grad in enumerate((grad_here, grad_there)):
        out[:, k * hidden : (k + 1) * hidden] = mm3(turned, split(grad[...])) * scale


def weight_term(name, who, scale, which, own, far, grad_here, grad_there):
    rows, half = own.shape
    hidden = grad_here.shape[1]
    return call(
        name,
        functools.partial(weight_kernel, scale, which),
        who,
        [own, far, grad_here, grad_there],
        [((half, 2 * hidden), F32)],
        flops=12 * rows * half * hidden,
    )[0]


def half_kernel(which, who, whole, out):
    rows = out.shape[0]
    out[...] = whole[pl.ds(pl.multiple_of((who[SIDE] ^ which) * rows, rows), rows), :]


def join_kernel(place, who, *refs):
    parts, out = refs[:-1], refs[-1]
    rows = parts[0].shape[0]
    for k, part in enumerate(parts):
        out[pl.ds(pl.multiple_of((who[place] ^ k) * rows, rows), rows), :] = part[...]


def join(name, who, place, parts, kind=pltpu.VMEM):
    rows, cols = parts[0].shape
    shape = (rows * len(parts), cols)
    return call(
        name, functools.partial(join_kernel, place), who, parts, [(shape, F32)], place=kind
    )[0]


def pick_kernel(who, ready, later, ready_sent, later_sent, out):
    rows = ready.shape[0]
    odd = who[CHIP] == 1
    for which, one, other in ((0, ready, ready_sent), (1, later, later_sent)):
        at = pl.ds(pl.multiple_of((who[LAYER] ^ which) * rows, rows), rows)
        out[at, :] = jnp.where(odd, one[...], other[...])


def pick(name, who, *parts):
    rows, cols = parts[0].shape
    return call(name, pick_kernel, who, parts, [((2 * rows, cols), F32)])[0]


def hand_out(full, outs, place):
    rows = outs[0].shape[0]
    for k, out in enumerate(outs):
        out[...] = full[pl.ds(pl.multiple_of((place ^ k) * rows, rows), rows), :]


def side_kernel(who, one, two, three, keep, give, full):
    full[...] = one[...] + two[...] + three[...]
    hand_out(full, (keep, give), who[LAYER])


def side_sum(name, who, *parts):
    rows, cols = parts[0].shape
    shape = ((rows // 2, cols), F32)
    return call(name, side_kernel, who, parts, [shape] * 2, [pltpu.VMEM((rows, cols), F32)])


def core_kernel(who, one, other, here, there):
    cols = here.shape[1]
    here[...] = one[:, :cols] + other[:, :cols]
    there[...] = one[:, cols:] + other[:, cols:]


def core_sum(name, who, one, other):
    rows, cols = one.shape
    return call(name, core_kernel, who, [one, other], [((rows, cols // 2), F32)] * 2)


def add_kernel(who, *refs):
    total = refs[0][...]
    for ref in refs[1:-1]:
        total = total + ref[...]
    refs[-1][...] = total


def add(name, who, *parts):
    return call(name, add_kernel, who, parts, [(parts[0].shape, F32)])[0]


def moved(value, axis, even, odd):
    peers = lax.axis_size(axis)
    perm = [(i, (i + (odd if i % 2 else even)) % peers) for i in range(peers)]
    return lax.ppermute(value, axis, perm)


def chosen(value, axis, target):
    peers = lax.axis_size(axis)
    pairs = [(i, target(i)) for i in range(peers)]
    return lax.ppermute(value, axis, [pair for pair in pairs if pair[1] is not None])


def swapped(value, axis):
    return chosen(value, axis, lambda i: i ^ 1)


def after(value, *others):
    return lax.optimization_barrier((value, *others))[0]


def body(features, weight, cotangent, block_rows, block_cols, block_counts, block_values):
    rows, width = features.shape
    hidden = weight.shape[1]
    depth = weight.shape[0]
    parts = lax.axis_size("dom")
    side = lax.axis_index("feat").astype(jnp.int32)
    place = lax.axis_index("dom").astype(jnp.int32)
    odd = place & 1
    zero = place * 0
    who = jnp.stack([side, odd, 1 + 2 * odd, 3 - 2 * odd, zero + 2, zero, (place >> 1) & 1,
                     (place >> 2) & 1])

    near = moved(features, "dom", 3, 1)
    far = moved(features, "dom", 1, 3)
    w_there = swapped(weight, "feat")
    half_shape = ((rows // 2, hidden), F32)
    cot_give = call("cot_give", functools.partial(half_kernel, 1), who, [cotangent], [half_shape])[0]
    cot_there = swapped(cot_give, "feat")

    a, t = lay_out(
        block_rows[0], block_cols[0], block_counts, who, block_values[0], rows
    )
    total = forward("agg_own", who, a, [(OWN, features)])
    near = after(near, total, w_there, cot_there)
    two = tuple(swapped(near[k * rows // 2 : (k + 1) * rows // 2], "dom") for k in range(2))
    total = forward("agg_near", who, a, [(NEAR, near)], total)
    give = forward("agg_two", who, a, [(TWO, two)], total, 1)
    far = after(far, give)
    give = forward("agg_give", who, a, [(FAR, far)], give, 1)
    there = swapped(give, "feat")
    keep = forward("agg_keep", who, a, [(FAR, far), (TWO, (after(two[0], give), two[1]))], total, 0)

    act_here, act_there, grad_here, grad_there, g_give = middle(
        who, keep, there, weight, w_there, cotangent, cot_there
    )
    g_there = swapped(g_give, "feat")
    scale = 1.0 / math.sqrt(rows * parts)
    w_give = weight_term("weight_give", who, scale, 1, keep, there, grad_here, grad_there)
    w_keep = weight_term(
        "weight_keep", who, scale, 0, after(keep, w_give), there, grad_here, grad_there
    )
    quick = parts == 16
    steps = weight_sum(who, w_keep, w_give, quick)

    last = next(steps)(grad_here)
    g_here = call(
        "keep",
        keep_kernel,
        who,
        [weight, w_there, after(grad_here, last), grad_there],
        [(keep.shape, F32)],
        flops=12 * rows // 2 * width * hidden,
    )[0]
    firsts = backward("back_here", who, t, [TWO, FAR, NEAR, OWN], after(g_here, last), [], 0)
    g_there = after(g_there, firsts[0])
    last = backward("back_two", who, t, [TWO], g_there, [firsts[0]], 1)[0]
    two_out = last
    last = next(steps)(last)
    two = swapped(after(two_out, last), "dom")
    last = backward("back_far", who, t, [FAR], after(g_there, last), [firsts[1]], 1)[0]
    far = moved(last, "dom", -3, -1)
    last = backward("back_near", who, t, [NEAR], after(g_there, last), [firsts[2], two], 1)[0]
    near = moved(last, "dom", -1, -3)
    last = next(steps)(last)
    act_got = swapped(after(act_there, last), "feat")
    mine = backward("back_own", who, t, [OWN], after(g_there, last), [firsts[3]], 1)[0]
    last = next(steps)(mine, far)
    last = next(steps)(last)
    activated = join("activated", who, SIDE, [after(act_here, last), act_got], jax.ShapeDtypeStruct)
    last = next(steps)(activated)
    feature_grad = call(
        "feature_grad",
        add_kernel,
        who,
        [after(mine, last), far, near],
        [(features.shape, F32)],
        place=jax.ShapeDtypeStruct,
    )[0]
    weight_grad = next(steps)(feature_grad)
    return (activated, feature_grad, weight_grad)


def weight_sum(who, keep, give, quick):
    if not quick:
        here, there = jnp.split(join("core_join", who, CORE, (keep, give)), 2, axis=1)
        total = lax.psum(here + swapped(there, "feat"), "dom")
        for _ in range(6):
            yield lambda *last: last[0]
        yield lambda *last: total
        return
    box = []

    def step(run):
        def go(*last):
            box.append(run(*last))
            return box[-1][0] if isinstance(box[-1], (list, tuple)) else box[-1]

        return go

    def up(value):
        return chosen(value, "dom", lambda i: i + 2 if i % 4 < 2 else None)

    got = swapped(give, "dom")
    yield step(lambda *last: core_sum("core_sum", who, after(keep, *last), got)[::-1])
    there, here = box[-1]
    got = up(there)
    yield step(lambda *last: add("chip_there", who, after(there, *last), got))
    got = swapped(box[-1], "feat")
    also = up(here)
    yield step(lambda *last: side_sum("side_sum", who, after(here, *last), also, got)[::-1])
    give, keep = box[-1]
    for name, bit in (("layer_sum", 4), ("pair_sum", 8)):
        got = chosen(give, "dom", lambda i: i ^ bit if i % 4 >= 2 else None)
        yield step(lambda *last: add(name, who, after(keep, *last), got))
        keep = give = box[-1]
    later_sent = chosen(keep, "dom", lambda i: (i ^ 4) - 2 if i % 4 >= 2 else None)
    later = chosen(keep, "dom", lambda i: i ^ 4 if i % 4 >= 2 else None)
    ready_sent = chosen(keep, "dom", lambda i: i - 2 if i % 4 >= 2 else None)
    yield step(
        lambda *last: pick("chip_pick", who, after(keep, *last), later, ready_sent, later_sent)
    )
    got = swapped(box[-1], "dom")
    yield step(
        lambda *last: join("weight_grad", who, CORE, [after(box[-1], *last), got], jax.ShapeDtypeStruct)
    )


def solution(mesh):
    in_specs = (
        P("dom", "feat"),
        P(None, "feat"),
        P("dom", "feat"),
        P("dom", None, None),
        P("dom", None, None),
        P("dom", None),
        P("dom", None, None, None, None),
    )
    out_specs = (P("dom", "feat"), P("dom", "feat"), P(None, "feat"))
    return jax.shard_map(body, mesh=mesh, in_specs=in_specs, out_specs=out_specs, check_vma=False)
```

```python
import functools
import math

import jax
import jax.numpy as jnp
from jax import lax
from jax.experimental import pallas as pl
from jax.experimental.pallas import tpu as pltpu
from jax.sharding import PartitionSpec as P

F32 = jnp.float32
BF16 = jnp.bfloat16
TILE = 256
LIMIT = 8 * 1024 * 1024
IN_VMEM = pl.BlockSpec(memory_space=pltpu.VMEM)
IN_SMEM = pl.BlockSpec(memory_space=pltpu.SMEM)

SIDE, CORE, NEAR, FAR, TWO, OWN, CHIP, LAYER = range(8)


def split(value):
    high = value.astype(BF16)
    low = (value - high.astype(F32)).astype(BF16)
    return high, low


def mm(a, b, dims=((1,), (0,))):
    return lax.dot_general(a, b, (dims, ((), ())), preferred_element_type=F32)


def mm3(a, b, dims=((1,), (0,))):
    (ah, al), (bh, bl) = a, b
    return mm(ah, bh, dims) + (mm(ah, bl, dims) + mm(al, bh, dims))


def call(name, kernel, who, operands, shapes, scratch=(), flops=0, place=pltpu.VMEM):
    moved = sum(a.size * a.dtype.itemsize for a in operands)
    pinned = [pltpu.with_memory_space_constraint(a, pltpu.VMEM) for a in operands]
    return pl.pallas_call(
        kernel,
        in_specs=[IN_SMEM] + [IN_VMEM] * len(operands),
        out_specs=[IN_VMEM] * len(shapes),
        out_shape=[place(*shape) for shape in shapes],
        scratch_shapes=list(scratch),
        compiler_params=pltpu.CompilerParams(vmem_limit_bytes=LIMIT),
        cost_estimate=pl.CostEstimate(flops=int(flops), bytes_accessed=moved, transcendentals=0),
        name=name,
    )(who, *pinned)


def lay_out_kernel(rows, cols, counts, who, blocks, a, t):
    slot = pl.program_id(0)
    cap = blocks.shape[1]
    size = blocks.shape[2]
    for out in (a, t):
        for part in range(2):
            out[part, slot] = jnp.zeros(out.shape[2:], out.dtype)

    def one(k, carry):
        r = pl.multiple_of(rows[slot, k] * size, size)
        c = pl.multiple_of(cols[slot, k] * size, size)
        block = blocks[0, k]
        for part, value in enumerate(split(block)):
            a[part, slot, pl.ds(r, size), pl.ds(c, size)] = value
        for part, value in enumerate(split(block.T)):
            t[part, slot, pl.ds(c, size), pl.ds(r, size)] = value
        return carry

    lax.fori_loop(0, jnp.minimum(counts[0, slot], cap), one, 0)


def lay_out(rows, cols, counts, who, blocks, size_all):
    window, cap, size, _ = blocks.shape
    shape = pltpu.VMEM((2, window, size_all, size_all), BF16)
    return pl.pallas_call(
        lay_out_kernel,
        grid_spec=pltpu.PrefetchScalarGridSpec(
            num_scalar_prefetch=4,
            grid=(window,),
            in_specs=[pl.BlockSpec((1, cap, size, size), lambda s, *_: (s, 0, 0, 0))],
            out_specs=[IN_VMEM] * 2,
        ),
        out_shape=[shape] * 2,
        compiler_params=pltpu.CompilerParams(vmem_limit_bytes=LIMIT),
        cost_estimate=pl.CostEstimate(flops=0, bytes_accessed=20_000_000, transcendentals=0),
        name="lay_out",
    )(rows, cols, counts, who, pltpu.with_memory_space_constraint(blocks, pltpu.HBM))


def forward_kernel(slots, halves, part, has_base, who, matrix, *refs):
    n = len(slots)
    sources, refs = list(refs[: sum(halves)]), refs[sum(halves) :]
    base, refs = (refs[0], refs[1:]) if has_base else (None, refs)
    out, (highs, lows) = refs[0], refs[1:]
    rows = out.shape[0]
    from_row = 0 if part is None else (who[SIDE] ^ part) * rows
    for i in range(n):
        depth = highs.shape[1] // halves[i]
        for k in range(halves[i]):
            at = pl.ds(k * depth, depth)
            highs[i, at, :], lows[i, at, :] = split(sources.pop(0)[...])

    def tile(k, carry):
        there = pl.ds(pl.multiple_of(k * TILE, TILE), TILE)
        here = pl.ds(pl.multiple_of(from_row + k * TILE, TILE), TILE)
        total = None
        if base is not None:
            total = base[here if base.shape[0] > rows else there, :]
        for i, slot in enumerate(slots):
            at = who[slot]
            term = mm3((matrix[0, at, here, :], matrix[1, at, here, :]), (highs[i], lows[i]))
            total = term if total is None else total + term
        out[there, :] = total
        return carry

    lax.fori_loop(0, rows // TILE, tile, 0)


def forward(name, who, matrix, terms, base=None, part=None):
    slots = [slot for slot, _ in terms]
    groups = [group if isinstance(group, tuple) else (group,) for _, group in terms]
    sources = [source for group in groups for source in group]
    width = sources[0].shape[1]
    depth = matrix.shape[3]
    rows = matrix.shape[2] // (1 if part is None else 2)
    extra = [] if base is None else [base]
    return call(
        name,
        functools.partial(
            forward_kernel, slots, [len(group) for group in groups], part, base is not None
        ),
        who,
        [matrix, *sources, *extra],
        [((rows, width), F32)],
        [pltpu.VMEM((len(terms), depth, width), BF16)] * 2,
        6 * len(terms) * rows * depth * width,
    )[0]


def backward_kernel(slots, part, n_add, first, pieces, who, matrix, source, *refs):
    addends, outs = refs[:n_add], refs[n_add:]
    depth = source.shape[0]
    parts = split(source[...])
    deep = pl.ds(pl.multiple_of((who[SIDE] ^ part) * depth, depth), depth)
    size = outs[0].shape[0]
    here = pl.ds(first, size * pieces)
    for i, slot in enumerate(slots):
        at = who[slot]
        total = mm3((matrix[0, at, here, deep], matrix[1, at, here, deep]), parts)
        for addend in addends:
            total = total + addend[here, :]
        for k in range(pieces):
            outs[i * pieces + k][...] = total[k * size : (k + 1) * size, :]


def backward(name, who, matrix, slots, source, addends, part, first=0, rows=None, pieces=1):
    depth, width = source.shape
    rows = rows or matrix.shape[2]
    return call(
        name,
        functools.partial(backward_kernel, slots, part, len(addends), first, pieces),
        who,
        [matrix, source, *addends],
        [((rows // pieces, width), F32)] * (len(slots) * pieces),
        flops=6 * len(slots) * rows * depth * width,
    )


def middle_kernel(who, own, far, w_here, w_there, cot, cot_there, *outs):
    act_here, act_there, grad_here, grad_there, g_there = outs
    half = own.shape[1]

    def rows_of(w, which):
        return split(w[pl.ds(pl.multiple_of((who[SIDE] ^ which) * half, half), half), :])

    rows = own.shape[0]
    cot_here = cot.at[pl.ds(pl.multiple_of(who[SIDE] * rows, rows), rows), :]
    source = split(own[...]), split(far[...])
    total = None
    for w, cot, act, grad in (
        (w_here, cot_here, act_here, grad_here),
        (w_there, cot_there, act_there, grad_there),
    ):
        pre = mm3(source[0], rows_of(w, 0)) + mm3(source[1], rows_of(w, 1))
        s = 1.0 / (1.0 + jnp.exp(-pre))
        act[...] = pre * s
        pg = cot[...] * (s + pre * s * (1.0 - s))
        grad[...] = pg
        term = mm3(split(pg), rows_of(w, 1), ((1,), (1,)))
        total = term if total is None else total + term
    g_there[...] = total


def middle(who, own, far, w_here, w_there, cot, cot_there):
    shape = (cot_there.shape, F32)
    flops = 36 * own.shape[0] * own.shape[1] * w_here.shape[1]
    operands = [own, far, w_here, w_there, cot, cot_there]
    return call("middle", middle_kernel, who, operands, [shape] * 5, flops=flops)


def keep_kernel(who, w_here, w_there, grad_here, grad_there, g_here):
    half = g_here.shape[1]
    at = pl.ds(pl.multiple_of(who[SIDE] * half, half), half)
    total = None
    for w, grad in ((w_here, grad_here), (w_there, grad_there)):
        term = mm3(split(grad[...]), split(w[at, :]), ((1,), (1,)))
        total = term if total is None else total + term
    g_here[...] = total


def weight_kernel(scale, which, who, own, far, grad_here, grad_there, out):
    mine = who[SIDE] == (who[CORE] ^ which)
    turned = split(jnp.where(mine, own[...], far[...]).T)
    hidden = grad_here.shape[1]
    for k, grad in enumerate((grad_here, grad_there)):
        out[:, k * hidden : (k + 1) * hidden] = mm3(turned, split(grad[...])) * scale


def weight_term(name, who, scale, which, own, far, grad_here, grad_there):
    rows, half = own.shape
    hidden = grad_here.shape[1]
    return call(
        name,
        functools.partial(weight_kernel, scale, which),
        who,
        [own, far, grad_here, grad_there],
        [((half, 2 * hidden), F32)],
        flops=12 * rows * half * hidden,
    )[0]


def half_kernel(which, who, whole, out):
    rows = out.shape[0]
    out[...] = whole[pl.ds(pl.multiple_of((who[SIDE] ^ which) * rows, rows), rows), :]


def join_kernel(place, who, *refs):
    parts, out = refs[:-1], refs[-1]
    rows = parts[0].shape[0]
    for k, part in enumerate(parts):
        out[pl.ds(pl.multiple_of((who[place] ^ k) * rows, rows), rows), :] = part[...]


def join(name, who, place, parts, kind=pltpu.VMEM):
    rows, cols = parts[0].shape
    shape = (rows * len(parts), cols)
    return call(
        name, functools.partial(join_kernel, place), who, parts, [(shape, F32)], place=kind
    )[0]


def pick_kernel(who, ready, later, ready_sent, later_sent, out):
    rows = ready.shape[0]
    odd = who[CHIP] == 1
    for which, one, other in ((0, ready, ready_sent), (1, later, later_sent)):
        at = pl.ds(pl.multiple_of((who[LAYER] ^ which) * rows, rows), rows)
        out[at, :] = jnp.where(odd, one[...], other[...])


def pick(name, who, *parts):
    rows, cols = parts[0].shape
    return call(name, pick_kernel, who, parts, [((2 * rows, cols), F32)])[0]


def hand_out(full, outs, place):
    rows = outs[0].shape[0]
    for k, out in enumerate(outs):
        out[...] = full[pl.ds(pl.multiple_of((place ^ k) * rows, rows), rows), :]


def side_kernel(who, one, two, three, keep, give, full):
    full[...] = one[...] + two[...] + three[...]
    hand_out(full, (keep, give), who[LAYER])


def side_sum(name, who, *parts):
    rows, cols = parts[0].shape
    shape = ((rows // 2, cols), F32)
    return call(name, side_kernel, who, parts, [shape] * 2, [pltpu.VMEM((rows, cols), F32)])


def core_kernel(who, one, other, here, there):
    cols = here.shape[1]
    here[...] = one[:, :cols] + other[:, :cols]
    there[...] = one[:, cols:] + other[:, cols:]


def core_sum(name, who, one, other):
    rows, cols = one.shape
    return call(name, core_kernel, who, [one, other], [((rows, cols // 2), F32)] * 2)


def add_kernel(who, *refs):
    total = refs[0][...]
    for ref in refs[1:-1]:
        total = total + ref[...]
    refs[-1][...] = total


def add(name, who, *parts):
    return call(name, add_kernel, who, parts, [(parts[0].shape, F32)])[0]


def moved(value, axis, even, odd):
    peers = lax.axis_size(axis)
    perm = [(i, (i + (odd if i % 2 else even)) % peers) for i in range(peers)]
    return lax.ppermute(value, axis, perm)


def chosen(value, axis, target):
    peers = lax.axis_size(axis)
    pairs = [(i, target(i)) for i in range(peers)]
    return lax.ppermute(value, axis, [pair for pair in pairs if pair[1] is not None])


def swapped(value, axis):
    return chosen(value, axis, lambda i: i ^ 1)


def after(value, *others):
    return lax.optimization_barrier((value, *others))[0]


def body(features, weight, cotangent, block_rows, block_cols, block_counts, block_values):
    rows, width = features.shape
    hidden = weight.shape[1]
    depth = weight.shape[0]
    parts = lax.axis_size("dom")
    side = lax.axis_index("feat").astype(jnp.int32)
    place = lax.axis_index("dom").astype(jnp.int32)
    odd = place & 1
    zero = place * 0
    who = jnp.stack([side, odd, 1 + 2 * odd, 3 - 2 * odd, zero + 2, zero, (place >> 1) & 1,
                     (place >> 2) & 1])

    near = moved(features, "dom", 3, 1)
    far = moved(features, "dom", 1, 3)
    w_there = swapped(weight, "feat")
    half_shape = ((rows // 2, hidden), F32)
    cot_give = call("cot_give", functools.partial(half_kernel, 1), who, [cotangent], [half_shape])[0]
    cot_there = swapped(cot_give, "feat")

    a, t = lay_out(
        block_rows[0], block_cols[0], block_counts, who, block_values[0], rows
    )
    total = forward("agg_own", who, a, [(OWN, features)])
    near = after(near, total, w_there, cot_there)
    two = tuple(swapped(near[k * rows // 2 : (k + 1) * rows // 2], "dom") for k in range(2))
    total = forward("agg_near", who, a, [(NEAR, near)], total)
    give = forward("agg_two", who, a, [(TWO, two)], total, 1)
    far = after(far, give)
    give = forward("agg_give", who, a, [(FAR, far)], give, 1)
    there = swapped(give, "feat")
    keep = forward("agg_keep", who, a, [(FAR, far), (TWO, (after(two[0], give), two[1]))], total, 0)

    act_here, act_there, grad_here, grad_there, g_give = middle(
        who, keep, there, weight, w_there, cotangent, cot_there
    )
    g_there = swapped(g_give, "feat")
    scale = 1.0 / math.sqrt(rows * parts)
    w_give = weight_term("weight_give", who, scale, 1, keep, there, grad_here, grad_there)
    w_keep = weight_term(
        "weight_keep", who, scale, 0, after(keep, w_give), there, grad_here, grad_there
    )
    quick = parts == 16
    steps = weight_sum(who, w_keep, w_give, quick)

    last = next(steps)(grad_here)
    g_here = call(
        "keep",
        keep_kernel,
        who,
        [weight, w_there, after(grad_here, last), grad_there],
        [(keep.shape, F32)],
        flops=12 * rows // 2 * width * hidden,
    )[0]
    firsts = backward("back_here", who, t, [TWO, FAR, NEAR, OWN], after(g_here, last), [], 0)
    g_there = after(g_there, firsts[0])
    two_out = backward("back_two", who, t, [TWO], g_there, [firsts[0]], 1)[0]
    far_out = backward("back_far", who, t, [FAR], after(g_there, two_out), [firsts[1]], 1)[0]
    last = next(steps)(far_out)
    two = swapped(after(two_out, last), "dom")
    far = moved(after(far_out, last), "dom", -3, -1)
    last = backward("back_near", who, t, [NEAR], after(g_there, last), [firsts[2], two], 1)[0]
    near = moved(last, "dom", -1, -3)
    last = next(steps)(last)
    act_got = swapped(after(act_there, last), "feat")
    mine = backward("back_own", who, t, [OWN], after(g_there, last), [firsts[3]], 1)[0]
    last = next(steps)(mine, far)
    last = next(steps)(last)
    activated = join("activated", who, SIDE, [after(act_here, last), act_got], jax.ShapeDtypeStruct)
    last = next(steps)(activated)
    feature_grad = call(
        "feature_grad",
        add_kernel,
        who,
        [after(mine, last), far, near],
        [(features.shape, F32)],
        place=jax.ShapeDtypeStruct,
    )[0]
    weight_grad = next(steps)(feature_grad)
    return (activated, feature_grad, weight_grad)


def weight_sum(who, keep, give, quick):
    if not quick:
        here, there = jnp.split(join("core_join", who, CORE, (keep, give)), 2, axis=1)
        total = lax.psum(here + swapped(there, "feat"), "dom")
        for _ in range(6):
            yield lambda *last: last[0]
        yield lambda *last: total
        return
    box = []

    def step(run):
        def go(*last):
            box.append(run(*last))
            return box[-1][0] if isinstance(box[-1], (list, tuple)) else box[-1]

        return go

    def up(value):
        return chosen(value, "dom", lambda i: i + 2 if i % 4 < 2 else None)

    got = swapped(give, "dom")
    yield step(lambda *last: core_sum("core_sum", who, after(keep, *last), got)[::-1])
    there, here = box[-1]
    got = up(there)
    yield step(lambda *last: add("chip_there", who, after(there, *last), got))
    got = swapped(box[-1], "feat")
    also = up(here)
    yield step(lambda *last: side_sum("side_sum", who, after(here, *last), also, got)[::-1])
    give, keep = box[-1]
    for name, bit in (("layer_sum", 4), ("pair_sum", 8)):
        got = chosen(give, "dom", lambda i: i ^ bit if i % 4 >= 2 else None)
        yield step(lambda *last: add(name, who, after(keep, *last), got))
        keep = give = box[-1]
    later_sent = chosen(keep, "dom", lambda i: (i ^ 4) - 2 if i % 4 >= 2 else None)
    later = chosen(keep, "dom", lambda i: i ^ 4 if i % 4 >= 2 else None)
    ready_sent = chosen(keep, "dom", lambda i: i - 2 if i % 4 >= 2 else None)
    yield step(
        lambda *last: pick("chip_pick", who, after(keep, *last), later, ready_sent, later_sent)
    )
    got = swapped(box[-1], "dom")
    yield step(
        lambda *last: join("weight_grad", who, CORE, [after(box[-1], *last), got], jax.ShapeDtypeStruct)
    )


def solution(mesh):
    in_specs = (
        P("dom", "feat"),
        P(None, "feat"),
        P("dom", "feat"),
        P("dom", None, None),
        P("dom", None, None),
        P("dom", None),
        P("dom", None, None, None, None),
    )
    out_specs = (P("dom", "feat"), P("dom", "feat"), P(None, "feat"))
    return jax.shard_map(body, mesh=mesh, in_specs=in_specs, out_specs=out_specs, check_vma=False)
```

```python
import functools
import math

import jax
import jax.numpy as jnp
from jax import lax
from jax.experimental import pallas as pl
from jax.experimental.pallas import tpu as pltpu
from jax.sharding import PartitionSpec as P

F32 = jnp.float32
BF16 = jnp.bfloat16
TILE = 256
LIMIT = 8 * 1024 * 1024
IN_VMEM = pl.BlockSpec(memory_space=pltpu.VMEM)
IN_SMEM = pl.BlockSpec(memory_space=pltpu.SMEM)

SIDE, CORE, NEAR, FAR, TWO, OWN, CHIP, LAYER = range(8)


def split(value):
    high = value.astype(BF16)
    low = (value - high.astype(F32)).astype(BF16)
    return high, low


def mm(a, b, dims=((1,), (0,))):
    return lax.dot_general(a, b, (dims, ((), ())), preferred_element_type=F32)


def mm3(a, b, dims=((1,), (0,))):
    (ah, al), (bh, bl) = a, b
    return mm(ah, bh, dims) + (mm(ah, bl, dims) + mm(al, bh, dims))


def call(name, kernel, who, operands, shapes, scratch=(), flops=0, place=pltpu.VMEM):
    moved = sum(a.size * a.dtype.itemsize for a in operands)
    pinned = [pltpu.with_memory_space_constraint(a, pltpu.VMEM) for a in operands]
    return pl.pallas_call(
        kernel,
        in_specs=[IN_SMEM] + [IN_VMEM] * len(operands),
        out_specs=[IN_VMEM] * len(shapes),
        out_shape=[place(*shape) for shape in shapes],
        scratch_shapes=list(scratch),
        compiler_params=pltpu.CompilerParams(vmem_limit_bytes=LIMIT),
        cost_estimate=pl.CostEstimate(flops=int(flops), bytes_accessed=moved, transcendentals=0),
        name=name,
    )(who, *pinned)


def lay_out_kernel(rows, cols, counts, who, blocks, a, t):
    slot = pl.program_id(0)
    cap = blocks.shape[1]
    size = blocks.shape[2]
    for out in (a, t):
        for part in range(2):
            out[part, slot] = jnp.zeros(out.shape[2:], out.dtype)

    def one(k, carry):
        r = pl.multiple_of(rows[slot, k] * size, size)
        c = pl.multiple_of(cols[slot, k] * size, size)
        block = blocks[0, k]
        for part, value in enumerate(split(block)):
            a[part, slot, pl.ds(r, size), pl.ds(c, size)] = value
        for part, value in enumerate(split(block.T)):
            t[part, slot, pl.ds(c, size), pl.ds(r, size)] = value
        return carry

    lax.fori_loop(0, jnp.minimum(counts[0, slot], cap), one, 0)


def lay_out(rows, cols, counts, who, blocks, size_all):
    window, cap, size, _ = blocks.shape
    shape = pltpu.VMEM((2, window, size_all, size_all), BF16)
    return pl.pallas_call(
        lay_out_kernel,
        grid_spec=pltpu.PrefetchScalarGridSpec(
            num_scalar_prefetch=4,
            grid=(window,),
            in_specs=[pl.BlockSpec((1, cap, size, size), lambda s, *_: (s, 0, 0, 0))],
            out_specs=[IN_VMEM] * 2,
        ),
        out_shape=[shape] * 2,
        compiler_params=pltpu.CompilerParams(vmem_limit_bytes=LIMIT),
        cost_estimate=pl.CostEstimate(flops=0, bytes_accessed=20_000_000, transcendentals=0),
        name="lay_out",
    )(rows, cols, counts, who, pltpu.with_memory_space_constraint(blocks, pltpu.HBM))


def forward_kernel(slots, halves, part, has_base, who, matrix, *refs):
    n = len(slots)
    sources, refs = list(refs[: sum(halves)]), refs[sum(halves) :]
    base, refs = (refs[0], refs[1:]) if has_base else (None, refs)
    out, (highs, lows) = refs[0], refs[1:]
    rows = out.shape[0]
    from_row = 0 if part is None else (who[SIDE] ^ part) * rows
    for i in range(n):
        depth = highs.shape[1] // halves[i]
        for k in range(halves[i]):
            at = pl.ds(k * depth, depth)
            highs[i, at, :], lows[i, at, :] = split(sources.pop(0)[...])

    def tile(k, carry):
        there = pl.ds(pl.multiple_of(k * TILE, TILE), TILE)
        here = pl.ds(pl.multiple_of(from_row + k * TILE, TILE), TILE)
        total = None
        if base is not None:
            total = base[here if base.shape[0] > rows else there, :]
        for i, slot in enumerate(slots):
            at = who[slot]
            term = mm3((matrix[0, at, here, :], matrix[1, at, here, :]), (highs[i], lows[i]))
            total = term if total is None else total + term
        out[there, :] = total
        return carry

    lax.fori_loop(0, rows // TILE, tile, 0)


def forward(name, who, matrix, terms, base=None, part=None):
    slots = [slot for slot, _ in terms]
    groups = [group if isinstance(group, tuple) else (group,) for _, group in terms]
    sources = [source for group in groups for source in group]
    width = sources[0].shape[1]
    depth = matrix.shape[3]
    rows = matrix.shape[2] // (1 if part is None else 2)
    extra = [] if base is None else [base]
    return call(
        name,
        functools.partial(
            forward_kernel, slots, [len(group) for group in groups], part, base is not None
        ),
        who,
        [matrix, *sources, *extra],
        [((rows, width), F32)],
        [pltpu.VMEM((len(terms), depth, width), BF16)] * 2,
        6 * len(terms) * rows * depth * width,
    )[0]


def backward_kernel(slots, part, n_add, first, pieces, who, matrix, source, *refs):
    addends, outs = refs[:n_add], refs[n_add:]
    depth = source.shape[0]
    parts = split(source[...])
    deep = pl.ds(pl.multiple_of((who[SIDE] ^ part) * depth, depth), depth)
    size = outs[0].shape[0]
    here = pl.ds(first, size * pieces)
    for i, slot in enumerate(slots):
        at = who[slot]
        total = mm3((matrix[0, at, here, deep], matrix[1, at, here, deep]), parts)
        for addend in addends:
            total = total + addend[here, :]
        for k in range(pieces):
            outs[i * pieces + k][...] = total[k * size : (k + 1) * size, :]


def backward(name, who, matrix, slots, source, addends, part, first=0, rows=None, pieces=1):
    depth, width = source.shape
    rows = rows or matrix.shape[2]
    return call(
        name,
        functools.partial(backward_kernel, slots, part, len(addends), first, pieces),
        who,
        [matrix, source, *addends],
        [((rows // pieces, width), F32)] * (len(slots) * pieces),
        flops=6 * len(slots) * rows * depth * width,
    )


def middle_kernel(who, own, far, w_here, w_there, cot, cot_there, *outs):
    act_here, act_there, grad_here, grad_there, g_there = outs
    half = own.shape[1]

    def rows_of(w, which):
        return split(w[pl.ds(pl.multiple_of((who[SIDE] ^ which) * half, half), half), :])

    rows = own.shape[0]
    cot_here = cot.at[pl.ds(pl.multiple_of(who[SIDE] * rows, rows), rows), :]
    source = split(own[...]), split(far[...])
    total = None
    for w, cot, act, grad in (
        (w_here, cot_here, act_here, grad_here),
        (w_there, cot_there, act_there, grad_there),
    ):
        pre = mm3(source[0], rows_of(w, 0)) + mm3(source[1], rows_of(w, 1))
        s = 1.0 / (1.0 + jnp.exp(-pre))
        act[...] = pre * s
        pg = cot[...] * (s + pre * s * (1.0 - s))
        grad[...] = pg
        term = mm3(split(pg), rows_of(w, 1), ((1,), (1,)))
        total = term if total is None else total + term
    g_there[...] = total


def middle(who, own, far, w_here, w_there, cot, cot_there):
    shape = (cot_there.shape, F32)
    flops = 36 * own.shape[0] * own.shape[1] * w_here.shape[1]
    operands = [own, far, w_here, w_there, cot, cot_there]
    return call("middle", middle_kernel, who, operands, [shape] * 5, flops=flops)


def keep_kernel(who, w_here, w_there, grad_here, grad_there, g_here):
    half = g_here.shape[1]
    at = pl.ds(pl.multiple_of(who[SIDE] * half, half), half)
    total = None
    for w, grad in ((w_here, grad_here), (w_there, grad_there)):
        term = mm3(split(grad[...]), split(w[at, :]), ((1,), (1,)))
        total = term if total is None else total + term
    g_here[...] = total


def weight_kernel(scale, which, who, own, far, grad_here, grad_there, out):
    mine = who[SIDE] == (who[CORE] ^ which)
    turned = split(jnp.where(mine, own[...], far[...]).T)
    hidden = grad_here.shape[1]
    for k, grad in enumerate((grad_here, grad_there)):
        out[:, k * hidden : (k + 1) * hidden] = mm3(turned, split(grad[...])) * scale


def weight_term(name, who, scale, which, own, far, grad_here, grad_there):
    rows, half = own.shape
    hidden = grad_here.shape[1]
    return call(
        name,
        functools.partial(weight_kernel, scale, which),
        who,
        [own, far, grad_here, grad_there],
        [((half, 2 * hidden), F32)],
        flops=12 * rows * half * hidden,
    )[0]


def half_kernel(which, who, whole, out):
    rows = out.shape[0]
    out[...] = whole[pl.ds(pl.multiple_of((who[SIDE] ^ which) * rows, rows), rows), :]


def join_kernel(place, who, *refs):
    parts, out = refs[:-1], refs[-1]
    rows = parts[0].shape[0]
    for k, part in enumerate(parts):
        out[pl.ds(pl.multiple_of((who[place] ^ k) * rows, rows), rows), :] = part[...]


def join(name, who, place, parts, kind=pltpu.VMEM):
    rows, cols = parts[0].shape
    shape = (rows * len(parts), cols)
    return call(
        name, functools.partial(join_kernel, place), who, parts, [(shape, F32)], place=kind
    )[0]


def pick_kernel(who, ready, later, ready_sent, later_sent, out):
    rows = ready.shape[0]
    odd = who[CHIP] == 1
    for which, one, other in ((0, ready, ready_sent), (1, later, later_sent)):
        at = pl.ds(pl.multiple_of((who[LAYER] ^ which) * rows, rows), rows)
        out[at, :] = jnp.where(odd, one[...], other[...])


def pick(name, who, *parts):
    rows, cols = parts[0].shape
    return call(name, pick_kernel, who, parts, [((2 * rows, cols), F32)])[0]


def hand_out(full, outs, place):
    rows = outs[0].shape[0]
    for k, out in enumerate(outs):
        out[...] = full[pl.ds(pl.multiple_of((place ^ k) * rows, rows), rows), :]


def side_kernel(who, one, two, three, keep, give, full):
    full[...] = one[...] + two[...] + three[...]
    hand_out(full, (keep, give), who[LAYER])


def side_sum(name, who, *parts):
    rows, cols = parts[0].shape
    shape = ((rows // 2, cols), F32)
    return call(name, side_kernel, who, parts, [shape] * 2, [pltpu.VMEM((rows, cols), F32)])


def core_kernel(who, one, other, here, there):
    cols = here.shape[1]
    here[...] = one[:, :cols] + other[:, :cols]
    there[...] = one[:, cols:] + other[:, cols:]


def core_sum(name, who, one, other):
    rows, cols = one.shape
    return call(name, core_kernel, who, [one, other], [((rows, cols // 2), F32)] * 2)


def add_kernel(who, *refs):
    total = refs[0][...]
    for ref in refs[1:-1]:
        total = total + ref[...]
    refs[-1][...] = total


def add(name, who, *parts):
    return call(name, add_kernel, who, parts, [(parts[0].shape, F32)])[0]


def moved(value, axis, even, odd):
    peers = lax.axis_size(axis)
    perm = [(i, (i + (odd if i % 2 else even)) % peers) for i in range(peers)]
    return lax.ppermute(value, axis, perm)


def chosen(value, axis, target):
    peers = lax.axis_size(axis)
    pairs = [(i, target(i)) for i in range(peers)]
    return lax.ppermute(value, axis, [pair for pair in pairs if pair[1] is not None])


def swapped(value, axis):
    return chosen(value, axis, lambda i: i ^ 1)


def after(value, *others):
    return lax.optimization_barrier((value, *others))[0]


def body(features, weight, cotangent, block_rows, block_cols, block_counts, block_values):
    rows, width = features.shape
    hidden = weight.shape[1]
    depth = weight.shape[0]
    parts = lax.axis_size("dom")
    side = lax.axis_index("feat").astype(jnp.int32)
    place = lax.axis_index("dom").astype(jnp.int32)
    odd = place & 1
    zero = place * 0
    who = jnp.stack([side, odd, 1 + 2 * odd, 3 - 2 * odd, zero + 2, zero, (place >> 1) & 1,
                     (place >> 2) & 1])

    near = moved(features, "dom", 3, 1)
    far = moved(features, "dom", 1, 3)
    w_there = swapped(weight, "feat")
    half_shape = ((rows // 2, hidden), F32)
    cot_give = call("cot_give", functools.partial(half_kernel, 1), who, [cotangent], [half_shape])[0]
    cot_there = swapped(cot_give, "feat")

    a, t = lay_out(
        block_rows[0], block_cols[0], block_counts, who, block_values[0], rows
    )
    total = forward("agg_own", who, a, [(OWN, features)])
    near = after(near, total, w_there, cot_there)
    two = tuple(swapped(near[k * rows // 2 : (k + 1) * rows // 2], "dom") for k in range(2))
    total = forward("agg_near", who, a, [(NEAR, near)], total)
    give = forward("agg_two", who, a, [(TWO, two)], total, 1)
    far = after(far, give)
    give = forward("agg_give", who, a, [(FAR, far)], give, 1)
    there = swapped(give, "feat")
    keep = forward("agg_keep", who, a, [(FAR, far), (TWO, (after(two[0], give), two[1]))], total, 0)

    act_here, act_there, grad_here, grad_there, g_give = middle(
        who, keep, there, weight, w_there, cotangent, cot_there
    )
    g_there = swapped(g_give, "feat")
    scale = 1.0 / math.sqrt(rows * parts)
    w_give = weight_term("weight_give", who, scale, 1, keep, there, grad_here, grad_there)
    w_keep = weight_term(
        "weight_keep", who, scale, 0, after(keep, w_give), there, grad_here, grad_there
    )
    quick = parts == 16
    steps = weight_sum(who, w_keep, w_give, quick)

    last = next(steps)(grad_here)
    g_here = call(
        "keep",
        keep_kernel,
        who,
        [weight, w_there, after(grad_here, last), grad_there],
        [(keep.shape, F32)],
        flops=12 * rows // 2 * width * hidden,
    )[0]
    firsts = backward("back_here", who, t, [TWO, FAR, NEAR, OWN], after(g_here, last), [], 0)
    g_there = after(g_there, firsts[0])
    far_out = backward("back_far", who, t, [FAR], g_there, [firsts[1]], 1)[0]
    two_out = backward("back_two", who, t, [TWO], after(g_there, far_out), [firsts[0]], 1)[0]
    last = next(steps)(two_out)
    far = moved(after(far_out, last), "dom", -3, -1)
    two = swapped(after(two_out, last), "dom")
    last = backward("back_near", who, t, [NEAR], after(g_there, last), [firsts[2], two], 1)[0]
    near = moved(last, "dom", -1, -3)
    last = next(steps)(last)
    act_got = swapped(after(act_there, last), "feat")
    mine = backward("back_own", who, t, [OWN], after(g_there, last), [firsts[3]], 1)[0]
    last = next(steps)(mine, far)
    last = next(steps)(last)
    activated = join("activated", who, SIDE, [after(act_here, last), act_got], jax.ShapeDtypeStruct)
    last = next(steps)(activated)
    feature_grad = call(
        "feature_grad",
        add_kernel,
        who,
        [after(mine, last), far, near],
        [(features.shape, F32)],
        place=jax.ShapeDtypeStruct,
    )[0]
    weight_grad = next(steps)(feature_grad)
    return (activated, feature_grad, weight_grad)


def weight_sum(who, keep, give, quick):
    if not quick:
        here, there = jnp.split(join("core_join", who, CORE, (keep, give)), 2, axis=1)
        total = lax.psum(here + swapped(there, "feat"), "dom")
        for _ in range(6):
            yield lambda *last: last[0]
        yield lambda *last: total
        return
    box = []

    def step(run):
        def go(*last):
            box.append(run(*last))
            return box[-1][0] if isinstance(box[-1], (list, tuple)) else box[-1]

        return go

    def up(value):
        return chosen(value, "dom", lambda i: i + 2 if i % 4 < 2 else None)

    got = swapped(give, "dom")
    yield step(lambda *last: core_sum("core_sum", who, after(keep, *last), got)[::-1])
    there, here = box[-1]
    got = up(there)
    yield step(lambda *last: add("chip_there", who, after(there, *last), got))
    got = swapped(box[-1], "feat")
    also = up(here)
    yield step(lambda *last: side_sum("side_sum", who, after(here, *last), also, got)[::-1])
    give, keep = box[-1]
    for name, bit in (("layer_sum", 4), ("pair_sum", 8)):
        got = chosen(give, "dom", lambda i: i ^ bit if i % 4 >= 2 else None)
        yield step(lambda *last: add(name, who, after(keep, *last), got))
        keep = give = box[-1]
    later_sent = chosen(keep, "dom", lambda i: (i ^ 4) - 2 if i % 4 >= 2 else None)
    later = chosen(keep, "dom", lambda i: i ^ 4 if i % 4 >= 2 else None)
    ready_sent = chosen(keep, "dom", lambda i: i - 2 if i % 4 >= 2 else None)
    yield step(
        lambda *last: pick("chip_pick", who, after(keep, *last), later, ready_sent, later_sent)
    )
    got = swapped(box[-1], "dom")
    yield step(
        lambda *last: join("weight_grad", who, CORE, [after(box[-1], *last), got], jax.ShapeDtypeStruct)
    )


def solution(mesh):
    in_specs = (
        P("dom", "feat"),
        P(None, "feat"),
        P("dom", "feat"),
        P("dom", None, None),
        P("dom", None, None),
        P("dom", None),
        P("dom", None, None, None, None),
    )
    out_specs = (P("dom", "feat"), P("dom", "feat"), P(None, "feat"))
    return jax.shard_map(body, mesh=mesh, in_specs=in_specs, out_specs=out_specs, check_vma=False)
```
